256 devices in a mesh: rep: 8 (over y, core), shard: 32 (over x, z).
Axes of the slice: x: 4, y: 4, z: 8, core: 2. Of those that a mesh axis runs over, the one named last changes fastest.
Arguments:
- tokens: bfloat16 [26624, 2048], P(('rep', 'shard')), may hold values from -6 to 6
- cotangent: bfloat16 [26624, 2048], P(('rep', 'shard')), may hold values from -0.119628906 to 0.119628906
- w_in: bfloat16 [2048, 8192], P(None, 'shard'), may hold values from -0.125 to 0.125
- w_out: bfloat16 [8192, 2048], P('shard'), may hold values from -0.0625 to 0.0625
- momentum: float32 [5, 2097152], P(None, 'shard'), may hold values from -6 to 6
- error: float32 [5, 2097152], P(None, 'shard'), may hold values from -0.3 to 0.3
- block_order: int32 [5, 262144], P(None, 'shard'), may hold values from 0 to 8191, as said below
- signs: int32 [5, 262144], P(None, 'shard'), may hold values from 0 to 1
- heavy_blocks: int32 [8, 2048], P('rep', 'shard'), may hold values from 0 to 8191
- heavy_count: int32 [8, 32], P('rep', 'shard'), may hold values from 1 to 64, as said below
Outputs:
- w_in_new: float32 [2048, 8192], P(None, 'shard')
- w_out_new: float32 [8192, 2048], P('shard')
- momentum_new: float32 [5, 2097152], P(None, 'shard')
- error_new: float32 [5, 2097152], P(None, 'shard')
The draws below stay inside these ranges and needn't reach their ends.
Inputs may be any that keep to these rules, and one draw needn't show every extreme that they name: `heavy_count`: for each shard exactly one replica has 64 live slots; every other count is at most 16. `block_order`: each row's 8192 entries of one shard are a permutation of 0 to 8191.
All inputs are finite; a program needn't handle non-finite values.
Results may differ from the reference program's by a relative error of at most 0.0028.
Values may be sent and summed in bfloat16 or wider, within the bound.
A program may use at most 192 MiB of HBM per device.

```python
import jax
import jax.numpy as jnp
from jax import lax

DW = 2048
FF = 8192
TOK_DEV = 104
ROWS = 5
SKC = 65536
MAXH = 64
TOKENS = 26624
NBLK_ALL = 262144
NBLK = 8192
N_REP = 8
N_SHARD = 32


def draw_heavy_count(key, part):
    key = jax.random.fold_in(key, 11)
    first, second = jax.random.split(key)
    base = jax.random.randint(first, (N_REP, N_SHARD), 1, MAXH // 4 + 1)
    chosen = jax.random.randint(second, (1, N_SHARD), 0, N_REP)
    ranks = jnp.arange(N_REP, dtype=jnp.int32)[:, None]
    return jnp.where(ranks == chosen, MAXH, base).astype(jnp.int32)


def draw_block_order(key, part):
    key = jax.random.fold_in(key, 5)
    keys = jax.random.split(key, ROWS * N_SHARD)
    perms = jax.vmap(lambda single: jax.random.permutation(single, NBLK))(keys)
    return perms.reshape(ROWS, N_SHARD * NBLK).astype(jnp.int32)


def place_ends(array, key, smallest, largest):
    longest = array.shape.index(max(array.shape))
    spots = []
    for shift in (0, 1):
        where = [jax.random.randint(jax.random.fold_in(key, axis), (), 0, length) for axis, length in enumerate(array.shape)]
        where[longest] = (where[longest] + shift) % array.shape[longest]
        spots.append(tuple(where))
    return array.at[spots[0]].set(smallest).at[spots[1]].set(largest)


def steps_of(stream_key, dims, shards, smallest, top_value):
    factor_of = 1.0
    for dim, parts in shards:
        draws = jax.random.uniform(jax.random.fold_in(jax.random.fold_in(stream_key, 6), dim), (parts,), jnp.float32, smallest / len(shards), top_value / len(shards))
        factor_of = factor_of * jnp.repeat(jnp.exp(draws), dims[dim] // parts).reshape((-1,) + (1,) * (len(dims) - 1 - dim))
    return factor_of


def scatter_about(rng, dims, width, bound, cuts=(), held_as=jnp.bfloat16):
    array = jax.random.normal(rng, dims, jnp.float32) * width
    if len(cuts) > 0:
        array = steps_of(rng, dims, cuts, -0.22, 0.18) * array
    return jnp.clip(array, min=-bound, max=bound).astype(held_as)


def setup_inputs(seed: int = 0) -> dict:
    splits = jax.random.split(jax.random.key(seed), 11)
    tokens = scatter_about(splits[0], (TOKENS, DW), 1.0, 6.0, ((0, 256),))
    cotangent = scatter_about(splits[1], (TOKENS, DW), 0.02, 0.119628906, ((0, 256),))
    w_in = scatter_about(splits[2], (DW, FF), DW ** -0.5, 0.125, ((1, 32),))
    w_out = scatter_about(splits[3], (FF, DW), FF ** -0.5, 0.0625, ((0, 32),))
    momentum = scatter_about(splits[4], (ROWS, SKC * N_SHARD), 1.0, 6.0, ((1, 32),), jnp.float32)
    error = scatter_about(splits[5], (ROWS, SKC * N_SHARD), 0.05, 0.3, ((1, 32),), jnp.float32)
    block_order = draw_block_order(jax.random.fold_in(splits[10], 71), 0)
    signs = place_ends(jax.random.randint(splits[7], (ROWS, NBLK_ALL), 0, 2), jax.random.fold_in(splits[7], 1), 0, 1).astype(jnp.int32)
    heavy_blocks = place_ends(jax.random.randint(splits[8], (N_REP, N_SHARD * MAXH), 0, NBLK), jax.random.fold_in(splits[8], 1), 0, NBLK - 1).astype(jnp.int32)
    heavy_count = draw_heavy_count(jax.random.fold_in(splits[10], 71), 0)
    return dict(tokens=tokens, cotangent=cotangent, w_in=w_in, w_out=w_out, momentum=momentum, error=error, block_order=block_order, signs=signs, heavy_blocks=heavy_blocks, heavy_count=heavy_count)


LEARN = 0.05
DECAY = 0.9
ROOT = 0.7978845608028654


def gelu_pair(pre):
    tangent = jnp.tanh(ROOT * (pre + 0.044715 * pre * pre * pre))
    value = 0.5 * pre * (1.0 + tangent)
    slope = 0.5 * (1.0 + tangent) + 0.5 * pre * (1.0 - tangent * tangent) * ROOT * (1.0 + 0.134145 * pre * pre)
    return value, slope


def sketch(blocks, order_rows, sign_rows, count):
    factor = jnp.where(sign_rows == 1, 1.0, -1.0).astype(blocks.dtype)
    signed = factor[:, :, None] * blocks[order_rows]
    return jnp.sum(signed.reshape(signed.shape[0], count, -1, 128), axis=2)


def reference(tokens, cotangent, w_in, w_out, momentum, error, block_order, signs, heavy_blocks, heavy_count):
    group = TOK_DEV * N_SHARD
    cols = FF // N_SHARD
    count = SKC // 128

    def add_group(carry, idx):
        tok_rows = lax.dynamic_slice_in_dim(tokens, idx * group, group, 0)
        cot_rows = lax.dynamic_slice_in_dim(cotangent, idx * group, group, 0)
        pre = jnp.dot(tok_rows, w_in, preferred_element_type=jnp.float32)
        value, slope = gelu_pair(pre)
        hidden = value.astype(jnp.bfloat16)
        back = lax.dot_general(cot_rows, w_out, (((1,), (1,)), ((), ())), preferred_element_type=jnp.float32)
        pre_grad = (back * slope).astype(jnp.bfloat16)
        grad_in = carry[0] + jnp.dot(tok_rows.T, pre_grad, preferred_element_type=jnp.float32)
        grad_out = carry[1] + jnp.dot(hidden.T, cot_rows, preferred_element_type=jnp.float32)
        return (grad_in, grad_out), None

    start = (jnp.zeros((DW, FF), jnp.float32), jnp.zeros((FF, DW), jnp.float32))
    (grad_in, grad_out), unused = lax.scan(add_group, start, jnp.arange(N_REP, dtype=jnp.int32))

    def one_shard(shard):
        gin = lax.dynamic_slice_in_dim(grad_in, shard * cols, cols, 1)
        gout = lax.dynamic_slice_in_dim(grad_out, shard * cols, cols, 0)
        grads = jnp.concatenate([gin.reshape(-1, 128), gout.reshape(-1, 128)], axis=0)
        nblk = grads.shape[0]
        per = nblk // count
        half = gin.size // 128
        order_rows = lax.dynamic_slice_in_dim(block_order, shard * nblk, nblk, 1)
        sign_rows = lax.dynamic_slice_in_dim(signs, shard * nblk, nblk, 1)
        table = sketch(grads, order_rows, sign_rows, count)
        mom = lax.dynamic_slice_in_dim(momentum, shard * SKC, SKC, 1).reshape(ROWS, count, 128)
        err = lax.dynamic_slice_in_dim(error, shard * SKC, SKC, 1).reshape(ROWS, count, 128)
        mom_new = DECAY * mom + table
        probe = err + (LEARN * DECAY) * mom
        lists = lax.dynamic_slice_in_dim(heavy_blocks, shard * MAXH, MAXH, 1).reshape(-1)
        counts = lax.dynamic_slice_in_dim(heavy_count, shard, 1, 1)
        live = (jnp.arange(MAXH, dtype=jnp.int32)[None, :] < counts).reshape(-1)
        exact = grads[lists]
        positions = jnp.arange(nblk, dtype=jnp.int32)
        match = order_rows[:, None, :] == lists[None, :, None]
        slot = jnp.sum(jnp.where(match, positions[None, None, :], 0), axis=2).astype(jnp.int32)
        slot_signs = jnp.take_along_axis(sign_rows, slot, axis=1)
        picked = probe[jnp.arange(ROWS, dtype=jnp.int32)[:, None], slot // per]
        factor = jnp.where(slot_signs == 1, 1.0, -1.0).astype(picked.dtype)
        median = jnp.sort(picked * factor[:, :, None], axis=0)[ROWS // 2]
        update = median + LEARN * exact
        target = jnp.where(live, lists, nblk)
        delta = jnp.zeros((nblk, 128), grads.dtype).at[target].set(update, mode="drop")
        err_new = err + LEARN * mom_new - sketch(delta, order_rows, sign_rows, count)
        win = lax.dynamic_slice_in_dim(w_in, shard * cols, cols, 1)
        wout = lax.dynamic_slice_in_dim(w_out, shard * cols, cols, 0)
        win_new = win.astype(jnp.float32) - delta[:half].reshape(DW, cols)
        wout_new = wout.astype(jnp.float32) - delta[half:].reshape(cols, DW)
        return win_new, wout_new, mom_new.reshape(ROWS, SKC), err_new.reshape(ROWS, SKC)

    win_all, wout_all, mom_all, err_all = lax.map(one_shard, jnp.arange(N_SHARD, dtype=jnp.int32))
    w_in_new = jnp.transpose(win_all, (1, 0, 2)).reshape(DW, FF)
    w_out_new = wout_all.reshape(FF, DW)
    momentum_new = jnp.transpose(mom_all, (1, 0, 2)).reshape(ROWS, SKC * N_SHARD)
    error_new = jnp.transpose(err_all, (1, 0, 2)).reshape(ROWS, SKC * N_SHARD)
    return (w_in_new, w_out_new, momentum_new, error_new)
```

```python
import functools

import jax
import jax.numpy as jnp
from jax import lax
from jax.experimental import pallas as pl
from jax.experimental.pallas import tpu as pltpu
from jax.sharding import PartitionSpec as P

MESH = pl.DeviceIdType.MESH
F32, BF16, I32 = jnp.float32, jnp.bfloat16, jnp.int32
LEARN = 0.05
DECAY = 0.9
ROOT = 0.7978845608028654

NX, NY, NZ = 4, 4, 8
TOK = 104
CHIP = 2 * TOK
SUBS = ((0, 112), (112, 96))
DW, COLS = 2048, 256
NB = 8192
COUNT = 512
ROWS = 5
LIVE = 256
TAB = LIVE + ROWS * COUNT
PIECES = ((0, 1280), (1280, 1024), (2304, 512))
CODE = ROWS * 64
META = CODE + 64


def nt(a, b):
    return lax.dot_general(a, b, (((1,), (1,)), ((), ())), preferred_element_type=F32)


def tn(a, b):
    return lax.dot_general(a, b, (((0,), (0,)), ((), ())), preferred_element_type=F32)


def nn(a, b):
    return jnp.dot(a, b, preferred_element_type=F32)


def iota(shape, dim):
    return lax.broadcasted_iota(I32, shape, dim)


def split2(x):
    hi = x.astype(BF16)
    return jnp.concatenate([hi, (x - hi.astype(F32)).astype(BF16)], axis=1)


def place_of(block):
    rest = block - 4096
    return jnp.where(
        block < 4096, (block & 1) * 2048 + (block >> 1), 4096 + (rest & 15) * 256 + (rest >> 4)
    )


def gelu_pair(pre):
    tangent = jnp.tanh(ROOT * (pre + 0.044715 * pre * pre * pre))
    value = 0.5 * pre * (1.0 + tangent)
    slope = 0.5 * (1.0 + tangent) + 0.5 * pre * (1.0 - tangent * tangent) * ROOT * (
        1.0 + 0.134145 * pre * pre
    )
    return value, slope


def invert(ord_ref, sgn_ref, meta_ref):
    step = 1024
    for j in range(ROWS):

        def body(c, acc, j=j):
            at = pl.ds(pl.multiple_of(c * step, step), step)
            place = place_of(ord_ref[j : j + 1, at])
            sign = sgn_ref[j : j + 1, at]
            bucket = (c * step + iota((1, step), 1)) >> 4
            row = iota((128, step), 0)
            value = jnp.where(row < 64, bucket >> 1, (bucket & 1) * 2 + sign)
            left = jnp.where((row & 63) == (place >> 7), value, 0).astype(F32).astype(BF16)
            right = jnp.where(row == (place & 127), 1.0, 0.0).astype(BF16)
            return acc + nt(left, right)

        acc = lax.fori_loop(0, NB // step, body, jnp.zeros((128, 128), F32))
        meta_ref[j * 64 : (j + 1) * 64, :] = (acc[:64] * 4.0 + acc[64:]).astype(I32)


def compact(lists, along):
    full = jnp.concatenate([lists, jnp.zeros((120, 128), I32)], axis=0)
    shape = (LIVE, 128)
    slot, lane = iota(shape, 0), iota(shape, 1)
    wanted = jnp.where(slot < 128, slot & 15, jnp.where(slot < 176, slot - 112, 127))
    pick = jnp.where(lane == wanted, 1.0, 0.0).astype(BF16)
    pick_count = jnp.where(lane == 64, 1.0, 0.0).astype(BF16)
    high = (full >> 7).astype(F32).astype(BF16)
    low = (full & 127).astype(F32).astype(BF16)
    if along == 0:
        values = nt(pick, high) * 128.0 + nt(pick, low)
        counts = nt(pick_count, low)
        spot, rep, axis = slot, lane, 1
    else:
        values = nt(high, pick) * 128.0 + nt(low, pick)
        counts = nt(low, pick_count)
        spot, rep, axis = iota((128, LIVE), 1), iota((128, LIVE), 0), 0
    first = (spot < 128) & (rep == (spot >> 4)) & (counts > (spot & 15).astype(F32))
    later = (spot >= 128) & (spot < 176) & (rep < 8) & (counts > 63.5)
    hit = jnp.where(first | later, 1.0, 0.0)
    live = jnp.sum(hit, axis=axis, keepdims=True)
    block = jnp.sum(hit * values, axis=axis, keepdims=True).astype(I32)
    return jnp.where(live > 0.5, place_of(block), -1)


def lists_of(meta_ref, *lead):
    total = jnp.zeros((8, 128), I32)
    for r in range(8):
        total = total + meta_ref[(*lead, slice(CODE + 8 * r, CODE + 8 * r + 8), slice(None))]
    return total


def middle_value(values):
    values = list(values)
    total = len(values)
    for rounds in range(total):
        for i in range(rounds % 2, total - 1, 2):
            lower = jnp.minimum(values[i], values[i + 1])
            upper = jnp.maximum(values[i], values[i + 1])
            values[i] = lower
            values[i + 1] = upper
    return values[total // 2]


def prepare(meta, momv, errv, medv, infov, acrossv):
    lists = lists_of(meta)
    down, across = compact(lists, 0), compact(lists, 1)
    shape = (LIVE, LIVE)
    same = (down == across) & (across >= 0) & (iota(shape, 1) < iota(shape, 0))
    earlier = jnp.max(jnp.where(same, 1.0, 0.0), axis=1, keepdims=True)
    keep = jnp.where((down >= 0) & (earlier < 0.5), 1, 0)
    codes = meta[...]
    high = (codes >> 2).astype(F32).astype(BF16)
    low = (codes & 3).astype(F32).astype(BF16)
    lane = iota((LIVE, 128), 1)
    lane_hit = lane == (down & 127)
    info = jnp.where(lane == ROWS, keep, 0)
    found = []
    for j in range(ROWS):
        pick = jnp.where(iota((LIVE, META), 1) == (down >> 7) + j * 64, 1.0, 0.0)
        pick = jnp.where(down >= 0, pick, 0.0).astype(BF16)
        value = nn(pick, high) * 4.0 + nn(pick, low)
        code = jnp.sum(jnp.where(lane_hit, value, 0.0), axis=1, keepdims=True).astype(I32)
        info = jnp.where(lane == j, code, info)
        probe = errv[j] + LEARN * DECAY * momv[j]
        got = nn(signed_hit(code), split2(probe))
        found.append(got[:, :128] + got[:, 128:])
    medv[...] = middle_value(found)
    infov[...] = info
    acrossv[...] = jnp.broadcast_to(across, acrossv.shape)


def signed_hit(code):
    sign = jnp.where((code & 1) == 1, 1.0, -1.0)
    return jnp.where(iota((LIVE, COUNT), 1) == (code >> 1), sign, 0.0).astype(BF16)


def main_kernel(
    tok_ref, cot_ref, win_ref, wout_ref, ord_ref, sgn_ref, lst_ref, mom_ref, err_ref,
    ghl_ref, codes_ref, spots_ref, med_ref, info_ref, across_ref,
    own, land, buf, wi, wo, gin, gout, ordv, sgnv, meta, meta2, ghl,
    momv, errv, medv, infov, acrossv, spots,
    lsem, land_sem, ring_s, ring_r, sib_s, sib_r, w_s, w_r, list_s, list_r, meta_s, meta_r,
):
    rep, shard = lax.axis_index("rep"), lax.axis_index("shard")
    y, core = rep // 2, rep % 2
    x, z = shard // NZ, shard % NZ
    other = 1 - core

    def dev(dx=0, dy=0, dz=0, to=None):
        c = core if to is None else to
        return {
            "rep": lax.rem(y + dy + NY, NY) * 2 + c,
            "shard": lax.rem(x + dx + NX, NX) * NZ + lax.rem(z + dz + NZ, NZ),
        }

    def remote(src, dst, send, recv, device):
        return pltpu.make_async_remote_copy(
            src_ref=src, dst_ref=dst, send_sem=send, recv_sem=recv, device_id=device, device_id_type=MESH
        )

    def on_core(c, *actions):
        @pl.when(core == c)
        def _():
            for action in actions:
                action()

    own_tok = pltpu.make_async_copy(tok_ref, own, lsem.at[0])
    own_cot = pltpu.make_async_copy(cot_ref, own, lsem.at[0])
    loads = [
        pltpu.make_async_copy(lst_ref, meta.at[pl.ds(pl.multiple_of(CODE + 8 * rep, 8), 8)], lsem.at[1]),
        pltpu.make_async_copy(ord_ref, ordv, lsem.at[2]),
        pltpu.make_async_copy(sgn_ref, sgnv, lsem.at[3]),
    ]
    tables = [pltpu.make_async_copy(mom_ref.at[:, j, :], momv.at[j], lsem.at[6 + j]) for j in range(ROWS)]
    tables += [pltpu.make_async_copy(err_ref.at[:, j, :], errv.at[j], lsem.at[11 + j]) for j in range(ROWS)]
    own_wi = pltpu.make_async_copy(win_ref, wi.at[:, pl.ds(0, COLS)], lsem.at[4])
    own_wo = pltpu.make_async_copy(wout_ref, wo.at[pl.ds(0, COLS)], lsem.at[5])
    on_core(0, own_tok.start)
    on_core(1, own_cot.start)
    for load in loads:
        load.start()

    barrier = pltpu.get_barrier_semaphore()
    partners = [dev(dz=1), dev(dz=-1)]
    partners += [dev(dx=d, to=c) for d in (1, -1, 2) for c in (0, 1)]
    partners += [dev(dy=d, to=c) for d in (1, 2, 3) for c in (0, 1)] + [dev(to=other)]
    for partner in partners:
        pl.semaphore_signal(barrier, inc=1, device_id=partner, device_id_type=MESH)
    pl.semaphore_wait(barrier, len(partners))

    give_cot = remote(cot_ref, land, land_sem.at[0], land_sem.at[1], dev(to=other))
    give_tok = remote(tok_ref, land, land_sem.at[0], land_sem.at[1], dev(to=other))
    on_core(0, give_cot.start)
    on_core(1, give_tok.start)

    toward = jnp.where(core == 0, -1, 1)
    lower, upper = pl.ds(0, COLS), pl.ds(COLS, COLS)
    landing = pl.ds(pl.multiple_of(other * COLS, COLS), COLS)
    w_in_first = remote(win_ref, wi.at[:, landing], w_s.at[0], w_r.at[0], dev(dx=toward))
    w_out_first = remote(wout_ref, wo.at[landing], w_s.at[1], w_r.at[1], dev(dx=toward))
    w_in_next = remote(wi.at[:, upper], wi.at[:, upper], w_s.at[2], w_r.at[2], dev(dx=-1, to=1))
    w_out_next = remote(wo.at[lower], wo.at[upper], w_s.at[3], w_r.at[3], dev(dx=1, to=1))
    on_core(0, w_in_first.start, w_out_first.start, own_wi.start, own_wo.start)
    on_core(1, w_out_first.start, w_in_first.start)

    loads[0].wait()
    list_row = meta.at[pl.ds(pl.multiple_of(CODE + 8 * rep, 8), 8)]
    peers = [(0, 1), (1, 0), (1, 1), (2, 0), (2, 1), (3, 0), (3, 1)]
    peers = [(n, dev(dy=d, to=other if flip else core)) for n, (d, flip) in enumerate(peers)]
    list_copies = [remote(list_row, list_row, list_s.at[n], list_r.at[n], peer) for n, peer in peers]
    for copy in list_copies:
        copy.start()

    on_core(0, own_tok.wait, give_cot.wait)
    on_core(1, own_cot.wait, give_tok.wait)
    for c in range(4):
        at = slice(c * 512, (c + 1) * 512)
        mine, theirs = own[:, at].astype(F32), land[:, at].astype(F32)
        first, second = jnp.where(core == 0, mine, theirs), jnp.where(core == 0, theirs, mine)
        buf[core, 0:CHIP, at] = jnp.concatenate([first, second], axis=0).astype(BF16)

    def slot_of(way, hops):
        return hops if way == 0 else (NZ - hops) % NZ

    def rows_of(slot, sub):
        return pl.ds(slot * CHIP + SUBS[sub][0], SUBS[sub][1])

    def ring(way, hops, sub):
        return remote(
            buf.at[core, rows_of(slot_of(way, hops), sub)],
            buf.at[core, rows_of(slot_of(way, hops + 1), sub)],
            ring_s.at[way, hops, sub], ring_r.at[way, hops, sub],
            dev(dz=1 if way == 0 else -1),
        )

    def sibling(slot, sub):
        at = buf.at[core, rows_of(slot, sub)]
        return remote(at, at, sib_s.at[slot, sub], sib_r.at[slot, sub], dev(to=other))

    for turn in (0, 1):
        ring(0, 0, turn).start()
        ring(1, 0, 1 - turn).start()
    for sub in (0, 1):
        sibling(0, sub).start()
    for load in tables:
        load.start()

    def arrive(hops, turn):
        for way in (0, 1):
            sub = turn if way == 0 else 1 - turn
            ring(way, hops - 1, sub).wait_recv()
            if hops < 3 or (hops == 3 and turn == 0):
                ring(way, hops, sub).start()
            sibling(slot_of(way, hops), sub).start()

    loads[1].wait()
    loads[2].wait()
    invert(ordv, sgnv, meta)
    for copy in list_copies:
        copy.wait_recv()
    meta_first = remote(meta, meta2.at[other], meta_s.at[0], meta_r.at[0], dev(dx=toward))
    meta_next = remote(meta, meta2.at[1], meta_s.at[1], meta_r.at[1], dev(dx=2))
    meta_first.start()
    on_core(1, meta_next.start)

    @pl.when(core == 0)
    def _():
        meta2[0] = meta[...]

    gin[...] = jnp.zeros_like(gin)
    gout[...] = jnp.zeros_like(gout)

    arrive(1, 0)
    on_core(0, w_in_first.wait_recv, w_in_next.start)
    on_core(1, w_out_first.wait_recv, w_out_next.start)
    arrive(1, 1)
    for load in tables:
        load.wait()
    prepare(meta, momv, errv, medv, infov, acrossv)
    ready = [
        pltpu.make_async_copy(medv, med_ref, lsem.at[16]),
        pltpu.make_async_copy(infov, info_ref, lsem.at[17]),
        pltpu.make_async_copy(acrossv, across_ref, lsem.at[18]),
    ]
    for copy in ready:
        copy.start()
    arrive(2, 0)
    on_core(0, w_out_first.wait_recv, own_wi.wait, own_wo.wait)
    on_core(1, w_in_first.wait_recv)
    arrive(2, 1)
    meta_first.wait_recv()
    on_core(1, meta_next.wait_recv)
    for k in (0, 1):
        spots[k] = jnp.broadcast_to(compact(lists_of(meta2, k), 0), (LIVE, 128))
    ready += [
        pltpu.make_async_copy(meta2, codes_ref, lsem.at[21]),
        pltpu.make_async_copy(spots, spots_ref, lsem.at[22]),
    ]
    for copy in ready[3:]:
        copy.start()
    on_core(1, w_in_next.wait_recv, w_out_next.wait_recv)

    def wait_sibling(slots):
        for slot in slots:
            for sub in (0, 1):
                sibling(slot, sub).wait_recv()

    def work(i, carry):
        @pl.when(i == 0)
        def _():
            wait_sibling((0, 1, 7))

        @pl.when(i == 3)
        def _():
            arrive(3, 0)
            wait_sibling((2, 6))

        @pl.when(i == 5)
        def _():
            arrive(3, 1)
            wait_sibling((3, 5))

        @pl.when(i == 7)
        def _():
            ring(0, 3, 0).wait_recv()
            sibling(4, 0).start()
            ring(1, 3, 1).wait_recv()
            sibling(4, 1).start()
            wait_sibling((4,))

        slot = lax.rem(jnp.where(i % 2 == 1, (i + 1) // 2, NZ - i // 2), NZ)
        rows = pl.ds(pl.multiple_of(slot * CHIP, 16), CHIP)

        value, slope = gelu_pair(nn(buf[0, rows, :], wi[...]))
        back = nt(buf[1, rows, :], wo[...])
        hidden = value.astype(BF16)
        grad = (back * slope).astype(BF16)
        for c in range(4):
            at = slice(c * 512, (c + 1) * 512)
            gin[at, :] += tn(buf[0, rows, at], grad)
            gout[:, at] += tn(hidden, buf[1, rows, at])
        return carry

    lax.fori_loop(0, NZ, work, 0)

    for k in (1, 0):
        for h in range(2):
            at = slice(k * COLS + h * 128, k * COLS + (h + 1) * 128)
            ghl[k, h * 2048 : (h + 1) * 2048, :] = split2(gin[:, at])
        for q in range(16):
            part = gout[k * COLS : (k + 1) * COLS, q * 128 : (q + 1) * 128]
            ghl[k, 4096 + q * 256 : 4352 + q * 256, :] = split2(part)
        ready.append(pltpu.make_async_copy(ghl.at[k], ghl_ref.at[k], lsem.at[19 + k]))
        ready[-1].start()

    for copy in list_copies + [w_in_first, w_out_first, meta_first]:
        copy.wait_send()
    for way in (0, 1):
        for hops in range(4):
            for sub in (0, 1):
                if hops < 3 or sub == way:
                    ring(way, hops, sub).wait_send()
    for slot in range(NZ):
        for sub in (0, 1):
            sibling(slot, sub).wait_send()
    on_core(0, w_in_next.wait_send)
    on_core(1, w_out_next.wait_send, meta_next.wait_send)
    for copy in ready:
        copy.wait()


def sketch_kernel(
    ghl_ref, codes_ref, spots_ref, table_ref,
    ghl, codes, spots, outb, recvx, yb, recvy, tot, lsem, x_s, x_r, y_s, y_r, a_s, a_r,
):
    rep, shard = lax.axis_index("rep"), lax.axis_index("shard")
    y, core = rep // 2, rep % 2
    x, z = shard // NZ, shard % NZ
    other = 1 - core

    def dev(dx=0, dy=0, dz=0, to=None):
        c = core if to is None else to
        return {
            "rep": lax.rem(y + dy + NY, NY) * 2 + c,
            "shard": lax.rem(x + dx + NX, NX) * NZ + lax.rem(z + dz + NZ, NZ),
        }

    def remote(src, dst, send, recv, device):
        return pltpu.make_async_remote_copy(
            src_ref=src, dst_ref=dst, send_sem=send, recv_sem=recv, device_id=device, device_id_type=MESH
        )

    def on_core(c, *actions):
        @pl.when(core == c)
        def _():
            for action in actions:
                action()

    loads = [
        pltpu.make_async_copy(codes_ref, codes, lsem.at[0]),
        pltpu.make_async_copy(spots_ref, spots, lsem.at[1]),
        pltpu.make_async_copy(ghl_ref.at[1], ghl.at[1], lsem.at[2]),
        pltpu.make_async_copy(ghl_ref.at[0], ghl.at[0], lsem.at[3]),
    ]
    for load in loads:
        load.start()
    barrier = pltpu.get_barrier_semaphore()
    partners = [dev(dx=d, to=c) for d in (1, -1, 2) for c in (0, 1)]
    partners += [dev(dy=d, to=c) for d in (1, 2, 3) for c in (0, 1)] + [dev(to=other)]
    for partner in partners:
        pl.semaphore_signal(barrier, inc=1, device_id=partner, device_id_type=MESH)
    pl.semaphore_wait(barrier, len(partners))
    peers = [(0, 1), (1, 0), (1, 1), (2, 0), (2, 1), (3, 0), (3, 1)]
    peers = [(n, dev(dy=d, to=other if flip else core)) for n, (d, flip) in enumerate(peers)]
    loads[0].wait()
    loads[1].wait()

    def one_hot(code, parts):
        ramp = iota((256, 128), 0).astype(F32).astype(BF16)
        code = jnp.broadcast_to(code, (16, 128))
        sign = jnp.where((code & 1) == 1, 1.0, -1.0).astype(BF16)
        bucket = (code >> 1).astype(F32)
        rows = []
        for part in parts:
            spot = (bucket - 256.0 * part).astype(BF16)
            for g in range(16):
                rows.append(jnp.where(spot == ramp[g * 16 : (g + 1) * 16], sign, jnp.zeros_like(sign)))
        return jnp.concatenate(rows, axis=0)

    def sketch(k, left, right, listed):
        step = 8
        parts = left[1]

        def run(*sums):
            def chunk(t, carry):
                tiles = [ghl[k, pl.ds(pl.multiple_of((t * step + i) * 256, 256), 256), :] for i in range(step)]
                found = [codes[k, pl.ds(pl.multiple_of(j * 64 + t * 2 * step, 16), 2 * step), :] for j, _ in (left, right)]
                for unit in (0, 1):
                    pltpu.matmul_push_rhs(tiles[0], 0, unit)
                for i in range(step):
                    if i + 1 < step:
                        for unit in (0, 1):
                            pltpu.matmul_push_rhs(tiles[i + 1], (i + 1) % 2, unit)
                    for unit in (0, 1):
                        code = found[unit][2 * i : 2 * i + 2, :]
                        hot = [one_hot(code[n : n + 1, :], (left, right)[unit][1]) for n in (0, 1)]
                        pltpu.matmul_acc_lhs(sums[unit], jnp.concatenate(hot, axis=1), load_staged_rhs=i % 2)
                        if listed:
                            spot = spots[k, unit * 128 : (unit + 1) * 128, :] - (t * step + i) * 256
                            lane = iota((128, 128), 1)
                            hot = [jnp.where(spot == lane + 128 * n, 1.0, 0.0).astype(BF16) for n in (0, 1)]
                            pltpu.matmul_acc_lhs(sums[2 + unit], jnp.concatenate(hot, axis=1))
                return carry

            lax.fori_loop(0, 32 // step, chunk, 0)
            for unit in (0, 1):
                j, part = (left, right)[unit]
                total = pltpu.matmul_pop(sums[unit])
                start = LIVE + j * COUNT + part[0] * 256
                outb[k, start : start + len(part) * 256, :] = (total[:, :128] + total[:, 128:]).astype(BF16)
                if listed:
                    total = pltpu.matmul_pop(sums[2 + unit])
                    outb[k, unit * 128 : (unit + 1) * 128, :] = (total[:, :128] + total[:, 128:]).astype(BF16)

        rows = [256 * len(parts)] + ([128] if listed else [])
        pl.run_scoped(run, *[pltpu.ACC(mxu_id=unit)((n, 256), F32) for n in rows for unit in (0, 1)])

    def half_of(p):
        return PIECES[p][0] // 2, PIECES[p][1] // 2

    def quarter_of(p):
        return PIECES[p][0] // 8, PIECES[p][1] // 8

    def x_copy(k, p, h, slot, device):
        start, rows = half_of(p)
        return remote(
            outb.at[k, pl.ds(PIECES[p][0] + h * rows, rows)], recvx.at[slot, pl.ds(start, rows)],
            x_s.at[k, p, h], x_r.at[slot, p], device,
        )

    x_far = [[x_copy(1, p, h, 1 + 2 * core, dev(dx=1 + core, to=h)) for h in (0, 1)] for p in range(3)]
    x_near = [[x_copy(0, p, h, 2, dev(dx=-1, to=h)) for h in (0, 1)] for p in range(3)]
    x_home = [x_copy(0, p, 1, 0, dev(to=1)) for p in range(3)]

    def x_far_start(p):
        for copy in x_far[p]:
            copy.start()

    def x_near_start(p):
        start, rows = half_of(p)
        on_core(1, *[copy.start for copy in x_near[p]])

        @pl.when(core == 0)
        def _():
            x_home[p].start()
            recvx[0, start : start + rows, :] = outb[0, PIECES[p][0] : PIECES[p][0] + rows, :]

    def my_quarter(p):
        rows = PIECES[p][1] // 8
        return pl.ds(pl.multiple_of(PIECES[p][0] + core * (4 * rows) + y * rows, 16), rows)

    def y_copy(p, d):
        start, rows = quarter_of(p)
        there = pl.ds(pl.multiple_of(4 * start + lax.rem(y + d, NY) * rows, 16), rows)
        return remote(yb.at[there], recvy.at[d - 1, pl.ds(start, rows)], y_s.at[p, d - 1], y_r.at[p, d - 1], dev(dy=d))

    def y_start(p):
        start, rows = half_of(p)
        on_core(1, x_copy(0, p, 1, 0, dev(to=1)).wait_recv)
        for slot in (1, 2, 3):
            x_copy(1, p, 0, slot, dev(dx=1)).wait_recv()
        part = recvx[0, start : start + rows, :].astype(F32)
        for slot in (1, 2, 3):
            part = part + recvx[slot, start : start + rows, :].astype(F32)
        yb[start : start + rows, :] = part.astype(BF16)
        tot[pl.ds(pl.multiple_of(PIECES[p][0] + core * rows, 16), rows), :] = part
        for d in (1, 2, 3):
            y_copy(p, d).start()

    def a_copy(p, n, peer):
        at = tot.at[my_quarter(p)]
        return remote(at, at, a_s.at[p, n], a_r.at[p, n], peer)

    def a_start(p):
        start, rows = quarter_of(p)
        total = tot[my_quarter(p), :]
        for d in (1, 2, 3):
            y_copy(p, d).wait_recv()
            total = total + recvy[d - 1, start : start + rows, :].astype(F32)
        tot[my_quarter(p), :] = total
        for n, peer in peers:
            a_copy(p, n, peer).start()

    def step(t, carry):
        k = jnp.where(t < 3, 1, 0)
        part = lax.rem(t, 3)

        @pl.when(part == 0)
        def _():
            @pl.when(t == 0)
            def _():
                loads[2].wait()

            @pl.when(t == 3)
            def _():
                loads[3].wait()

            sketch(k, (0, (0, 1)), (1, (0, 1)), True)

        @pl.when(part == 1)
        def _():
            sketch(k, (2, (0, 1)), (3, (0, 1)), False)

        @pl.when(part == 2)
        def _():
            sketch(k, (4, (0,)), (4, (1,)), False)

        for when, action, p in (
            (0, x_far_start, 0), (1, x_far_start, 1), (2, x_far_start, 2),
            (3, x_near_start, 0), (4, x_near_start, 1), (4, y_start, 0), (5, x_near_start, 2), (5, a_start, 0),
            (5, y_start, 1),
        ):

            @pl.when(t == when)
            def _(action=action, p=p):
                action(p)

        return carry

    lax.fori_loop(0, 6, step, 0)
    y_start(2)
    a_start(1)
    a_start(2)
    for p in range(3):
        for n, peer in peers:
            a_copy(p, n, peer).wait_recv()
    result = pltpu.make_async_copy(tot, table_ref, lsem.at[4])
    result.start()

    for p in range(3):
        for copy in x_far[p] + [y_copy(p, d) for d in (1, 2, 3)] + [a_copy(p, n, peer) for n, peer in peers]:
            copy.wait_send()
    on_core(0, *[copy.wait_send for copy in x_home])
    on_core(1, *[c.wait_send for p in range(3) for c in x_near[p]])
    result.wait()


def run_main(tokens, cotangent, w_in, w_out, order, signs, lists, mom, err):
    anywhere = pl.BlockSpec(memory_space=pl.ANY)
    dma = pltpu.SemaphoreType.DMA
    return pl.pallas_call(
        main_kernel,
        out_shape=(
            jax.ShapeDtypeStruct((2, NB, 256), BF16),
            jax.ShapeDtypeStruct((2, META, 128), I32),
            jax.ShapeDtypeStruct((2, LIVE, 128), I32),
            jax.ShapeDtypeStruct((LIVE, 128), F32),
            jax.ShapeDtypeStruct((LIVE, 128), I32),
            jax.ShapeDtypeStruct((8, LIVE), I32),
        ),
        in_specs=[anywhere] * 9,
        out_specs=(anywhere,) * 6,
        scratch_shapes=[
            pltpu.VMEM((TOK, DW), BF16),
            pltpu.VMEM((TOK, DW), BF16),
            pltpu.VMEM((2, NZ * CHIP, DW), BF16),
            pltpu.VMEM((DW, 2 * COLS), BF16),
            pltpu.VMEM((2 * COLS, DW), BF16),
            pltpu.VMEM((DW, 2 * COLS), F32),
            pltpu.VMEM((2 * COLS, DW), F32),
            pltpu.VMEM((ROWS, NB), I32),
            pltpu.VMEM((ROWS, NB), I32),
            pltpu.VMEM((META, 128), I32),
            pltpu.VMEM((2, META, 128), I32),
            pltpu.VMEM((2, NB, 256), BF16),
            pltpu.VMEM((ROWS, COUNT, 128), F32),
            pltpu.VMEM((ROWS, COUNT, 128), F32),
            pltpu.VMEM((LIVE, 128), F32),
            pltpu.VMEM((LIVE, 128), I32),
            pltpu.VMEM((8, LIVE), I32),
            pltpu.VMEM((2, LIVE, 128), I32),
            dma((23,)), dma((2,)),
            dma((2, 4, 2)), dma((2, 4, 2)), dma((NZ, 2)), dma((NZ, 2)), dma((4,)), dma((4,)),
            dma((7,)), dma((7,)), dma((2,)), dma((2,)),
        ],
        compiler_params=pltpu.CompilerParams(
            collective_id=0, has_side_effects=True, vmem_limit_bytes=62 * 1024 * 1024
        ),
        cost_estimate=pl.CostEstimate(flops=15_000_000_000, bytes_accessed=20_000_000, transcendentals=2_000_000),
        name="gather_grad",
    )(tokens, cotangent, w_in, w_out, order, signs, lists, mom, err)


def run_sketch(ghl, codes, spots):
    anywhere = pl.BlockSpec(memory_space=pl.ANY)
    dma = pltpu.SemaphoreType.DMA
    return pl.pallas_call(
        sketch_kernel,
        out_shape=jax.ShapeDtypeStruct((TAB, 128), F32),
        in_specs=[anywhere] * 3,
        out_specs=anywhere,
        scratch_shapes=[
            pltpu.VMEM((2, NB, 256), BF16),
            pltpu.VMEM((2, META, 128), I32),
            pltpu.VMEM((2, LIVE, 128), I32),
            pltpu.VMEM((2, TAB, 128), BF16),
            pltpu.VMEM((4, TAB // 2, 128), BF16),
            pltpu.VMEM((TAB // 2, 128), BF16),
            pltpu.VMEM((3, TAB // 8, 128), BF16),
            pltpu.VMEM((TAB, 128), F32),
            dma((5,)), dma((2, 3, 2)), dma((4, 3)), dma((3, 3)), dma((3, 3)), dma((3, 7)), dma((3, 7)),
        ],
        compiler_params=pltpu.CompilerParams(
            collective_id=1, has_side_effects=True, vmem_limit_bytes=62 * 1024 * 1024
        ),
        cost_estimate=pl.CostEstimate(flops=24_000_000_000, bytes_accessed=10_000_000, transcendentals=0),
        name="sketch_reduce",
    )(ghl, codes, spots)


def finish_kernel(
    table, med, info, across, mom, err, w_in, w_out,
    win_new, wout_new, mom_new, err_new,
    tabv, medv, infov, acrossv, momv, errv, winv, woutv, winn, woutn, momn, errn, sem, out_sem,
):
    pairs = [(info, infov), (med, medv), (table, tabv), (across, acrossv), (w_in, winv), (w_out, woutv)]
    for j in range(ROWS):
        pairs += [(mom.at[:, j, :], momv.at[j]), (err.at[:, j, :], errv.at[j])]
    loads = [pltpu.make_async_copy(src, dst, sem.at[n]) for n, (src, dst) in enumerate(pairs)]
    for load in loads:
        load.start()
    stores = []

    def store(src, dst):
        stores.append(pltpu.make_async_copy(src, dst, out_sem.at[len(stores)]))
        stores[-1].start()

    for load in loads[:4]:
        load.wait()
    codes = infov[...]
    update = medv[...] + LEARN * tabv[:LIVE, :]
    kept = split2(jnp.where(codes[:, ROWS : ROWS + 1] == 1, update, 0.0))
    places = acrossv[0:1, :]

    def delta(start, rows):
        hit = jnp.where(iota((rows, LIVE), 0) + start == places, 1.0, 0.0).astype(BF16)
        got = nn(hit, kept)
        return got[:, :128] + got[:, 128:]

    loads[4].wait()
    for c in range(4):
        rows = pl.ds(c * 512, 512)
        for h in range(2):
            at = slice(h * 128, (h + 1) * 128)
            winn[rows, at] = winv[rows, at].astype(F32) - delta(h * 2048 + c * 512, 512)
        store(winn.at[rows], win_new.at[rows])
    loads[5].wait()
    for c in range(4):
        for q in range(4 * c, 4 * c + 4):
            at = slice(q * 128, (q + 1) * 128)
            woutn[:, at] = woutv[:, at].astype(F32) - delta(4096 + q * 256, 256)
        at = pl.ds(c * 512, 512)
        store(woutn.at[:, at], wout_new.at[:, at])
    for j in range(ROWS):
        loads[6 + 2 * j].wait()
        loads[7 + 2 * j].wait()
        fresh = DECAY * momv[j] + tabv[LIVE + j * COUNT : LIVE + (j + 1) * COUNT, :]
        momn[j] = fresh
        store(momn.at[j], mom_new.at[:, j, :])
        gone = tn(signed_hit(codes[:, j : j + 1]), kept)
        errn[j] = errv[j] + LEARN * fresh - (gone[:, :128] + gone[:, 128:])
        store(errn.at[j], err_new.at[:, j, :])
    for copy in stores:
        copy.wait()


def run_finish(table, med, info, across, mom, err, w_in, w_out):
    anywhere = pl.BlockSpec(memory_space=pl.ANY)
    vmem = pltpu.VMEM
    deep = vmem((ROWS, COUNT, 128), F32)
    return pl.pallas_call(
        finish_kernel,
        out_shape=(
            jax.ShapeDtypeStruct(w_in.shape, F32),
            jax.ShapeDtypeStruct(w_out.shape, F32),
            jax.ShapeDtypeStruct(mom.shape, F32),
            jax.ShapeDtypeStruct(err.shape, F32),
        ),
        in_specs=[anywhere] * 8,
        out_specs=(anywhere,) * 4,
        scratch_shapes=[
            vmem((TAB, 128), F32), vmem((LIVE, 128), F32), vmem((LIVE, 128), I32), vmem((8, LIVE), I32),
            deep, deep, vmem(w_in.shape, BF16), vmem(w_out.shape, BF16), vmem(w_in.shape, F32), vmem(w_out.shape, F32),
            deep, deep, pltpu.SemaphoreType.DMA((16,)), pltpu.SemaphoreType.DMA((18,)),
        ],
        compiler_params=pltpu.CompilerParams(vmem_limit_bytes=62 * 1024 * 1024),
        cost_estimate=pl.CostEstimate(flops=3_000_000_000, bytes_accessed=16_000_000, transcendentals=0),
        name="finish",
    )(table, med, info, across, mom, err, w_in, w_out)


def per_device(
    tokens, cotangent, w_in, w_out, momentum, error, block_order, signs, heavy_blocks, heavy_count
):
    listed = jnp.concatenate([heavy_blocks, jnp.broadcast_to(heavy_count, heavy_blocks.shape)], axis=1)
    here = lax.broadcasted_iota(I32, (8, 128), 0) == lax.axis_index("rep")
    lists = jnp.where(here, listed, 0)
    mom, err = by_bucket(momentum), by_bucket(error)
    ghl, codes, spots, med, info, across = run_main(
        tokens, cotangent, w_in, w_out, block_order, signs, lists, mom, err
    )
    table = run_sketch(ghl, codes, spots)
    win_new, wout_new, mom_new, err_new = run_finish(table, med, info, across, mom, err, w_in, w_out)
    return win_new, wout_new, by_row(mom_new), by_row(err_new)


def by_bucket(table):
    return jnp.transpose(table.reshape(ROWS, COUNT, 128), (1, 0, 2))


def by_row(table):
    return jnp.transpose(table, (1, 0, 2)).reshape(ROWS, COUNT * 128)


def solution(mesh):
    placed = (
        P(("rep", "shard"), None),
        P(("rep", "shard"), None),
        P(None, "shard"),
        P("shard", None),
        P(None, "shard"),
        P(None, "shard"),
        P(None, "shard"),
        P(None, "shard"),
        P("rep", "shard"),
        P("rep", "shard"),
    )
    return jax.shard_map(
        per_device,
        mesh=mesh,
        in_specs=placed,
        out_specs=(P(None, "shard"), P("shard", None), P(None, "shard"), P(None, "shard")),
        check_vma=False,
    )
```

```python
import functools

import jax
import jax.numpy as jnp
from jax import lax
from jax.experimental import pallas as pl
from jax.experimental.pallas import tpu as pltpu
from jax.sharding import PartitionSpec as P

MESH = pl.DeviceIdType.MESH
F32, BF16, I32 = jnp.float32, jnp.bfloat16, jnp.int32
LEARN = 0.05
DECAY = 0.9
ROOT = 0.7978845608028654

NX, NY, NZ = 4, 4, 8
TOK = 104
CHIP = 2 * TOK
SUBS = ((0, 112), (112, 96))
DW, COLS = 2048, 256
NB = 8192
COUNT = 512
ROWS = 5
LIVE = 256
TAB = LIVE + ROWS * COUNT
PIECES = ((0, 1280), (1280, 1024), (2304, 512))
CODE = ROWS * 64
META = CODE + 64


def nt(a, b):
    return lax.dot_general(a, b, (((1,), (1,)), ((), ())), preferred_element_type=F32)


def tn(a, b):
    return lax.dot_general(a, b, (((0,), (0,)), ((), ())), preferred_element_type=F32)


def nn(a, b):
    return jnp.dot(a, b, preferred_element_type=F32)


def iota(shape, dim):
    return lax.broadcasted_iota(I32, shape, dim)


def split2(x):
    hi = x.astype(BF16)
    return jnp.concatenate([hi, (x - hi.astype(F32)).astype(BF16)], axis=1)


def place_of(block):
    rest = block - 4096
    return jnp.where(
        block < 4096, (block & 1) * 2048 + (block >> 1), 4096 + (rest & 15) * 256 + (rest >> 4)
    )


def gelu_pair(pre):
    tangent = jnp.tanh(ROOT * (pre + 0.044715 * pre * pre * pre))
    value = 0.5 * pre * (1.0 + tangent)
    slope = 0.5 * (1.0 + tangent) + 0.5 * pre * (1.0 - tangent * tangent) * ROOT * (
        1.0 + 0.134145 * pre * pre
    )
    return value, slope


def invert(ord_ref, sgn_ref, meta_ref):
    step = 1024
    for j in range(ROWS):

        def body(c, acc, j=j):
            at = pl.ds(pl.multiple_of(c * step, step), step)
            place = place_of(ord_ref[j : j + 1, at])
            sign = sgn_ref[j : j + 1, at]
            bucket = (c * step + iota((1, step), 1)) >> 4
            row = iota((128, step), 0)
            value = jnp.where(row < 64, bucket >> 1, (bucket & 1) * 2 + sign)
            left = jnp.where((row & 63) == (place >> 7), value, 0).astype(F32).astype(BF16)
            right = jnp.where(row == (place & 127), 1.0, 0.0).astype(BF16)
            return acc + nt(left, right)

        acc = lax.fori_loop(0, NB // step, body, jnp.zeros((128, 128), F32))
        meta_ref[j * 64 : (j + 1) * 64, :] = (acc[:64] * 4.0 + acc[64:]).astype(I32)


def compact(lists, along):
    full = jnp.concatenate([lists, jnp.zeros((120, 128), I32)], axis=0)
    shape = (LIVE, 128)
    slot, lane = iota(shape, 0), iota(shape, 1)
    wanted = jnp.where(slot < 128, slot & 15, jnp.where(slot < 176, slot - 112, 127))
    pick = jnp.where(lane == wanted, 1.0, 0.0).astype(BF16)
    pick_count = jnp.where(lane == 64, 1.0, 0.0).astype(BF16)
    high = (full >> 7).astype(F32).astype(BF16)
    low = (full & 127).astype(F32).astype(BF16)
    if along == 0:
        values = nt(pick, high) * 128.0 + nt(pick, low)
        counts = nt(pick_count, low)
        spot, rep, axis = slot, lane, 1
    else:
        values = nt(high, pick) * 128.0 + nt(low, pick)
        counts = nt(low, pick_count)
        spot, rep, axis = iota((128, LIVE), 1), iota((128, LIVE), 0), 0
    first = (spot < 128) & (rep == (spot >> 4)) & (counts > (spot & 15).astype(F32))
    later = (spot >= 128) & (spot < 176) & (rep < 8) & (counts > 63.5)
    hit = jnp.where(first | later, 1.0, 0.0)
    live = jnp.sum(hit, axis=axis, keepdims=True)
    block = jnp.sum(hit * values, axis=axis, keepdims=True).astype(I32)
    return jnp.where(live > 0.5, place_of(block), -1)


def lists_of(meta_ref, *lead):
    total = jnp.zeros((8, 128), I32)
    for r in range(8):
        total = total + meta_ref[(*lead, slice(CODE + 8 * r, CODE + 8 * r + 8), slice(None))]
    return total


def middle_value(values):
    values = list(values)
    total = len(values)
    for rounds in range(total):
        for i in range(rounds % 2, total - 1, 2):
            lower = jnp.minimum(values[i], values[i + 1])
            upper = jnp.maximum(values[i], values[i + 1])
            values[i] = lower
            values[i + 1] = upper
    return values[total // 2]


def prepare(meta, momv, errv, medv, infov, acrossv):
    lists = lists_of(meta)
    down, across = compact(lists, 0), compact(lists, 1)
    shape = (LIVE, LIVE)
    same = (down == across) & (across >= 0) & (iota(shape, 1) < iota(shape, 0))
    earlier = jnp.max(jnp.where(same, 1.0, 0.0), axis=1, keepdims=True)
    keep = jnp.where((down >= 0) & (earlier < 0.5), 1, 0)
    codes = meta[...]
    high = (codes >> 2).astype(F32).astype(BF16)
    low = (codes & 3).astype(F32).astype(BF16)
    lane = iota((LIVE, 128), 1)
    lane_hit = lane == (down & 127)
    info = jnp.where(lane == ROWS, keep, 0)
    found = []
    for j in range(ROWS):
        pick = jnp.where(iota((LIVE, META), 1) == (down >> 7) + j * 64, 1.0, 0.0)
        pick = jnp.where(down >= 0, pick, 0.0).astype(BF16)
        value = nn(pick, high) * 4.0 + nn(pick, low)
        code = jnp.sum(jnp.where(lane_hit, value, 0.0), axis=1, keepdims=True).astype(I32)
        info = jnp.where(lane == j, code, info)
        probe = errv[j] + LEARN * DECAY * momv[j]
        got = nn(signed_hit(code), split2(probe))
        found.append(got[:, :128] + got[:, 128:])
    medv[...] = middle_value(found)
    infov[...] = info
    acrossv[...] = jnp.broadcast_to(across, acrossv.shape)


def signed_hit(code):
    sign = jnp.where((code & 1) == 1, 1.0, -1.0)
    return jnp.where(iota((LIVE, COUNT), 1) == (code >> 1), sign, 0.0).astype(BF16)


def main_kernel(
    tok_ref, cot_ref, win_ref, wout_ref, ord_ref, sgn_ref, lst_ref, cnt_ref, mom_ref, err_ref,
    ghl_ref, codes_ref, spots_ref, med_ref, info_ref, across_ref,
    own, land, buf, wi, wo, gin, gout, ordv, sgnv, meta, meta2, ghl,
    momv, errv, medv, infov, acrossv, spots, lstv,
    lsem, land_sem, ring_s, ring_r, sib_s, sib_r, w_s, w_r, list_s, list_r, meta_s, meta_r,
):
    rep, shard = lax.axis_index("rep"), lax.axis_index("shard")
    y, core = rep // 2, rep % 2
    x, z = shard // NZ, shard % NZ
    other = 1 - core

    def dev(dx=0, dy=0, dz=0, to=None):
        c = core if to is None else to
        return {
            "rep": lax.rem(y + dy + NY, NY) * 2 + c,
            "shard": lax.rem(x + dx + NX, NX) * NZ + lax.rem(z + dz + NZ, NZ),
        }

    def remote(src, dst, send, recv, device):
        return pltpu.make_async_remote_copy(
            src_ref=src, dst_ref=dst, send_sem=send, recv_sem=recv, device_id=device, device_id_type=MESH
        )

    def on_core(c, *actions):
        @pl.when(core == c)
        def _():
            for action in actions:
                action()

    own_tok = pltpu.make_async_copy(tok_ref, own, lsem.at[0])
    own_cot = pltpu.make_async_copy(cot_ref, own, lsem.at[0])
    loads = [
        pltpu.make_async_copy(lst_ref, lstv, lsem.at[1]),
        pltpu.make_async_copy(ord_ref, ordv, lsem.at[2]),
        pltpu.make_async_copy(sgn_ref, sgnv, lsem.at[3]),
    ]
    tables = [pltpu.make_async_copy(mom_ref.at[:, j, :], momv.at[j], lsem.at[6 + j]) for j in range(ROWS)]
    tables += [pltpu.make_async_copy(err_ref.at[:, j, :], errv.at[j], lsem.at[11 + j]) for j in range(ROWS)]
    own_wi = pltpu.make_async_copy(win_ref, wi.at[:, pl.ds(0, COLS)], lsem.at[4])
    own_wo = pltpu.make_async_copy(wout_ref, wo.at[pl.ds(0, COLS)], lsem.at[5])
    on_core(0, own_tok.start)
    on_core(1, own_cot.start)
    for load in loads:
        load.start()

    barrier = pltpu.get_barrier_semaphore()
    partners = [dev(dz=1), dev(dz=-1)]
    partners += [dev(dx=d, to=c) for d in (1, -1, 2) for c in (0, 1)]
    partners += [dev(dy=d, to=c) for d in (1, 2, 3) for c in (0, 1)] + [dev(to=other)]
    for partner in partners:
        pl.semaphore_signal(barrier, inc=1, device_id=partner, device_id_type=MESH)
    pl.semaphore_wait(barrier, len(partners))

    give_cot = remote(cot_ref, land, land_sem.at[0], land_sem.at[1], dev(to=other))
    give_tok = remote(tok_ref, land, land_sem.at[0], land_sem.at[1], dev(to=other))
    on_core(0, give_cot.start)
    on_core(1, give_tok.start)

    toward = jnp.where(core == 0, -1, 1)
    lower, upper = pl.ds(0, COLS), pl.ds(COLS, COLS)
    landing = pl.ds(pl.multiple_of(other * COLS, COLS), COLS)
    w_in_first = remote(win_ref, wi.at[:, landing], w_s.at[0], w_r.at[0], dev(dx=toward))
    w_out_first = remote(wout_ref, wo.at[landing], w_s.at[1], w_r.at[1], dev(dx=toward))
    w_in_next = remote(wi.at[:, upper], wi.at[:, upper], w_s.at[2], w_r.at[2], dev(dx=-1, to=1))
    w_out_next = remote(wo.at[lower], wo.at[upper], w_s.at[3], w_r.at[3], dev(dx=1, to=1))
    on_core(0, w_in_first.start, w_out_first.start, own_wi.start, own_wo.start)
    on_core(1, w_out_first.start, w_in_first.start)

    loads[0].wait()
    listed = jnp.concatenate([lstv[...], jnp.full(lstv.shape, cnt_ref[0, 0], I32)], axis=1)
    meta[pl.ds(pl.multiple_of(CODE + 8 * rep, 8), 8), :] = jnp.where(iota((8, 128), 0) == rep, listed, 0)
    list_row = meta.at[pl.ds(pl.multiple_of(CODE + 8 * rep, 8), 8)]
    peers = [(0, 1), (1, 0), (1, 1), (2, 0), (2, 1), (3, 0), (3, 1)]
    peers = [(n, dev(dy=d, to=other if flip else core)) for n, (d, flip) in enumerate(peers)]
    list_copies = [remote(list_row, list_row, list_s.at[n], list_r.at[n], peer) for n, peer in peers]
    for copy in list_copies:
        copy.start()

    on_core(0, own_tok.wait, give_cot.wait)
    on_core(1, own_cot.wait, give_tok.wait)
    for c in range(4):
        at = slice(c * 512, (c + 1) * 512)
        mine, theirs = own[:, at].astype(F32), land[:, at].astype(F32)
        first, second = jnp.where(core == 0, mine, theirs), jnp.where(core == 0, theirs, mine)
        buf[core, 0:CHIP, at] = jnp.concatenate([first, second], axis=0).astype(BF16)

    def slot_of(way, hops):
        return hops if way == 0 else (NZ - hops) % NZ

    def rows_of(slot, sub):
        return pl.ds(slot * CHIP + SUBS[sub][0], SUBS[sub][1])

    def ring(way, hops, sub):
        return remote(
            buf.at[core, rows_of(slot_of(way, hops), sub)],
            buf.at[core, rows_of(slot_of(way, hops + 1), sub)],
            ring_s.at[way, hops, sub], ring_r.at[way, hops, sub],
            dev(dz=1 if way == 0 else -1),
        )

    def sibling(slot, sub):
        at = buf.at[core, rows_of(slot, sub)]
        return remote(at, at, sib_s.at[slot, sub], sib_r.at[slot, sub], dev(to=other))

    for turn in (0, 1):
        ring(0, 0, turn).start()
        ring(1, 0, 1 - turn).start()
    for sub in (0, 1):
        sibling(0, sub).start()
    for load in tables:
        load.start()

    def arrive(hops, turn):
        for way in (0, 1):
            sub = turn if way == 0 else 1 - turn
            ring(way, hops - 1, sub).wait_recv()
            if hops < 3 or (hops == 3 and turn == 0):
                ring(way, hops, sub).start()
            sibling(slot_of(way, hops), sub).start()

    loads[1].wait()
    loads[2].wait()
    invert(ordv, sgnv, meta)
    for copy in list_copies:
        copy.wait_recv()
    meta_first = remote(meta, meta2.at[other], meta_s.at[0], meta_r.at[0], dev(dx=toward))
    meta_next = remote(meta, meta2.at[1], meta_s.at[1], meta_r.at[1], dev(dx=2))
    meta_first.start()
    on_core(1, meta_next.start)

    @pl.when(core == 0)
    def _():
        meta2[0] = meta[...]

    gin[...] = jnp.zeros_like(gin)
    gout[...] = jnp.zeros_like(gout)

    arrive(1, 0)
    on_core(0, w_in_first.wait_recv, w_in_next.start)
    on_core(1, w_out_first.wait_recv, w_out_next.start)
    arrive(1, 1)
    for load in tables:
        load.wait()
    prepare(meta, momv, errv, medv, infov, acrossv)
    ready = [
        pltpu.make_async_copy(medv, med_ref, lsem.at[16]),
        pltpu.make_async_copy(infov, info_ref, lsem.at[17]),
        pltpu.make_async_copy(acrossv, across_ref, lsem.at[18]),
    ]
    for copy in ready:
        copy.start()
    meta_first.wait_recv()
    on_core(1, meta_next.wait_recv)
    for k in (0, 1):
        spots[k] = jnp.broadcast_to(compact(lists_of(meta2, k), 0), (LIVE, 128))
    ready += [
        pltpu.make_async_copy(meta2, codes_ref, lsem.at[21]),
        pltpu.make_async_copy(spots, spots_ref, lsem.at[22]),
    ]
    for copy in ready[3:]:
        copy.start()
    arrive(2, 0)
    on_core(0, w_out_first.wait_recv, own_wi.wait, own_wo.wait)
    on_core(1, w_in_first.wait_recv, w_in_next.wait_recv, w_out_next.wait_recv)

    def slots_of(hops, turn):
        return (hops, (NZ - hops) % NZ) if turn == 0 else ((NZ - hops) % NZ, hops)

    def wait_sibling(hops, turn):
        for sub, slot in enumerate(slots_of(hops, turn)):
            sibling(slot, sub).wait_recv()

    out_first = pltpu.make_async_copy(ghl.at[:, pl.ds(0, 4096)], ghl_ref.at[:, pl.ds(0, 4096)], lsem.at[19])
    out_last = pltpu.make_async_copy(ghl.at[:, pl.ds(4096, 4096)], ghl_ref.at[:, pl.ds(4096, 4096)], lsem.at[20])
    ready += [out_first, out_last]

    def work(i, carry):
        @pl.when(i == 0)
        def _():
            for hops, turn in ((0, 0), (1, 0), (1, 1), (2, 0)):
                wait_sibling(hops, turn)

        @pl.when(i == 2)
        def _():
            arrive(2, 1)

        @pl.when(i == 4)
        def _():
            wait_sibling(2, 1)
            arrive(3, 0)

        @pl.when(i == 5)
        def _():
            wait_sibling(3, 0)

        @pl.when(i == 6)
        def _():
            arrive(3, 1)
            wait_sibling(3, 1)

        @pl.when(i == 7)
        def _():
            ring(0, 3, 0).wait_recv()
            sibling(4, 0).start()
            ring(1, 3, 1).wait_recv()
            sibling(4, 1).start()
            wait_sibling(4, 0)

        hops = (i + 1) // 2
        slot_a = lax.rem(jnp.where(i % 2 == 1, hops, NZ - hops), NZ)
        slot_b = lax.rem(NZ - slot_a, NZ)
        rows_a = pl.ds(pl.multiple_of(slot_a * CHIP, 16), SUBS[0][1])
        rows_b = pl.ds(pl.multiple_of(slot_b * CHIP + SUBS[1][0], 16), SUBS[1][1])

        def rows(kind, at):
            return jnp.concatenate([buf[kind, rows_a, at], buf[kind, rows_b, at]], axis=0)

        everything = slice(None)
        value, slope = gelu_pair(nn(rows(0, everything), wi[...]))
        back = nt(rows(1, everything), wo[...])
        hidden = value.astype(BF16)
        grad = (back * slope).astype(BF16)
        for c in range(4):
            at = slice(c * 512, (c + 1) * 512)
            total = gin[at, :] + tn(rows(0, at), grad)

            @pl.when(i < 7)
            def _(at=at, total=total):
                gin[at, :] = total

            @pl.when(i == 7)
            def _(c=c, total=total):
                for k in range(2):
                    for h in range(2):
                        part = total[:, k * COLS + h * 128 : k * COLS + (h + 1) * 128]
                        ghl[k, h * 2048 + c * 512 : h * 2048 + (c + 1) * 512, :] = split2(part)

        @pl.when(i == 7)
        def _():
            out_first.start()

        for c in range(4):
            at = slice(c * 512, (c + 1) * 512)
            total = gout[:, at] + tn(hidden, rows(1, at))

            @pl.when(i < 7)
            def _(at=at, total=total):
                gout[:, at] = total

            @pl.when(i == 7)
            def _(c=c, total=total):
                for k in range(2):
                    for q in range(4 * c, 4 * c + 4):
                        part = total[k * COLS : (k + 1) * COLS, (q - 4 * c) * 128 : (q - 4 * c + 1) * 128]
                        ghl[k, 4096 + q * 256 : 4352 + q * 256, :] = split2(part)

        return carry

    lax.fori_loop(0, NZ, work, 0)
    out_last.start()

    for copy in list_copies + [w_in_first, w_out_first, meta_first]:
        copy.wait_send()
    for way in (0, 1):
        for hops in range(4):
            for sub in (0, 1):
                if hops < 3 or sub == way:
                    ring(way, hops, sub).wait_send()
    for slot in range(NZ):
        for sub in (0, 1):
            sibling(slot, sub).wait_send()
    on_core(0, w_in_next.wait_send)
    on_core(1, w_out_next.wait_send, meta_next.wait_send)
    for copy in ready:
        copy.wait()


def sketch_kernel(
    ghl_ref, codes_ref, spots_ref, table_ref,
    ghl, codes, spots, outb, recvx, yb, recvy, tot, lsem, x_s, x_r, y_s, y_r, a_s, a_r,
):
    rep, shard = lax.axis_index("rep"), lax.axis_index("shard")
    y, core = rep // 2, rep % 2
    x, z = shard // NZ, shard % NZ
    other = 1 - core

    def dev(dx=0, dy=0, dz=0, to=None):
        c = core if to is None else to
        return {
            "rep": lax.rem(y + dy + NY, NY) * 2 + c,
            "shard": lax.rem(x + dx + NX, NX) * NZ + lax.rem(z + dz + NZ, NZ),
        }

    def remote(src, dst, send, recv, device):
        return pltpu.make_async_remote_copy(
            src_ref=src, dst_ref=dst, send_sem=send, recv_sem=recv, device_id=device, device_id_type=MESH
        )

    def on_core(c, *actions):
        @pl.when(core == c)
        def _():
            for action in actions:
                action()

    loads = [
        pltpu.make_async_copy(codes_ref, codes, lsem.at[0]),
        pltpu.make_async_copy(spots_ref, spots, lsem.at[1]),
        pltpu.make_async_copy(ghl_ref.at[1], ghl.at[1], lsem.at[2]),
        pltpu.make_async_copy(ghl_ref.at[0], ghl.at[0], lsem.at[3]),
    ]
    for load in loads:
        load.start()
    barrier = pltpu.get_barrier_semaphore()
    partners = [dev(dx=d, to=c) for d in (1, -1, 2) for c in (0, 1)]
    partners += [dev(dy=d) for d in (1, 2, 3)] + [dev(to=other)]
    for partner in partners:
        pl.semaphore_signal(barrier, inc=1, device_id=partner, device_id_type=MESH)
    pl.semaphore_wait(barrier, len(partners))
    loads[0].wait()
    loads[1].wait()

    def spread(code):
        code = jnp.broadcast_to(code, (16, 128))
        bucket = (code >> 1).astype(F32)
        return jnp.where((code & 1) == 1, 1.0, -1.0).astype(BF16), [(bucket - 256.0 * h).astype(BF16) for h in (0, 1)]

    def one_hot(spread_code, quarter):
        sign, spot = spread_code[0], spread_code[1][quarter // 2]
        ramp = iota((256, 128), 0).astype(F32).astype(BF16)
        first = 8 * (quarter % 2)
        hits = [spot == ramp[g * 16 : (g + 1) * 16] for g in range(first, first + 8)]
        return jnp.concatenate([jnp.where(hit, sign, jnp.zeros_like(sign)) for hit in hits], axis=0)

    def sketch(k, work):
        step = 8
        count = len(work[0])

        def run(*sums):
            def chunk(t, carry):
                tiles = [ghl[k, pl.ds(pl.multiple_of((t * step + i) * 256, 256), 256), :] for i in range(step)]
                used = sorted({j for part in work[0] + work[1] for j in part[:1] if j is not None})
                found = {j: codes[k, pl.ds(pl.multiple_of(j * 64 + t * 2 * step, 16), 2 * step), :] for j in used}
                for unit in (0, 1):
                    pltpu.matmul_push_rhs(tiles[0], 0, unit)
                for i in range(step):
                    if i + 1 < step:
                        for unit in (0, 1):
                            pltpu.matmul_push_rhs(tiles[i + 1], (i + 1) % 2, unit)
                    rows = {j: [spread(found[j][2 * i + n : 2 * i + n + 1, :]) for n in (0, 1)] for j in used}
                    for c in range(count):
                        for unit in (0, 1):
                            j, q = work[unit][c]
                            if j is None:
                                spot = spots[k, q * 128 : (q + 1) * 128, :] - (t * step + i) * 256
                                lane = iota((128, 128), 1)
                                hot = [jnp.where(spot == lane + 128 * n, 1.0, 0.0).astype(BF16) for n in (0, 1)]
                            else:
                                hot = [one_hot(rows[j][n], q) for n in (0, 1)]
                            pltpu.matmul_acc_lhs(
                                sums[2 * c + unit],
                                jnp.concatenate(hot, axis=1),
                                load_staged_rhs=i % 2 if c == 0 else None,
                            )
                return carry

            lax.fori_loop(0, 32 // step, chunk, 0)
            for c in range(count):
                for unit in (0, 1):
                    j, q = work[unit][c]
                    total = pltpu.matmul_pop(sums[2 * c + unit])
                    start = q * 128 + (0 if j is None else LIVE + j * COUNT)
                    outb[k, start : start + 128, :] = (total[:, :128] + total[:, 128:]).astype(BF16)

        pl.run_scoped(run, *[pltpu.ACC(mxu_id=unit)((128, 256), F32) for c in range(count) for unit in (0, 1)])

    def whole(j):
        return [(j, q) for q in range(4)]

    def half_of(p):
        return PIECES[p][0] // 2, PIECES[p][1] // 2

    def quarter_of(p):
        return PIECES[p][0] // 8, PIECES[p][1] // 8

    def x_copy(k, p, h, slot, device):
        start, rows = half_of(p)
        return remote(
            outb.at[k, pl.ds(PIECES[p][0] + h * rows, rows)], recvx.at[slot, pl.ds(start, rows)],
            x_s.at[k, p, h], x_r.at[slot, p], device,
        )

    x_far = [[x_copy(1, p, h, 1 + 2 * core, dev(dx=1 + core, to=h)) for h in (0, 1)] for p in range(3)]
    x_near = [[x_copy(0, p, h, 2, dev(dx=-1, to=h)) for h in (0, 1)] for p in range(3)]
    x_home = [x_copy(0, p, 1, 0, dev(to=1)) for p in range(3)]

    def x_far_start(p):
        for copy in x_far[p]:
            copy.start()

    def x_near_start(p):
        start, rows = half_of(p)
        on_core(1, *[copy.start for copy in x_near[p]])

        @pl.when(core == 0)
        def _():
            x_home[p].start()
            recvx[0, start : start + rows, :] = outb[0, PIECES[p][0] : PIECES[p][0] + rows, :]

    def my_quarter(p):
        rows = PIECES[p][1] // 8
        return pl.ds(pl.multiple_of(PIECES[p][0] + core * (4 * rows) + y * rows, 16), rows)

    def y_copy(p, d):
        start, rows = quarter_of(p)
        there = pl.ds(pl.multiple_of(4 * start + lax.rem(y + d, NY) * rows, 16), rows)
        return remote(yb.at[there], recvy.at[d - 1, pl.ds(start, rows)], y_s.at[p, d - 1], y_r.at[p, d - 1], dev(dy=d))

    def y_start(p):
        start, rows = half_of(p)
        on_core(1, x_copy(0, p, 1, 0, dev(to=1)).wait_recv)
        for slot in (1, 2, 3):
            x_copy(1, p, 0, slot, dev(dx=1)).wait_recv()
        part = recvx[0, start : start + rows, :].astype(F32)
        for slot in (1, 2, 3):
            part = part + recvx[slot, start : start + rows, :].astype(F32)
        yb[start : start + rows, :] = part.astype(BF16)
        tot[pl.ds(pl.multiple_of(PIECES[p][0] + core * rows, 16), rows), :] = part
        for d in (1, 2, 3):
            y_copy(p, d).start()

    def a_copy(p, d):
        at = tot.at[my_quarter(p)]
        return remote(at, at, a_s.at[p, d - 1], a_r.at[p, d - 1], dev(dy=d))

    def a_start(p):
        start, rows = quarter_of(p)
        total = tot[my_quarter(p), :]
        for d in (1, 2, 3):
            y_copy(p, d).wait_recv()
            total = total + recvy[d - 1, start : start + rows, :].astype(F32)
        tot[my_quarter(p), :] = total
        for d in (1, 2, 3):
            a_copy(p, d).start()

    def e_copy(p):
        rows = PIECES[p][1] // 2
        at = tot.at[pl.ds(pl.multiple_of(PIECES[p][0] + core * rows, 16), rows)]
        return remote(at, at, a_s.at[p, 3], a_r.at[p, 3], dev(to=other))

    def e_start(p):
        for d in (1, 2, 3):
            a_copy(p, d).wait_recv()
        e_copy(p).start()

    loads[2].wait()
    sketch(1, (whole(0) + whole(2), whole(1) + whole(3)))
    x_far_start(1)
    sketch(1, ([(4, 0), (4, 1), (None, 0)], [(4, 2), (4, 3), (None, 1)]))
    x_far_start(0)
    x_far_start(2)
    loads[3].wait()
    sketch(0, (whole(0) + [(None, 0)], whole(1) + [(None, 1)]))
    x_near_start(0)
    sketch(0, (whole(2), whole(3)))
    x_near_start(1)
    y_start(0)
    sketch(0, ([(4, 0), (4, 1)], [(4, 2), (4, 3)]))
    x_near_start(2)
    a_start(0)
    y_start(1)
    y_start(2)
    a_start(1)
    a_start(2)
    for p in range(3):
        e_start(p)
    for p in range(3):
        e_copy(p).wait_recv()
    result = pltpu.make_async_copy(tot, table_ref, lsem.at[4])
    result.start()

    for p in range(3):
        for copy in x_far[p] + [y_copy(p, d) for d in (1, 2, 3)] + [a_copy(p, d) for d in (1, 2, 3)] + [e_copy(p)]:
            copy.wait_send()
    on_core(0, *[copy.wait_send for copy in x_home])
    on_core(1, *[c.wait_send for p in range(3) for c in x_near[p]])
    result.wait()


def run_main(*args):
    anywhere = pl.BlockSpec(memory_space=pl.ANY)
    dma = pltpu.SemaphoreType.DMA
    return pl.pallas_call(
        main_kernel,
        out_shape=(
            jax.ShapeDtypeStruct((2, NB, 256), BF16),
            jax.ShapeDtypeStruct((2, META, 128), I32),
            jax.ShapeDtypeStruct((2, LIVE, 128), I32),
            jax.ShapeDtypeStruct((LIVE, 128), F32),
            jax.ShapeDtypeStruct((LIVE, 128), I32),
            jax.ShapeDtypeStruct((8, LIVE), I32),
        ),
        in_specs=[anywhere] * 7 + [pl.BlockSpec(memory_space=pltpu.SMEM)] + [anywhere] * 2,
        out_specs=(anywhere,) * 6,
        scratch_shapes=[
            pltpu.VMEM((TOK, DW), BF16),
            pltpu.VMEM((TOK, DW), BF16),
            pltpu.VMEM((2, NZ * CHIP, DW), BF16),
            pltpu.VMEM((DW, 2 * COLS), BF16),
            pltpu.VMEM((2 * COLS, DW), BF16),
            pltpu.VMEM((DW, 2 * COLS), F32),
            pltpu.VMEM((2 * COLS, DW), F32),
            pltpu.VMEM((ROWS, NB), I32),
            pltpu.VMEM((ROWS, NB), I32),
            pltpu.VMEM((META, 128), I32),
            pltpu.VMEM((2, META, 128), I32),
            pltpu.VMEM((2, NB, 256), BF16),
            pltpu.VMEM((ROWS, COUNT, 128), F32),
            pltpu.VMEM((ROWS, COUNT, 128), F32),
            pltpu.VMEM((LIVE, 128), F32),
            pltpu.VMEM((LIVE, 128), I32),
            pltpu.VMEM((8, LIVE), I32),
            pltpu.VMEM((2, LIVE, 128), I32),
            pltpu.VMEM((1, 64), I32),
            dma((23,)), dma((2,)),
            dma((2, 4, 2)), dma((2, 4, 2)), dma((NZ, 2)), dma((NZ, 2)), dma((4,)), dma((4,)),
            dma((7,)), dma((7,)), dma((2,)), dma((2,)),
        ],
        compiler_params=pltpu.CompilerParams(
            collective_id=0, has_side_effects=True, vmem_limit_bytes=62 * 1024 * 1024
        ),
        cost_estimate=pl.CostEstimate(flops=15_000_000_000, bytes_accessed=20_000_000, transcendentals=2_000_000),
        name="gather_grad",
    )(*args)


def run_sketch(ghl, codes, spots):
    anywhere = pl.BlockSpec(memory_space=pl.ANY)
    dma = pltpu.SemaphoreType.DMA
    return pl.pallas_call(
        sketch_kernel,
        out_shape=jax.ShapeDtypeStruct((TAB, 128), F32),
        in_specs=[anywhere] * 3,
        out_specs=anywhere,
        scratch_shapes=[
            pltpu.VMEM((2, NB, 256), BF16),
            pltpu.VMEM((2, META, 128), I32),
            pltpu.VMEM((2, LIVE, 128), I32),
            pltpu.VMEM((2, TAB, 128), BF16),
            pltpu.VMEM((4, TAB // 2, 128), BF16),
            pltpu.VMEM((TAB // 2, 128), BF16),
            pltpu.VMEM((3, TAB // 8, 128), BF16),
            pltpu.VMEM((TAB, 128), F32),
            dma((5,)), dma((2, 3, 2)), dma((4, 3)), dma((3, 3)), dma((3, 3)), dma((3, 4)), dma((3, 4)),
        ],
        compiler_params=pltpu.CompilerParams(
            collective_id=1, has_side_effects=True, vmem_limit_bytes=62 * 1024 * 1024
        ),
        cost_estimate=pl.CostEstimate(flops=24_000_000_000, bytes_accessed=10_000_000, transcendentals=0),
        name="sketch_reduce",
    )(ghl, codes, spots)


def finish_kernel(
    table, med, info, across, mom, err, w_in, w_out,
    win_new, wout_new, mom_new, err_new,
    tabv, medv, infov, acrossv, momv, errv, winv, woutv, winn, woutn, momn, errn, sem, out_sem,
):
    pairs = [(info, infov), (med, medv), (table, tabv), (across, acrossv), (w_in, winv), (w_out, woutv)]
    for j in range(ROWS):
        pairs += [(mom.at[:, j, :], momv.at[j]), (err.at[:, j, :], errv.at[j])]
    loads = [pltpu.make_async_copy(src, dst, sem.at[n]) for n, (src, dst) in enumerate(pairs)]
    for load in loads:
        load.start()
    stores = []

    def store(src, dst):
        stores.append(pltpu.make_async_copy(src, dst, out_sem.at[len(stores)]))
        stores[-1].start()

    for load in loads[:4]:
        load.wait()
    codes = infov[...]
    update = medv[...] + LEARN * tabv[:LIVE, :]
    kept = split2(jnp.where(codes[:, ROWS : ROWS + 1] == 1, update, 0.0))
    places = acrossv[0:1, :]

    def delta(start, rows):
        hit = jnp.where(iota((rows, LIVE), 0) + start == places, 1.0, 0.0).astype(BF16)
        got = nn(hit, kept)
        return got[:, :128] + got[:, 128:]

    loads[4].wait()
    for c in range(4):
        rows = pl.ds(c * 512, 512)
        for h in range(2):
            at = slice(h * 128, (h + 1) * 128)
            winn[rows, at] = winv[rows, at].astype(F32) - delta(h * 2048 + c * 512, 512)
        store(winn.at[rows], win_new.at[rows])
    loads[5].wait()
    for c in range(4):
        for q in range(4 * c, 4 * c + 4):
            at = slice(q * 128, (q + 1) * 128)
            woutn[:, at] = woutv[:, at].astype(F32) - delta(4096 + q * 256, 256)
        at = pl.ds(c * 512, 512)
        store(woutn.at[:, at], wout_new.at[:, at])
    for j in range(ROWS):
        loads[6 + 2 * j].wait()
        loads[7 + 2 * j].wait()
        fresh = DECAY * momv[j] + tabv[LIVE + j * COUNT : LIVE + (j + 1) * COUNT, :]
        momn[j] = fresh
        store(momn.at[j], mom_new.at[:, j, :])
        gone = tn(signed_hit(codes[:, j : j + 1]), kept)
        errn[j] = errv[j] + LEARN * fresh - (gone[:, :128] + gone[:, 128:])
        store(errn.at[j], err_new.at[:, j, :])
    for copy in stores:
        copy.wait()


def run_finish(table, med, info, across, mom, err, w_in, w_out):
    anywhere = pl.BlockSpec(memory_space=pl.ANY)
    vmem = pltpu.VMEM
    deep = vmem((ROWS, COUNT, 128), F32)
    return pl.pallas_call(
        finish_kernel,
        out_shape=(
            jax.ShapeDtypeStruct(w_in.shape, F32),
            jax.ShapeDtypeStruct(w_out.shape, F32),
            jax.ShapeDtypeStruct(mom.shape, F32),
            jax.ShapeDtypeStruct(err.shape, F32),
        ),
        in_specs=[anywhere] * 8,
        out_specs=(anywhere,) * 4,
        scratch_shapes=[
            vmem((TAB, 128), F32), vmem((LIVE, 128), F32), vmem((LIVE, 128), I32), vmem((8, LIVE), I32),
            deep, deep, vmem(w_in.shape, BF16), vmem(w_out.shape, BF16), vmem(w_in.shape, F32), vmem(w_out.shape, F32),
            deep, deep, pltpu.SemaphoreType.DMA((16,)), pltpu.SemaphoreType.DMA((18,)),
        ],
        compiler_params=pltpu.CompilerParams(vmem_limit_bytes=62 * 1024 * 1024),
        cost_estimate=pl.CostEstimate(flops=3_000_000_000, bytes_accessed=16_000_000, transcendentals=0),
        name="finish",
    )(table, med, info, across, mom, err, w_in, w_out)


def per_device(
    tokens, cotangent, w_in, w_out, momentum, error, block_order, signs, heavy_blocks, heavy_count
):
    mom, err = by_bucket(momentum), by_bucket(error)
    ghl, codes, spots, med, info, across = run_main(
        tokens, cotangent, w_in, w_out, block_order, signs, heavy_blocks, heavy_count, mom, err
    )
    table = run_sketch(ghl, codes, spots)
    win_new, wout_new, mom_new, err_new = run_finish(table, med, info, across, mom, err, w_in, w_out)
    return win_new, wout_new, by_row(mom_new), by_row(err_new)


def by_bucket(table):
    return jnp.transpose(table.reshape(ROWS, COUNT, 128), (1, 0, 2))


def by_row(table):
    return jnp.transpose(table, (1, 0, 2)).reshape(ROWS, COUNT * 128)


def solution(mesh):
    placed = (
        P(("rep", "shard"), None),
        P(("rep", "shard"), None),
        P(None, "shard"),
        P("shard", None),
        P(None, "shard"),
        P(None, "shard"),
        P(None, "shard"),
        P(None, "shard"),
        P("rep", "shard"),
        P("rep", "shard"),
    )
    return jax.shard_map(
        per_device,
        mesh=mesh,
        in_specs=placed,
        out_specs=(P(None, "shard"), P("shard", None), P(None, "shard"), P(None, "shard")),
        check_vma=False,
    )
```

```python
import functools

import jax
import jax.numpy as jnp
from jax import lax
from jax.experimental import pallas as pl
from jax.experimental.pallas import tpu as pltpu
from jax.sharding import PartitionSpec as P

MESH = pl.DeviceIdType.MESH
F32, BF16, I32 = jnp.float32, jnp.bfloat16, jnp.int32
LEARN = 0.05
DECAY = 0.9
ROOT = 0.7978845608028654

NX, NY, NZ = 4, 4, 8
TOK = 104
CHIP = 2 * TOK
SUBS = ((0, 112), (112, 96))
DW, COLS = 2048, 256
NB = 8192
COUNT = 512
ROWS = 5
LIVE = 256
LISTED = ROWS * COUNT
TAB = LISTED + LIVE
PIECES = ((0, 1024), (1024, 1024), (2048, 768))
CODE = ROWS * 64
META = CODE + 64


def nt(a, b):
    return lax.dot_general(a, b, (((1,), (1,)), ((), ())), preferred_element_type=F32)


def tn(a, b):
    return lax.dot_general(a, b, (((0,), (0,)), ((), ())), preferred_element_type=F32)


def nn(a, b):
    return jnp.dot(a, b, preferred_element_type=F32)


def iota(shape, dim):
    return lax.broadcasted_iota(I32, shape, dim)


def split2(x):
    hi = x.astype(BF16)
    return jnp.concatenate([hi, (x - hi.astype(F32)).astype(BF16)], axis=1)


def place_of(block):
    rest = block - 4096
    return jnp.where(
        block < 4096, (block & 1) * 2048 + (block >> 1), 4096 + (rest & 15) * 256 + (rest >> 4)
    )


def gelu_pair(pre):
    tangent = jnp.tanh(ROOT * (pre + 0.044715 * pre * pre * pre))
    value = 0.5 * pre * (1.0 + tangent)
    slope = 0.5 * (1.0 + tangent) + 0.5 * pre * (1.0 - tangent * tangent) * ROOT * (
        1.0 + 0.134145 * pre * pre
    )
    return value, slope


def invert(ord_ref, sgn_ref, meta_ref):
    step = 1024
    for j in range(ROWS):

        def body(c, acc, j=j):
            at = pl.ds(pl.multiple_of(c * step, step), step)
            place = place_of(ord_ref[j : j + 1, at])
            sign = sgn_ref[j : j + 1, at]
            bucket = (c * step + iota((1, step), 1)) >> 4
            row = iota((128, step), 0)
            value = jnp.where(row < 64, bucket >> 1, (bucket & 1) * 2 + sign)
            left = jnp.where((row & 63) == (place >> 7), value, 0).astype(F32).astype(BF16)
            right = jnp.where(row == (place & 127), 1.0, 0.0).astype(BF16)
            return acc + nt(left, right)

        acc = lax.fori_loop(0, NB // step, body, jnp.zeros((128, 128), F32))
        meta_ref[j * 64 : (j + 1) * 64, :] = (acc[:64] * 4.0 + acc[64:]).astype(I32)


def compact(lists, along):
    full = jnp.concatenate([lists, jnp.zeros((120, 128), I32)], axis=0)
    shape = (LIVE, 128)
    slot, lane = iota(shape, 0), iota(shape, 1)
    wanted = jnp.where(slot < 128, slot & 15, jnp.where(slot < 176, slot - 112, 127))
    pick = jnp.where(lane == wanted, 1.0, 0.0).astype(BF16)
    pick_count = jnp.where(lane == 64, 1.0, 0.0).astype(BF16)
    high = (full >> 7).astype(F32).astype(BF16)
    low = (full & 127).astype(F32).astype(BF16)
    if along == 0:
        values = nt(pick, high) * 128.0 + nt(pick, low)
        counts = nt(pick_count, low)
        spot, rep, axis = slot, lane, 1
    else:
        values = nt(high, pick) * 128.0 + nt(low, pick)
        counts = nt(low, pick_count)
        spot, rep, axis = iota((128, LIVE), 1), iota((128, LIVE), 0), 0
    first = (spot < 128) & (rep == (spot >> 4)) & (counts > (spot & 15).astype(F32))
    later = (spot >= 128) & (spot < 176) & (rep < 8) & (counts > 63.5)
    hit = jnp.where(first | later, 1.0, 0.0)
    live = jnp.sum(hit, axis=axis, keepdims=True)
    block = jnp.sum(hit * values, axis=axis, keepdims=True).astype(I32)
    return jnp.where(live > 0.5, place_of(block), -1)


def lists_of(meta_ref, *lead):
    total = jnp.zeros((8, 128), I32)
    for r in range(8):
        total = total + meta_ref[(*lead, slice(CODE + 8 * r, CODE + 8 * r + 8), slice(None))]
    return total


def middle_value(values):
    values = list(values)
    total = len(values)
    for rounds in range(total):
        for i in range(rounds % 2, total - 1, 2):
            lower = jnp.minimum(values[i], values[i + 1])
            upper = jnp.maximum(values[i], values[i + 1])
            values[i] = lower
            values[i + 1] = upper
    return values[total // 2]


def prepare(meta, momv, errv, medv, infov, acrossv):
    lists = lists_of(meta)
    down, across = compact(lists, 0), compact(lists, 1)
    shape = (LIVE, LIVE)
    same = (down == across) & (across >= 0) & (iota(shape, 1) < iota(shape, 0))
    earlier = jnp.max(jnp.where(same, 1.0, 0.0), axis=1, keepdims=True)
    keep = jnp.where((down >= 0) & (earlier < 0.5), 1, 0)
    codes = meta[...]
    high = (codes >> 2).astype(F32).astype(BF16)
    low = (codes & 3).astype(F32).astype(BF16)
    lane = iota((LIVE, 128), 1)
    lane_hit = lane == (down & 127)
    info = jnp.where(lane == ROWS, keep, 0)
    found = []
    for j in range(ROWS):
        pick = jnp.where(iota((LIVE, META), 1) == (down >> 7) + j * 64, 1.0, 0.0)
        pick = jnp.where(down >= 0, pick, 0.0).astype(BF16)
        value = nn(pick, high) * 4.0 + nn(pick, low)
        code = jnp.sum(jnp.where(lane_hit, value, 0.0), axis=1, keepdims=True).astype(I32)
        info = jnp.where(lane == j, code, info)
        probe = errv[j] + LEARN * DECAY * momv[j]
        got = nn(signed_hit(code), split2(probe))
        found.append(got[:, :128] + got[:, 128:])
    medv[...] = middle_value(found)
    infov[...] = info
    acrossv[...] = jnp.broadcast_to(across, acrossv.shape)


def signed_hit(code):
    sign = jnp.where((code & 1) == 1, 1.0, -1.0)
    return jnp.where(iota((LIVE, COUNT), 1) == (code >> 1), sign, 0.0).astype(BF16)


def main_kernel(
    tok_ref, cot_ref, win_ref, wout_ref, ord_ref, sgn_ref, lst_ref, cnt_ref, mom_ref, err_ref,
    ghl_ref, codes_ref, spots_ref, med_ref, info_ref, across_ref,
    own, land, buf, wi, wo, gin, gout, ordv, sgnv, meta, meta2, ghl,
    momv, errv, medv, infov, acrossv, spots, lstv,
    lsem, land_sem, ring_s, ring_r, sib_s, sib_r, w_s, w_r, list_s, list_r, meta_s, meta_r,
):
    rep, shard = lax.axis_index("rep"), lax.axis_index("shard")
    y, core = rep // 2, rep % 2
    x, z = shard // NZ, shard % NZ
    other = 1 - core

    def dev(dx=0, dy=0, dz=0, to=None):
        c = core if to is None else to
        return {
            "rep": lax.rem(y + dy + NY, NY) * 2 + c,
            "shard": lax.rem(x + dx + NX, NX) * NZ + lax.rem(z + dz + NZ, NZ),
        }

    def remote(src, dst, send, recv, device):
        return pltpu.make_async_remote_copy(
            src_ref=src, dst_ref=dst, send_sem=send, recv_sem=recv, device_id=device, device_id_type=MESH
        )

    def on_core(c, *actions):
        @pl.when(core == c)
        def _():
            for action in actions:
                action()

    own_tok = pltpu.make_async_copy(tok_ref, own, lsem.at[0])
    own_cot = pltpu.make_async_copy(cot_ref, own, lsem.at[0])
    loads = [
        pltpu.make_async_copy(lst_ref, lstv, lsem.at[1]),
        pltpu.make_async_copy(ord_ref, ordv, lsem.at[2]),
        pltpu.make_async_copy(sgn_ref, sgnv, lsem.at[3]),
    ]
    tables = [pltpu.make_async_copy(mom_ref.at[:, j, :], momv.at[j], lsem.at[6 + j]) for j in range(ROWS)]
    tables += [pltpu.make_async_copy(err_ref.at[:, j, :], errv.at[j], lsem.at[11 + j]) for j in range(ROWS)]
    own_wi = pltpu.make_async_copy(win_ref, wi.at[:, pl.ds(0, COLS)], lsem.at[4])
    own_wo = pltpu.make_async_copy(wout_ref, wo.at[pl.ds(0, COLS)], lsem.at[5])
    on_core(0, own_tok.start)
    on_core(1, own_cot.start)
    for load in loads:
        load.start()

    barrier = pltpu.get_barrier_semaphore()
    partners = [dev(dz=1), dev(dz=-1)]
    partners += [dev(dx=d, to=c) for d in (1, -1, 2) for c in (0, 1)]
    partners += [dev(dy=d, to=c) for d in (1, 2, 3) for c in (0, 1)] + [dev(to=other)]
    for partner in partners:
        pl.semaphore_signal(barrier, inc=1, device_id=partner, device_id_type=MESH)
    pl.semaphore_wait(barrier, len(partners))

    give_cot = remote(cot_ref, land, land_sem.at[0], land_sem.at[1], dev(to=other))
    give_tok = remote(tok_ref, land, land_sem.at[0], land_sem.at[1], dev(to=other))
    on_core(0, give_cot.start)
    on_core(1, give_tok.start)

    toward = jnp.where(core == 0, -1, 1)
    lower, upper = pl.ds(0, COLS), pl.ds(COLS, COLS)
    landing = pl.ds(pl.multiple_of(other * COLS, COLS), COLS)
    w_in_first = remote(win_ref, wi.at[:, landing], w_s.at[0], w_r.at[0], dev(dx=toward))
    w_out_first = remote(wout_ref, wo.at[landing], w_s.at[1], w_r.at[1], dev(dx=toward))
    w_in_next = remote(wi.at[:, upper], wi.at[:, upper], w_s.at[2], w_r.at[2], dev(dx=-1, to=1))
    w_out_next = remote(wo.at[lower], wo.at[upper], w_s.at[3], w_r.at[3], dev(dx=1, to=1))
    on_core(0, w_in_first.start, w_out_first.start, own_wi.start, own_wo.start)
    on_core(1, w_out_first.start, w_in_first.start)

    loads[0].wait()
    listed = jnp.concatenate([lstv[...], jnp.full(lstv.shape, cnt_ref[0, 0], I32)], axis=1)
    meta[pl.ds(pl.multiple_of(CODE + 8 * rep, 8), 8), :] = jnp.where(iota((8, 128), 0) == rep, listed, 0)
    list_row = meta.at[pl.ds(pl.multiple_of(CODE + 8 * rep, 8), 8)]
    peers = [(0, 1), (1, 0), (1, 1), (2, 0), (2, 1), (3, 0), (3, 1)]
    peers = [(n, dev(dy=d, to=other if flip else core)) for n, (d, flip) in enumerate(peers)]
    list_copies = [remote(list_row, list_row, list_s.at[n], list_r.at[n], peer) for n, peer in peers]
    for copy in list_copies:
        copy.start()

    on_core(0, own_tok.wait, give_cot.wait)
    on_core(1, own_cot.wait, give_tok.wait)
    for c in range(4):
        at = slice(c * 512, (c + 1) * 512)
        mine, theirs = own[:, at].astype(F32), land[:, at].astype(F32)
        first, second = jnp.where(core == 0, mine, theirs), jnp.where(core == 0, theirs, mine)
        buf[core, 0:CHIP, at] = jnp.concatenate([first, second], axis=0).astype(BF16)

    def turn_of(way, sub):
        return sub if way == 0 else 1 - sub

    def unit_of(hops, turn):
        return 0 if hops == 0 else 2 * hops - 1 + turn

    def rows_of(unit, sub):
        return pl.ds(unit * CHIP + SUBS[sub][0], SUBS[sub][1])

    def ring(way, hops, sub):
        turn = turn_of(way, sub)
        return remote(
            buf.at[core, rows_of(unit_of(hops, turn), sub)],
            buf.at[core, rows_of(unit_of(hops + 1, turn), sub)],
            ring_s.at[way, hops, sub], ring_r.at[way, hops, sub],
            dev(dz=1 if way == 0 else -1),
        )

    def sibling(unit, sub):
        at = buf.at[core, rows_of(unit, sub)]
        return remote(at, at, sib_s.at[unit, sub], sib_r.at[unit, sub], dev(to=other))

    for turn in (0, 1):
        ring(0, 0, turn).start()
        ring(1, 0, 1 - turn).start()
    for sub in (0, 1):
        sibling(0, sub).start()
    for load in tables:
        load.start()

    def arrive(hops, turn):
        for way in (0, 1):
            sub = turn if way == 0 else 1 - turn
            ring(way, hops - 1, sub).wait_recv()
            if hops < 3 or (hops == 3 and turn == 0):
                ring(way, hops, sub).start()
            sibling(unit_of(hops, turn), sub).start()

    loads[1].wait()
    loads[2].wait()
    invert(ordv, sgnv, meta)
    for copy in list_copies:
        copy.wait_recv()
    meta_first = remote(meta, meta2.at[other], meta_s.at[0], meta_r.at[0], dev(dx=toward))
    meta_next = remote(meta, meta2.at[1], meta_s.at[1], meta_r.at[1], dev(dx=2))
    meta_first.start()
    on_core(1, meta_next.start)

    @pl.when(core == 0)
    def _():
        meta2[0] = meta[...]

    gin[...] = jnp.zeros_like(gin)
    gout[...] = jnp.zeros_like(gout)

    arrive(1, 0)
    on_core(0, w_in_first.wait_recv, w_in_next.start)
    on_core(1, w_out_first.wait_recv, w_out_next.start)
    arrive(1, 1)
    for load in tables:
        load.wait()
    prepare(meta, momv, errv, medv, infov, acrossv)
    ready = [
        pltpu.make_async_copy(medv, med_ref, lsem.at[16]),
        pltpu.make_async_copy(infov, info_ref, lsem.at[17]),
        pltpu.make_async_copy(acrossv, across_ref, lsem.at[18]),
    ]
    for copy in ready:
        copy.start()
    meta_first.wait_recv()
    on_core(1, meta_next.wait_recv)
    for k in (0, 1):
        spots[k] = jnp.broadcast_to(compact(lists_of(meta2, k), 0), (LIVE, 128))
    ready += [
        pltpu.make_async_copy(meta2, codes_ref, lsem.at[21]),
        pltpu.make_async_copy(spots, spots_ref, lsem.at[22]),
    ]
    for copy in ready[3:]:
        copy.start()
    arrive(2, 0)
    on_core(0, w_out_first.wait_recv, own_wi.wait, own_wo.wait)
    on_core(1, w_in_first.wait_recv, w_in_next.wait_recv, w_out_next.wait_recv)

    def wait_sibling(*units):
        for unit in units:
            for sub in (0, 1):
                sibling(unit, sub).wait_recv()

    out_first = pltpu.make_async_copy(ghl.at[:, pl.ds(0, 4096)], ghl_ref.at[:, pl.ds(0, 4096)], lsem.at[19])
    out_last = pltpu.make_async_copy(ghl.at[:, pl.ds(4096, 4096)], ghl_ref.at[:, pl.ds(4096, 4096)], lsem.at[20])
    ready += [out_first, out_last]

    def work(start, count, last=False):
        rows = pl.ds(start, count)
        value, slope = gelu_pair(nn(buf[0, rows, :], wi[...]))
        back = nt(buf[1, rows, :], wo[...])
        hidden = value.astype(BF16)
        grad = (back * slope).astype(BF16)
        for c in range(4):
            at = slice(c * 512, (c + 1) * 512)
            total = gin[at, :] + tn(buf[0, rows, at], grad)
            if not last:
                gin[at, :] = total
                continue
            for k in range(2):
                for h in range(2):
                    part = total[:, k * COLS + h * 128 : k * COLS + (h + 1) * 128]
                    ghl[k, h * 2048 + c * 512 : h * 2048 + (c + 1) * 512, :] = split2(part)
        if last:
            out_first.start()
        for c in range(4):
            at = slice(c * 512, (c + 1) * 512)
            total = gout[:, at] + tn(hidden, buf[1, rows, at])
            if not last:
                gout[:, at] = total
                continue
            for k in range(2):
                for q in range(4 * c, 4 * c + 4):
                    part = total[k * COLS : (k + 1) * COLS, (q - 4 * c) * 128 : (q - 4 * c + 1) * 128]
                    ghl[k, 4096 + q * 256 : 4352 + q * 256, :] = split2(part)

    def work_pair(i, carry):
        @pl.when(i == 0)
        def _():
            wait_sibling(0, 1)

        @pl.when(i == 1)
        def _():
            wait_sibling(2, 3)

        @pl.when(i == 2)
        def _():
            arrive(2, 1)
            arrive(3, 0)
            wait_sibling(4, 5)

        work(pl.multiple_of(i * (2 * CHIP), 16), 2 * CHIP)
        return carry

    lax.fori_loop(0, 3, work_pair, 0)
    arrive(3, 1)
    wait_sibling(6)
    work(6 * CHIP, CHIP)
    ring(0, 3, 0).wait_recv()
    sibling(7, 0).start()
    ring(1, 3, 1).wait_recv()
    sibling(7, 1).start()
    wait_sibling(7)
    work(7 * CHIP, CHIP, last=True)
    out_last.start()

    for copy in list_copies + [w_in_first, w_out_first, meta_first]:
        copy.wait_send()
    for way in (0, 1):
        for hops in range(4):
            for sub in (0, 1):
                if hops < 3 or sub == way:
                    ring(way, hops, sub).wait_send()
    for unit in range(NZ):
        for sub in (0, 1):
            sibling(unit, sub).wait_send()
    on_core(0, w_in_next.wait_send)
    on_core(1, w_out_next.wait_send, meta_next.wait_send)
    for copy in ready:
        copy.wait()


def sketch_kernel(
    ghl_ref, codes_ref, spots_ref, table_ref,
    ghl, codes, spots, outb, recvx, yb, recvy, tot, lsem, x_s, x_r, y_s, y_r, a_s, a_r,
):
    rep, shard = lax.axis_index("rep"), lax.axis_index("shard")
    y, core = rep // 2, rep % 2
    x, z = shard // NZ, shard % NZ
    other = 1 - core

    def dev(dx=0, dy=0, dz=0, to=None):
        c = core if to is None else to
        return {
            "rep": lax.rem(y + dy + NY, NY) * 2 + c,
            "shard": lax.rem(x + dx + NX, NX) * NZ + lax.rem(z + dz + NZ, NZ),
        }

    def remote(src, dst, send, recv, device):
        return pltpu.make_async_remote_copy(
            src_ref=src, dst_ref=dst, send_sem=send, recv_sem=recv, device_id=device, device_id_type=MESH
        )

    def on_core(c, *actions):
        @pl.when(core == c)
        def _():
            for action in actions:
                action()

    loads = [
        pltpu.make_async_copy(codes_ref, codes, lsem.at[0]),
        pltpu.make_async_copy(spots_ref, spots, lsem.at[1]),
        pltpu.make_async_copy(ghl_ref.at[1], ghl.at[1], lsem.at[2]),
        pltpu.make_async_copy(ghl_ref.at[0], ghl.at[0], lsem.at[3]),
    ]
    for load in loads:
        load.start()
    barrier = pltpu.get_barrier_semaphore()
    partners = [dev(dx=d, to=c) for d in (1, -1, 2) for c in (0, 1)]
    partners += [dev(dy=d) for d in (1, 2, 3)] + [dev(to=other)]
    for partner in partners:
        pl.semaphore_signal(barrier, inc=1, device_id=partner, device_id_type=MESH)
    pl.semaphore_wait(barrier, len(partners))
    loads[0].wait()
    loads[1].wait()

    def spread(code):
        code = jnp.broadcast_to(code, (16, 128))
        bucket = (code >> 1).astype(F32)
        return jnp.where((code & 1) == 1, 1.0, -1.0).astype(BF16), [(bucket - 256.0 * h).astype(BF16) for h in (0, 1)]

    def one_hot(spread_code, quarter):
        sign, spot = spread_code[0], spread_code[1][quarter // 2]
        ramp = iota((256, 128), 0).astype(F32).astype(BF16)
        first = 8 * (quarter % 2)
        hits = [spot == ramp[g * 16 : (g + 1) * 16] for g in range(first, first + 8)]
        return jnp.concatenate([jnp.where(hit, sign, jnp.zeros_like(sign)) for hit in hits], axis=0)

    def sketch(k, work):
        step = 4
        per = NB // 512
        used = sorted({j for j, _ in work if j is not None})

        def run(*sums):
            def chunk(t, carry):
                first = [unit * per + t * step for unit in (0, 1)]

                def tile(unit, i):
                    return ghl[k, pl.ds(pl.multiple_of((first[unit] + i) * 256, 256), 256), :]

                found = [
                    {j: codes[k, pl.ds(pl.multiple_of(j * 64 + 2 * first[unit], 8), 2 * step), :] for j in used}
                    for unit in (0, 1)
                ]
                for unit in (0, 1):
                    pltpu.matmul_push_rhs(tile(unit, 0), 0, unit)
                for i in range(step):
                    if i + 1 < step:
                        for unit in (0, 1):
                            pltpu.matmul_push_rhs(tile(unit, i + 1), (i + 1) % 2, unit)
                    rows = [
                        {j: [spread(found[unit][j][2 * i + n : 2 * i + n + 1, :]) for n in (0, 1)] for j in used}
                        for unit in (0, 1)
                    ]
                    for c, (j, q) in enumerate(work):
                        for unit in (0, 1):
                            if j is None:
                                spot = spots[k, q * 128 : (q + 1) * 128, :] - (first[unit] + i) * 256
                                lane = iota((128, 128), 1)
                                hot = [jnp.where(spot == lane + 128 * n, 1.0, 0.0).astype(BF16) for n in (0, 1)]
                            else:
                                hot = [one_hot(rows[unit][j][n], q) for n in (0, 1)]
                            pltpu.matmul_acc_lhs(
                                sums[2 * c + unit],
                                jnp.concatenate(hot, axis=1),
                                load_staged_rhs=i % 2 if c == 0 else None,
                            )
                return carry

            lax.fori_loop(0, per // step, chunk, 0)
            for c, (j, q) in enumerate(work):
                total = pltpu.matmul_pop(sums[2 * c]) + pltpu.matmul_pop(sums[2 * c + 1])
                start = q * 128 + (LISTED if j is None else j * COUNT)
                outb[k, start : start + 128, :] = (total[:, :128] + total[:, 128:]).astype(BF16)

        pl.run_scoped(run, *[pltpu.ACC(mxu_id=unit)((128, 256), F32) for _ in work for unit in (0, 1)])

    def whole(*rows):
        return [(j, q) for j in rows for q in range(4)]

    def half_of(p):
        return PIECES[p][0] // 2, PIECES[p][1] // 2

    def quarter_of(p):
        return PIECES[p][0] // 8, PIECES[p][1] // 8

    def x_copy(k, p, h, slot, device):
        start, rows = half_of(p)
        return remote(
            outb.at[k, pl.ds(PIECES[p][0] + h * rows, rows)], recvx.at[slot, pl.ds(start, rows)],
            x_s.at[k, p, h], x_r.at[slot, p], device,
        )

    x_far = [[x_copy(1, p, h, 1 + 2 * core, dev(dx=1 + core, to=h)) for h in (0, 1)] for p in range(3)]
    x_near = [[x_copy(0, p, h, 2, dev(dx=-1, to=h)) for h in (0, 1)] for p in range(3)]
    x_home = [x_copy(0, p, 1, 0, dev(to=1)) for p in range(3)]

    def x_far_start(p):
        for copy in x_far[p]:
            copy.start()

    def x_near_start(p):
        start, rows = half_of(p)
        on_core(1, *[copy.start for copy in x_near[p]])

        @pl.when(core == 0)
        def _():
            x_home[p].start()
            recvx[0, start : start + rows, :] = outb[0, PIECES[p][0] : PIECES[p][0] + rows, :]

    def my_quarter(p):
        rows = PIECES[p][1] // 8
        return pl.ds(pl.multiple_of(PIECES[p][0] + core * (4 * rows) + y * rows, 16), rows)

    def y_copy(p, d):
        start, rows = quarter_of(p)
        there = pl.ds(pl.multiple_of(4 * start + lax.rem(y + d, NY) * rows, 16), rows)
        return remote(yb.at[there], recvy.at[d - 1, pl.ds(start, rows)], y_s.at[p, d - 1], y_r.at[p, d - 1], dev(dy=d))

    def y_start(p):
        start, rows = half_of(p)
        on_core(1, x_copy(0, p, 1, 0, dev(to=1)).wait_recv)
        for slot in (1, 2, 3):
            x_copy(1, p, 0, slot, dev(dx=1)).wait_recv()
        part = recvx[0, start : start + rows, :].astype(F32)
        for slot in (1, 2, 3):
            part = part + recvx[slot, start : start + rows, :].astype(F32)
        yb[start : start + rows, :] = part.astype(BF16)
        tot[pl.ds(pl.multiple_of(PIECES[p][0] + core * rows, 16), rows), :] = part
        for d in (1, 2, 3):
            y_copy(p, d).start()

    def a_copy(p, d):
        at = tot.at[my_quarter(p)]
        return remote(at, at, a_s.at[p, d - 1], a_r.at[p, d - 1], dev(dy=d))

    def a_start(p):
        start, rows = quarter_of(p)
        total = tot[my_quarter(p), :]
        for d in (1, 2, 3):
            y_copy(p, d).wait_recv()
            total = total + recvy[d - 1, start : start + rows, :].astype(F32)
        tot[my_quarter(p), :] = total
        for d in (1, 2, 3):
            a_copy(p, d).start()

    def e_copy(p):
        rows = PIECES[p][1] // 2
        at = tot.at[pl.ds(pl.multiple_of(PIECES[p][0] + core * rows, 16), rows)]
        return remote(at, at, a_s.at[p, 3], a_r.at[p, 3], dev(to=other))

    def e_start(p):
        for d in (1, 2, 3):
            a_copy(p, d).wait_recv()
        e_copy(p).start()

    passes = (whole(0, 1), whole(2, 3), whole(4) + [(None, 0), (None, 1)])
    loads[2].wait()
    for p in range(3):
        sketch(1, passes[p])
        x_far_start(p)
    loads[3].wait()
    sketch(0, passes[0])
    x_near_start(0)
    sketch(0, passes[1])
    x_near_start(1)
    y_start(0)
    sketch(0, passes[2])
    x_near_start(2)
    a_start(0)
    y_start(1)
    y_start(2)
    a_start(1)
    a_start(2)
    for p in range(3):
        e_start(p)
    for p in range(3):
        e_copy(p).wait_recv()
    result = pltpu.make_async_copy(tot, table_ref, lsem.at[4])
    result.start()

    for p in range(3):
        for copy in x_far[p] + [y_copy(p, d) for d in (1, 2, 3)] + [a_copy(p, d) for d in (1, 2, 3)] + [e_copy(p)]:
            copy.wait_send()
    on_core(0, *[copy.wait_send for copy in x_home])
    on_core(1, *[c.wait_send for p in range(3) for c in x_near[p]])
    result.wait()


def run_main(*args):
    anywhere = pl.BlockSpec(memory_space=pl.ANY)
    dma = pltpu.SemaphoreType.DMA
    return pl.pallas_call(
        main_kernel,
        out_shape=(
            jax.ShapeDtypeStruct((2, NB, 256), BF16),
            jax.ShapeDtypeStruct((2, META, 128), I32),
            jax.ShapeDtypeStruct((2, LIVE, 128), I32),
            jax.ShapeDtypeStruct((LIVE, 128), F32),
            jax.ShapeDtypeStruct((LIVE, 128), I32),
            jax.ShapeDtypeStruct((8, LIVE), I32),
        ),
        in_specs=[anywhere] * 7 + [pl.BlockSpec(memory_space=pltpu.SMEM)] + [anywhere] * 2,
        out_specs=(anywhere,) * 6,
        scratch_shapes=[
            pltpu.VMEM((TOK, DW), BF16),
            pltpu.VMEM((TOK, DW), BF16),
            pltpu.VMEM((2, NZ * CHIP, DW), BF16),
            pltpu.VMEM((DW, 2 * COLS), BF16),
            pltpu.VMEM((2 * COLS, DW), BF16),
            pltpu.VMEM((DW, 2 * COLS), F32),
            pltpu.VMEM((2 * COLS, DW), F32),
            pltpu.VMEM((ROWS, NB), I32),
            pltpu.VMEM((ROWS, NB), I32),
            pltpu.VMEM((META, 128), I32),
            pltpu.VMEM((2, META, 128), I32),
            pltpu.VMEM((2, NB, 256), BF16),
            pltpu.VMEM((ROWS, COUNT, 128), F32),
            pltpu.VMEM((ROWS, COUNT, 128), F32),
            pltpu.VMEM((LIVE, 128), F32),
            pltpu.VMEM((LIVE, 128), I32),
            pltpu.VMEM((8, LIVE), I32),
            pltpu.VMEM((2, LIVE, 128), I32),
            pltpu.VMEM((1, 64), I32),
            dma((23,)), dma((2,)),
            dma((2, 4, 2)), dma((2, 4, 2)), dma((NZ, 2)), dma((NZ, 2)), dma((4,)), dma((4,)),
            dma((7,)), dma((7,)), dma((2,)), dma((2,)),
        ],
        compiler_params=pltpu.CompilerParams(
            collective_id=0, has_side_effects=True, vmem_limit_bytes=62 * 1024 * 1024
        ),
        cost_estimate=pl.CostEstimate(flops=15_000_000_000, bytes_accessed=20_000_000, transcendentals=2_000_000),
        name="gather_grad",
    )(*args)


def run_sketch(ghl, codes, spots):
    anywhere = pl.BlockSpec(memory_space=pl.ANY)
    dma = pltpu.SemaphoreType.DMA
    return pl.pallas_call(
        sketch_kernel,
        out_shape=jax.ShapeDtypeStruct((TAB, 128), F32),
        in_specs=[anywhere] * 3,
        out_specs=anywhere,
        scratch_shapes=[
            pltpu.VMEM((2, NB, 256), BF16),
            pltpu.VMEM((2, META, 128), I32),
            pltpu.VMEM((2, LIVE, 128), I32),
            pltpu.VMEM((2, TAB, 128), BF16),
            pltpu.VMEM((4, TAB // 2, 128), BF16),
            pltpu.VMEM((TAB // 2, 128), BF16),
            pltpu.VMEM((3, TAB // 8, 128), BF16),
            pltpu.VMEM((TAB, 128), F32),
            dma((5,)), dma((2, 3, 2)), dma((4, 3)), dma((3, 3)), dma((3, 3)), dma((3, 4)), dma((3, 4)),
        ],
        compiler_params=pltpu.CompilerParams(
            collective_id=1, has_side_effects=True, vmem_limit_bytes=62 * 1024 * 1024
        ),
        cost_estimate=pl.CostEstimate(flops=24_000_000_000, bytes_accessed=10_000_000, transcendentals=0),
        name="sketch_reduce",
    )(ghl, codes, spots)


def finish_kernel(
    table, med, info, across, mom, err, w_in, w_out,
    win_new, wout_new, mom_new, err_new,
    tabv, medv, infov, acrossv, momv, errv, winv, woutv, winn, woutn, momn, errn, sem, out_sem,
):
    pairs = [(info, infov), (med, medv), (table, tabv), (across, acrossv), (w_in, winv), (w_out, woutv)]
    for j in range(ROWS):
        pairs += [(mom.at[:, j, :], momv.at[j]), (err.at[:, j, :], errv.at[j])]
    loads = [pltpu.make_async_copy(src, dst, sem.at[n]) for n, (src, dst) in enumerate(pairs)]
    for load in loads:
        load.start()
    stores = []

    def store(src, dst):
        stores.append(pltpu.make_async_copy(src, dst, out_sem.at[len(stores)]))
        stores[-1].start()

    for load in loads[:4]:
        load.wait()
    codes = infov[...]
    update = medv[...] + LEARN * tabv[LISTED:, :]
    kept = split2(jnp.where(codes[:, ROWS : ROWS + 1] == 1, update, 0.0))
    places = acrossv[0:1, :]

    def delta(start, rows):
        hit = jnp.where(iota((rows, LIVE), 0) + start == places, 1.0, 0.0).astype(BF16)
        got = nn(hit, kept)
        return got[:, :128] + got[:, 128:]

    loads[4].wait()
    for c in range(4):
        rows = pl.ds(c * 512, 512)
        for h in range(2):
            at = slice(h * 128, (h + 1) * 128)
            winn[rows, at] = winv[rows, at].astype(F32) - delta(h * 2048 + c * 512, 512)
        store(winn.at[rows], win_new.at[rows])
    loads[5].wait()
    for c in range(4):
        for q in range(4 * c, 4 * c + 4):
            at = slice(q * 128, (q + 1) * 128)
            woutn[:, at] = woutv[:, at].astype(F32) - delta(4096 + q * 256, 256)
        at = pl.ds(c * 512, 512)
        store(woutn.at[:, at], wout_new.at[:, at])
    for j in range(ROWS):
        loads[6 + 2 * j].wait()
        loads[7 + 2 * j].wait()
        fresh = DECAY * momv[j] + tabv[j * COUNT : (j + 1) * COUNT, :]
        momn[j] = fresh
        store(momn.at[j], mom_new.at[:, j, :])
        gone = tn(signed_hit(codes[:, j : j + 1]), kept)
        errn[j] = errv[j] + LEARN * fresh - (gone[:, :128] + gone[:, 128:])
        store(errn.at[j], err_new.at[:, j, :])
    for copy in stores:
        copy.wait()


def run_finish(table, med, info, across, mom, err, w_in, w_out):
    anywhere = pl.BlockSpec(memory_space=pl.ANY)
    vmem = pltpu.VMEM
    deep = vmem((ROWS, COUNT, 128), F32)
    return pl.pallas_call(
        finish_kernel,
        out_shape=(
            jax.ShapeDtypeStruct(w_in.shape, F32),
            jax.ShapeDtypeStruct(w_out.shape, F32),
            jax.ShapeDtypeStruct(mom.shape, F32),
            jax.ShapeDtypeStruct(err.shape, F32),
        ),
        in_specs=[anywhere] * 8,
        out_specs=(anywhere,) * 4,
        scratch_shapes=[
            vmem((TAB, 128), F32), vmem((LIVE, 128), F32), vmem((LIVE, 128), I32), vmem((8, LIVE), I32),
            deep, deep, vmem(w_in.shape, BF16), vmem(w_out.shape, BF16), vmem(w_in.shape, F32), vmem(w_out.shape, F32),
            deep, deep, pltpu.SemaphoreType.DMA((16,)), pltpu.SemaphoreType.DMA((18,)),
        ],
        compiler_params=pltpu.CompilerParams(vmem_limit_bytes=62 * 1024 * 1024),
        cost_estimate=pl.CostEstimate(flops=3_000_000_000, bytes_accessed=16_000_000, transcendentals=0),
        name="finish",
    )(table, med, info, across, mom, err, w_in, w_out)


def per_device(
    tokens, cotangent, w_in, w_out, momentum, error, block_order, signs, heavy_blocks, heavy_count
):
    mom, err = by_bucket(momentum), by_bucket(error)
    ghl, codes, spots, med, info, across = run_main(
        tokens, cotangent, w_in, w_out, block_order, signs, heavy_blocks, heavy_count, mom, err
    )
    table = run_sketch(ghl, codes, spots)
    win_new, wout_new, mom_new, err_new = run_finish(table, med, info, across, mom, err, w_in, w_out)
    return win_new, wout_new, by_row(mom_new), by_row(err_new)


def by_bucket(table):
    return jnp.transpose(table.reshape(ROWS, COUNT, 128), (1, 0, 2))


def by_row(table):
    return jnp.transpose(table, (1, 0, 2)).reshape(ROWS, COUNT * 128)


def solution(mesh):
    placed = (
        P(("rep", "shard"), None),
        P(("rep", "shard"), None),
        P(None, "shard"),
        P("shard", None),
        P(None, "shard"),
        P(None, "shard"),
        P(None, "shard"),
        P(None, "shard"),
        P("rep", "shard"),
        P("rep", "shard"),
    )
    return jax.shard_map(
        per_device,
        mesh=mesh,
        in_specs=placed,
        out_specs=(P(None, "shard"), P("shard", None), P(None, "shard"), P(None, "shard")),
        check_vma=False,
    )
```

```python
import functools

import jax
import jax.numpy as jnp
from jax import lax
from jax.experimental import pallas as pl
from jax.experimental.pallas import tpu as pltpu
from jax.sharding import PartitionSpec as P

MESH = pl.DeviceIdType.MESH
F32, BF16, I32 = jnp.float32, jnp.bfloat16, jnp.int32
LEARN = 0.05
DECAY = 0.9
ROOT = 0.7978845608028654

NX, NY, NZ = 4, 4, 8
TOK = 104
CHIP = 2 * TOK
SUBS = ((0, 112), (112, 96))
DW, COLS = 2048, 256
NB = 8192
COUNT = 512
ROWS = 5
LIVE = 256
LISTED = ROWS * COUNT
TAB = LISTED + LIVE
PIECES = ((0, 1024), (1024, 1024), (2048, 768))
CODE = ROWS * 64
META = CODE + 64


def nt(a, b):
    return lax.dot_general(a, b, (((1,), (1,)), ((), ())), preferred_element_type=F32)


def tn(a, b):
    return lax.dot_general(a, b, (((0,), (0,)), ((), ())), preferred_element_type=F32)


def nn(a, b):
    return jnp.dot(a, b, preferred_element_type=F32)


def iota(shape, dim):
    return lax.broadcasted_iota(I32, shape, dim)


def split2(x):
    hi = x.astype(BF16)
    return jnp.concatenate([hi, (x - hi.astype(F32)).astype(BF16)], axis=1)


def place_of(block):
    rest = block - 4096
    return jnp.where(
        block < 4096, (block & 1) * 2048 + (block >> 1), 4096 + (rest & 15) * 256 + (rest >> 4)
    )


def gelu_pair(pre):
    tangent = jnp.tanh(ROOT * (pre + 0.044715 * pre * pre * pre))
    value = 0.5 * pre * (1.0 + tangent)
    slope = 0.5 * (1.0 + tangent) + 0.5 * pre * (1.0 - tangent * tangent) * ROOT * (
        1.0 + 0.134145 * pre * pre
    )
    return value, slope


def invert(ord_ref, sgn_ref, meta_ref):
    step = 1024
    for j in range(ROWS):

        def body(c, acc, j=j):
            at = pl.ds(pl.multiple_of(c * step, step), step)
            place = place_of(ord_ref[j : j + 1, at])
            sign = sgn_ref[j : j + 1, at]
            bucket = (c * step + iota((1, step), 1)) >> 4
            row = iota((128, step), 0)
            value = jnp.where(row < 64, bucket >> 1, (bucket & 1) * 2 + sign)
            left = jnp.where((row & 63) == (place >> 7), value, 0).astype(F32).astype(BF16)
            right = jnp.where(row == (place & 127), 1.0, 0.0).astype(BF16)
            return acc + nt(left, right)

        acc = lax.fori_loop(0, NB // step, body, jnp.zeros((128, 128), F32))
        meta_ref[j * 64 : (j + 1) * 64, :] = (acc[:64] * 4.0 + acc[64:]).astype(I32)


def compact(lists, along):
    full = jnp.concatenate([lists, jnp.zeros((120, 128), I32)], axis=0)
    shape = (LIVE, 128)
    slot, lane = iota(shape, 0), iota(shape, 1)
    wanted = jnp.where(slot < 128, slot & 15, jnp.where(slot < 176, slot - 112, 127))
    pick = jnp.where(lane == wanted, 1.0, 0.0).astype(BF16)
    pick_count = jnp.where(lane == 64, 1.0, 0.0).astype(BF16)
    high = (full >> 7).astype(F32).astype(BF16)
    low = (full & 127).astype(F32).astype(BF16)
    if along == 0:
        values = nt(pick, high) * 128.0 + nt(pick, low)
        counts = nt(pick_count, low)
        spot, rep, axis = slot, lane, 1
    else:
        values = nt(high, pick) * 128.0 + nt(low, pick)
        counts = nt(low, pick_count)
        spot, rep, axis = iota((128, LIVE), 1), iota((128, LIVE), 0), 0
    first = (spot < 128) & (rep == (spot >> 4)) & (counts > (spot & 15).astype(F32))
    later = (spot >= 128) & (spot < 176) & (rep < 8) & (counts > 63.5)
    hit = jnp.where(first | later, 1.0, 0.0)
    live = jnp.sum(hit, axis=axis, keepdims=True)
    block = jnp.sum(hit * values, axis=axis, keepdims=True).astype(I32)
    return jnp.where(live > 0.5, place_of(block), -1)


def lists_of(meta_ref, *lead):
    total = jnp.zeros((8, 128), I32)
    for r in range(8):
        total = total + meta_ref[(*lead, slice(CODE + 8 * r, CODE + 8 * r + 8), slice(None))]
    return total


def middle_value(values):
    values = list(values)
    total = len(values)
    for rounds in range(total):
        for i in range(rounds % 2, total - 1, 2):
            lower = jnp.minimum(values[i], values[i + 1])
            upper = jnp.maximum(values[i], values[i + 1])
            values[i] = lower
            values[i + 1] = upper
    return values[total // 2]


def prepare(meta, momv, errv, medv, infov, acrossv):
    lists = lists_of(meta)
    down, across = compact(lists, 0), compact(lists, 1)
    shape = (LIVE, LIVE)
    same = (down == across) & (across >= 0) & (iota(shape, 1) < iota(shape, 0))
    earlier = jnp.max(jnp.where(same, 1.0, 0.0), axis=1, keepdims=True)
    keep = jnp.where((down >= 0) & (earlier < 0.5), 1, 0)
    codes = meta[...]
    high = (codes >> 2).astype(F32).astype(BF16)
    low = (codes & 3).astype(F32).astype(BF16)
    lane = iota((LIVE, 128), 1)
    lane_hit = lane == (down & 127)
    info = jnp.where(lane == ROWS, keep, 0)
    found = []
    for j in range(ROWS):
        pick = jnp.where(iota((LIVE, META), 1) == (down >> 7) + j * 64, 1.0, 0.0)
        pick = jnp.where(down >= 0, pick, 0.0).astype(BF16)
        value = nn(pick, high) * 4.0 + nn(pick, low)
        code = jnp.sum(jnp.where(lane_hit, value, 0.0), axis=1, keepdims=True).astype(I32)
        info = jnp.where(lane == j, code, info)
        probe = errv[j] + LEARN * DECAY * momv[j]
        got = nn(signed_hit(code), split2(probe))
        found.append(got[:, :128] + got[:, 128:])
    medv[...] = middle_value(found)
    infov[...] = info
    acrossv[...] = jnp.broadcast_to(across, acrossv.shape)


def signed_hit(code):
    sign = jnp.where((code & 1) == 1, 1.0, -1.0)
    return jnp.where(iota((LIVE, COUNT), 1) == (code >> 1), sign, 0.0).astype(BF16)


def main_kernel(
    tok_ref, cot_ref, win_ref, wout_ref, ord_ref, sgn_ref, lst_ref, cnt_ref, mom_ref, err_ref,
    ghl_ref, codes_ref, spots_ref, med_ref, info_ref, across_ref,
    own, land, buf, wi, wo, gin, gout, ordv, sgnv, meta, meta2, ghl,
    momv, errv, medv, infov, acrossv, spots, lstv,
    lsem, land_sem, ring_s, ring_r, sib_s, sib_r, w_s, w_r, list_s, list_r, meta_s, meta_r,
):
    rep, shard = lax.axis_index("rep"), lax.axis_index("shard")
    y, core = rep // 2, rep % 2
    x, z = shard // NZ, shard % NZ
    other = 1 - core

    def dev(dx=0, dy=0, dz=0, to=None):
        c = core if to is None else to
        return {
            "rep": lax.rem(y + dy + NY, NY) * 2 + c,
            "shard": lax.rem(x + dx + NX, NX) * NZ + lax.rem(z + dz + NZ, NZ),
        }

    def remote(src, dst, send, recv, device):
        return pltpu.make_async_remote_copy(
            src_ref=src, dst_ref=dst, send_sem=send, recv_sem=recv, device_id=device, device_id_type=MESH
        )

    def on_core(c, *actions):
        @pl.when(core == c)
        def _():
            for action in actions:
                action()

    own_tok = pltpu.make_async_copy(tok_ref, own, lsem.at[0])
    own_cot = pltpu.make_async_copy(cot_ref, own, lsem.at[0])
    loads = [
        pltpu.make_async_copy(lst_ref, lstv, lsem.at[1]),
        pltpu.make_async_copy(ord_ref, ordv, lsem.at[2]),
        pltpu.make_async_copy(sgn_ref, sgnv, lsem.at[3]),
    ]
    tables = [pltpu.make_async_copy(mom_ref.at[:, j, :], momv.at[j], lsem.at[6 + j]) for j in range(ROWS)]
    tables += [pltpu.make_async_copy(err_ref.at[:, j, :], errv.at[j], lsem.at[11 + j]) for j in range(ROWS)]
    own_wi = pltpu.make_async_copy(win_ref, wi.at[:, pl.ds(0, COLS)], lsem.at[4])
    own_wo = pltpu.make_async_copy(wout_ref, wo.at[pl.ds(0, COLS)], lsem.at[5])
    on_core(0, own_tok.start)
    on_core(1, own_cot.start)
    for load in loads:
        load.start()

    barrier = pltpu.get_barrier_semaphore()
    partners = [dev(dz=1), dev(dz=-1)]
    partners += [dev(dx=d, to=c) for d in (1, -1, 2) for c in (0, 1)]
    partners += [dev(dy=d, to=c) for d in (1, 2, 3) for c in (0, 1)] + [dev(to=other)]
    for partner in partners:
        pl.semaphore_signal(barrier, inc=1, device_id=partner, device_id_type=MESH)
    pl.semaphore_wait(barrier, len(partners))

    give_cot = remote(cot_ref, land, land_sem.at[0], land_sem.at[1], dev(to=other))
    give_tok = remote(tok_ref, land, land_sem.at[0], land_sem.at[1], dev(to=other))
    on_core(0, give_cot.start)
    on_core(1, give_tok.start)

    toward = jnp.where(core == 0, -1, 1)
    lower, upper = pl.ds(0, COLS), pl.ds(COLS, COLS)
    landing = pl.ds(pl.multiple_of(other * COLS, COLS), COLS)
    w_in_first = remote(win_ref, wi.at[:, landing], w_s.at[0], w_r.at[0], dev(dx=toward))
    w_out_first = remote(wout_ref, wo.at[landing], w_s.at[1], w_r.at[1], dev(dx=toward))
    w_in_next = remote(wi.at[:, upper], wi.at[:, upper], w_s.at[2], w_r.at[2], dev(dx=-1, to=1))
    w_out_next = remote(wo.at[lower], wo.at[upper], w_s.at[3], w_r.at[3], dev(dx=1, to=1))
    on_core(0, w_in_first.start, w_out_first.start, own_wi.start, own_wo.start)
    on_core(1, w_out_first.start, w_in_first.start)

    loads[0].wait()
    listed = jnp.concatenate([lstv[...], jnp.full(lstv.shape, cnt_ref[0, 0], I32)], axis=1)
    meta[pl.ds(pl.multiple_of(CODE + 8 * rep, 8), 8), :] = jnp.where(iota((8, 128), 0) == rep, listed, 0)
    list_row = meta.at[pl.ds(pl.multiple_of(CODE + 8 * rep, 8), 8)]
    peers = [(0, 1), (1, 0), (1, 1), (2, 0), (2, 1), (3, 0), (3, 1)]
    peers = [(n, dev(dy=d, to=other if flip else core)) for n, (d, flip) in enumerate(peers)]
    list_copies = [remote(list_row, list_row, list_s.at[n], list_r.at[n], peer) for n, peer in peers]
    for copy in list_copies:
        copy.start()

    on_core(0, own_tok.wait, give_cot.wait)
    on_core(1, own_cot.wait, give_tok.wait)
    for c in range(4):
        at = slice(c * 512, (c + 1) * 512)
        mine, theirs = own[:, at].astype(F32), land[:, at].astype(F32)
        first, second = jnp.where(core == 0, mine, theirs), jnp.where(core == 0, theirs, mine)
        buf[core, 0:CHIP, at] = jnp.concatenate([first, second], axis=0).astype(BF16)

    def turn_of(way, sub):
        return sub if way == 0 else 1 - sub

    def unit_of(hops, turn):
        return 0 if hops == 0 else 2 * hops - 1 + turn

    def rows_of(unit, sub):
        return pl.ds(unit * CHIP + SUBS[sub][0], SUBS[sub][1])

    def ring(way, hops, sub):
        turn = turn_of(way, sub)
        return remote(
            buf.at[core, rows_of(unit_of(hops, turn), sub)],
            buf.at[core, rows_of(unit_of(hops + 1, turn), sub)],
            ring_s.at[way, hops, sub], ring_r.at[way, hops, sub],
            dev(dz=1 if way == 0 else -1),
        )

    def sibling(unit, sub):
        at = buf.at[core, rows_of(unit, sub)]
        return remote(at, at, sib_s.at[unit, sub], sib_r.at[unit, sub], dev(to=other))

    for turn in (0, 1):
        ring(0, 0, turn).start()
        ring(1, 0, 1 - turn).start()
    for sub in (0, 1):
        sibling(0, sub).start()
    for load in tables:
        load.start()

    def arrive(hops, turn):
        for way in (0, 1):
            sub = turn if way == 0 else 1 - turn
            ring(way, hops - 1, sub).wait_recv()
            if hops < 3 or (hops == 3 and turn == 0):
                ring(way, hops, sub).start()
            sibling(unit_of(hops, turn), sub).start()

    loads[1].wait()
    loads[2].wait()
    invert(ordv, sgnv, meta)
    for copy in list_copies:
        copy.wait_recv()
    meta_first = remote(meta, meta2.at[other], meta_s.at[0], meta_r.at[0], dev(dx=toward))
    meta_next = remote(meta, meta2.at[1], meta_s.at[1], meta_r.at[1], dev(dx=2))
    meta_first.start()
    on_core(1, meta_next.start)

    @pl.when(core == 0)
    def _():
        meta2[0] = meta[...]

    gin[...] = jnp.zeros_like(gin)
    gout[...] = jnp.zeros_like(gout)

    arrive(1, 0)
    on_core(0, w_in_first.wait_recv, w_in_next.start)
    on_core(1, w_out_first.wait_recv, w_out_next.start)
    arrive(1, 1)
    for load in tables:
        load.wait()
    prepare(meta, momv, errv, medv, infov, acrossv)
    ready = [
        pltpu.make_async_copy(medv, med_ref, lsem.at[16]),
        pltpu.make_async_copy(infov, info_ref, lsem.at[17]),
        pltpu.make_async_copy(acrossv, across_ref, lsem.at[18]),
    ]
    for copy in ready:
        copy.start()
    meta_first.wait_recv()
    on_core(1, meta_next.wait_recv)
    for k in (0, 1):
        spots[k] = jnp.broadcast_to(compact(lists_of(meta2, k), 0), (LIVE, 128))
    ready += [
        pltpu.make_async_copy(meta2, codes_ref, lsem.at[21]),
        pltpu.make_async_copy(spots, spots_ref, lsem.at[22]),
    ]
    for copy in ready[3:]:
        copy.start()
    arrive(2, 0)
    on_core(0, w_out_first.wait_recv, own_wi.wait, own_wo.wait)
    on_core(1, w_in_first.wait_recv, w_in_next.wait_recv, w_out_next.wait_recv)

    def wait_sibling(*units):
        for unit in units:
            for sub in (0, 1):
                sibling(unit, sub).wait_recv()

    out_first = pltpu.make_async_copy(ghl.at[:, pl.ds(0, 4096)], ghl_ref.at[:, pl.ds(0, 4096)], lsem.at[19])
    out_last = pltpu.make_async_copy(ghl.at[:, pl.ds(4096, 4096)], ghl_ref.at[:, pl.ds(4096, 4096)], lsem.at[20])
    ready += [out_first, out_last]

    def work(start, count, last=False):
        rows = pl.ds(start, count)
        value, slope = gelu_pair(nn(buf[0, rows, :], wi[...]))
        back = nt(buf[1, rows, :], wo[...])
        hidden = value.astype(BF16)
        grad = (back * slope).astype(BF16)
        for c in range(4):
            at = slice(c * 512, (c + 1) * 512)
            total = gin[at, :] + tn(buf[0, rows, at], grad)
            if not last:
                gin[at, :] = total
                continue
            for k in range(2):
                for h in range(2):
                    part = total[:, k * COLS + h * 128 : k * COLS + (h + 1) * 128]
                    ghl[k, h * 2048 + c * 512 : h * 2048 + (c + 1) * 512, :] = split2(part)
        if last:
            out_first.start()
        for c in range(4):
            at = slice(c * 512, (c + 1) * 512)
            total = gout[:, at] + tn(hidden, buf[1, rows, at])
            if not last:
                gout[:, at] = total
                continue
            for k in range(2):
                for q in range(4 * c, 4 * c + 4):
                    part = total[k * COLS : (k + 1) * COLS, (q - 4 * c) * 128 : (q - 4 * c + 1) * 128]
                    ghl[k, 4096 + q * 256 : 4352 + q * 256, :] = split2(part)

    def work_pair(i, carry):
        @pl.when(i == 0)
        def _():
            wait_sibling(0, 1)

        @pl.when(i == 1)
        def _():
            wait_sibling(2, 3)

        @pl.when(i == 2)
        def _():
            arrive(2, 1)
            arrive(3, 0)
            wait_sibling(4, 5)

        work(pl.multiple_of(i * (2 * CHIP), 16), 2 * CHIP)
        return carry

    lax.fori_loop(0, 3, work_pair, 0)
    arrive(3, 1)
    wait_sibling(6)
    work(6 * CHIP, CHIP)
    ring(0, 3, 0).wait_recv()
    sibling(7, 0).start()
    ring(1, 3, 1).wait_recv()
    sibling(7, 1).start()
    wait_sibling(7)
    work(7 * CHIP, CHIP, last=True)
    out_last.start()

    for copy in list_copies + [w_in_first, w_out_first, meta_first]:
        copy.wait_send()
    for way in (0, 1):
        for hops in range(4):
            for sub in (0, 1):
                if hops < 3 or sub == way:
                    ring(way, hops, sub).wait_send()
    for unit in range(NZ):
        for sub in (0, 1):
            sibling(unit, sub).wait_send()
    on_core(0, w_in_next.wait_send)
    on_core(1, w_out_next.wait_send, meta_next.wait_send)
    for copy in ready:
        copy.wait()


def sketch_kernel(
    ghl_ref, codes_ref, spots_ref, table_ref,
    ghl, codes, spots, outb, recvx, yb, recvy, tot, lsem, x_s, x_r, y_s, y_r, a_s, a_r,
):
    rep, shard = lax.axis_index("rep"), lax.axis_index("shard")
    y, core = rep // 2, rep % 2
    x, z = shard // NZ, shard % NZ
    other = 1 - core

    def dev(dx=0, dy=0, dz=0, to=None):
        c = core if to is None else to
        return {
            "rep": lax.rem(y + dy + NY, NY) * 2 + c,
            "shard": lax.rem(x + dx + NX, NX) * NZ + lax.rem(z + dz + NZ, NZ),
        }

    def remote(src, dst, send, recv, device):
        return pltpu.make_async_remote_copy(
            src_ref=src, dst_ref=dst, send_sem=send, recv_sem=recv, device_id=device, device_id_type=MESH
        )

    def on_core(c, *actions):
        @pl.when(core == c)
        def _():
            for action in actions:
                action()

    loads = [
        pltpu.make_async_copy(codes_ref, codes, lsem.at[0]),
        pltpu.make_async_copy(spots_ref, spots, lsem.at[1]),
        pltpu.make_async_copy(ghl_ref.at[1], ghl.at[1], lsem.at[2]),
        pltpu.make_async_copy(ghl_ref.at[0], ghl.at[0], lsem.at[3]),
    ]
    for load in loads:
        load.start()
    barrier = pltpu.get_barrier_semaphore()
    partners = [dev(dx=d, to=c) for d in (1, -1, 2) for c in (0, 1)]
    partners += [dev(dy=d) for d in (1, 2, 3)] + [dev(to=other)]
    for partner in partners:
        pl.semaphore_signal(barrier, inc=1, device_id=partner, device_id_type=MESH)
    pl.semaphore_wait(barrier, len(partners))
    loads[0].wait()
    loads[1].wait()

    def spread(code):
        code = jnp.broadcast_to(code, (16, 128))
        bucket = (code >> 1).astype(F32)
        return jnp.where((code & 1) == 1, 1.0, -1.0).astype(BF16), [(bucket - 256.0 * h).astype(BF16) for h in (0, 1)]

    def one_hot(spread_code, quarter):
        sign, spot = spread_code[0], spread_code[1][quarter // 2]
        ramp = iota((256, 128), 0).astype(F32).astype(BF16)
        first = 8 * (quarter % 2)
        hits = [spot == ramp[g * 16 : (g + 1) * 16] for g in range(first, first + 8)]
        return jnp.concatenate([jnp.where(hit, sign, jnp.zeros_like(sign)) for hit in hits], axis=0)

    def sketch(k, work, midway=()):
        step = 8
        per = NB // 512
        used = sorted({j for j, _ in work if j is not None})

        def run(*sums):
            def chunk(t, carry):
                for action, p in midway:

                    @pl.when(t == 1)
                    def _(action=action, p=p):
                        action(p)

                first = [unit * per + t * step for unit in (0, 1)]

                def tile(unit, i):
                    return ghl[k, pl.ds(pl.multiple_of((first[unit] + i) * 256, 256), 256), :]

                found = [
                    {j: codes[k, pl.ds(pl.multiple_of(j * 64 + 2 * first[unit], 8), 2 * step), :] for j in used}
                    for unit in (0, 1)
                ]
                for unit in (0, 1):
                    pltpu.matmul_push_rhs(tile(unit, 0), 0, unit)
                for i in range(step):
                    if i + 1 < step:
                        for unit in (0, 1):
                            pltpu.matmul_push_rhs(tile(unit, i + 1), (i + 1) % 2, unit)
                    rows = [
                        {j: [spread(found[unit][j][2 * i + n : 2 * i + n + 1, :]) for n in (0, 1)] for j in used}
                        for unit in (0, 1)
                    ]
                    for c, (j, q) in enumerate(work):
                        for unit in (0, 1):
                            if j is None:
                                spot = spots[k, q * 128 : (q + 1) * 128, :] - (first[unit] + i) * 256
                                lane = iota((128, 128), 1)
                                hot = [jnp.where(spot == lane + 128 * n, 1.0, 0.0).astype(BF16) for n in (0, 1)]
                            else:
                                hot = [one_hot(rows[unit][j][n], q) for n in (0, 1)]
                            pltpu.matmul_acc_lhs(
                                sums[2 * c + unit],
                                jnp.concatenate(hot, axis=1),
                                load_staged_rhs=i % 2 if c == 0 else None,
                            )
                return carry

            lax.fori_loop(0, per // step, chunk, 0)
            for c, (j, q) in enumerate(work):
                total = pltpu.matmul_pop(sums[2 * c]) + pltpu.matmul_pop(sums[2 * c + 1])
                start = q * 128 + (LISTED if j is None else j * COUNT)
                outb[k, start : start + 128, :] = (total[:, :128] + total[:, 128:]).astype(BF16)

        pl.run_scoped(run, *[pltpu.ACC(mxu_id=unit)((128, 256), F32) for _ in work for unit in (0, 1)])

    def whole(*rows):
        return [(j, q) for j in rows for q in range(4)]

    def half_of(p):
        return PIECES[p][0] // 2, PIECES[p][1] // 2

    def quarter_of(p):
        return PIECES[p][0] // 8, PIECES[p][1] // 8

    def x_copy(k, p, h, slot, device):
        start, rows = half_of(p)
        return remote(
            outb.at[k, pl.ds(PIECES[p][0] + h * rows, rows)], recvx.at[slot, pl.ds(start, rows)],
            x_s.at[k, p, h], x_r.at[slot, p], device,
        )

    x_far = [[x_copy(1, p, h, 1 + 2 * core, dev(dx=1 + core, to=h)) for h in (0, 1)] for p in range(3)]
    x_near = [[x_copy(0, p, h, 2, dev(dx=-1, to=h)) for h in (0, 1)] for p in range(3)]
    x_home = [x_copy(0, p, 1, 0, dev(to=1)) for p in range(3)]

    def x_far_start(p):
        for copy in x_far[p]:
            copy.start()

    def x_near_start(p):
        start, rows = half_of(p)
        on_core(1, *[copy.start for copy in x_near[p]])

        @pl.when(core == 0)
        def _():
            x_home[p].start()
            recvx[0, start : start + rows, :] = outb[0, PIECES[p][0] : PIECES[p][0] + rows, :]

    def my_quarter(p):
        rows = PIECES[p][1] // 8
        return pl.ds(pl.multiple_of(PIECES[p][0] + core * (4 * rows) + y * rows, 16), rows)

    def y_copy(p, d):
        start, rows = quarter_of(p)
        there = pl.ds(pl.multiple_of(4 * start + lax.rem(y + d, NY) * rows, 16), rows)
        return remote(yb.at[there], recvy.at[d - 1, pl.ds(start, rows)], y_s.at[p, d - 1], y_r.at[p, d - 1], dev(dy=d))

    def y_start(p):
        start, rows = half_of(p)
        on_core(1, x_copy(0, p, 1, 0, dev(to=1)).wait_recv)
        for slot in (1, 2, 3):
            x_copy(1, p, 0, slot, dev(dx=1)).wait_recv()
        part = recvx[0, start : start + rows, :].astype(F32)
        for slot in (1, 2, 3):
            part = part + recvx[slot, start : start + rows, :].astype(F32)
        yb[start : start + rows, :] = part.astype(BF16)
        tot[pl.ds(pl.multiple_of(PIECES[p][0] + core * rows, 16), rows), :] = part
        for d in (1, 2, 3):
            y_copy(p, d).start()

    def a_copy(p, d):
        at = tot.at[my_quarter(p)]
        return remote(at, at, a_s.at[p, d - 1], a_r.at[p, d - 1], dev(dy=d))

    def a_start(p):
        start, rows = quarter_of(p)
        total = tot[my_quarter(p), :]
        for d in (1, 2, 3):
            y_copy(p, d).wait_recv()
            total = total + recvy[d - 1, start : start + rows, :].astype(F32)
        tot[my_quarter(p), :] = total
        for d in (1, 2, 3):
            a_copy(p, d).start()

    def e_copy(p):
        rows = PIECES[p][1] // 2
        at = tot.at[pl.ds(pl.multiple_of(PIECES[p][0] + core * rows, 16), rows)]
        return remote(at, at, a_s.at[p, 3], a_r.at[p, 3], dev(to=other))

    def e_start(p):
        for d in (1, 2, 3):
            a_copy(p, d).wait_recv()
        e_copy(p).start()

    def piece_out(p):
        at = pl.ds(*PIECES[p])
        return pltpu.make_async_copy(tot.at[at], table_ref.at[at], lsem.at[4 + p])

    def e_finish(p):
        e_copy(p).wait_recv()
        piece_out(p).start()

    passes = (whole(0, 1), whole(2, 3), whole(4) + [(None, 0), (None, 1)])
    loads[2].wait()
    for p in range(3):
        sketch(1, passes[p])
        x_far_start(p)
    loads[3].wait()
    sketch(0, passes[0])
    x_near_start(0)
    sketch(0, passes[1], [(y_start, 0)])
    x_near_start(1)
    a_start(0)
    sketch(0, passes[2], [(y_start, 1), (e_start, 0)])
    x_near_start(2)
    a_start(1)
    e_finish(0)
    y_start(2)
    e_start(1)
    a_start(2)
    e_finish(1)
    e_start(2)
    e_finish(2)

    for p in range(3):
        for copy in x_far[p] + [y_copy(p, d) for d in (1, 2, 3)] + [a_copy(p, d) for d in (1, 2, 3)] + [e_copy(p)]:
            copy.wait_send()
    on_core(0, *[copy.wait_send for copy in x_home])
    on_core(1, *[c.wait_send for p in range(3) for c in x_near[p]])
    for p in range(3):
        piece_out(p).wait()


def run_main(*args):
    anywhere = pl.BlockSpec(memory_space=pl.ANY)
    dma = pltpu.SemaphoreType.DMA
    return pl.pallas_call(
        main_kernel,
        out_shape=(
            jax.ShapeDtypeStruct((2, NB, 256), BF16),
            jax.ShapeDtypeStruct((2, META, 128), I32),
            jax.ShapeDtypeStruct((2, LIVE, 128), I32),
            jax.ShapeDtypeStruct((LIVE, 128), F32),
            jax.ShapeDtypeStruct((LIVE, 128), I32),
            jax.ShapeDtypeStruct((8, LIVE), I32),
        ),
        in_specs=[anywhere] * 7 + [pl.BlockSpec(memory_space=pltpu.SMEM)] + [anywhere] * 2,
        out_specs=(anywhere,) * 6,
        scratch_shapes=[
            pltpu.VMEM((TOK, DW), BF16),
            pltpu.VMEM((TOK, DW), BF16),
            pltpu.VMEM((2, NZ * CHIP, DW), BF16),
            pltpu.VMEM((DW, 2 * COLS), BF16),
            pltpu.VMEM((2 * COLS, DW), BF16),
            pltpu.VMEM((DW, 2 * COLS), F32),
            pltpu.VMEM((2 * COLS, DW), F32),
            pltpu.VMEM((ROWS, NB), I32),
            pltpu.VMEM((ROWS, NB), I32),
            pltpu.VMEM((META, 128), I32),
            pltpu.VMEM((2, META, 128), I32),
            pltpu.VMEM((2, NB, 256), BF16),
            pltpu.VMEM((ROWS, COUNT, 128), F32),
            pltpu.VMEM((ROWS, COUNT, 128), F32),
            pltpu.VMEM((LIVE, 128), F32),
            pltpu.VMEM((LIVE, 128), I32),
            pltpu.VMEM((8, LIVE), I32),
            pltpu.VMEM((2, LIVE, 128), I32),
            pltpu.VMEM((1, 64), I32),
            dma((23,)), dma((2,)),
            dma((2, 4, 2)), dma((2, 4, 2)), dma((NZ, 2)), dma((NZ, 2)), dma((4,)), dma((4,)),
            dma((7,)), dma((7,)), dma((2,)), dma((2,)),
        ],
        compiler_params=pltpu.CompilerParams(
            collective_id=0, has_side_effects=True, vmem_limit_bytes=62 * 1024 * 1024
        ),
        cost_estimate=pl.CostEstimate(flops=15_000_000_000, bytes_accessed=20_000_000, transcendentals=2_000_000),
        name="gather_grad",
    )(*args)


def run_sketch(ghl, codes, spots):
    anywhere = pl.BlockSpec(memory_space=pl.ANY)
    dma = pltpu.SemaphoreType.DMA
    return pl.pallas_call(
        sketch_kernel,
        out_shape=jax.ShapeDtypeStruct((TAB, 128), F32),
        in_specs=[anywhere] * 3,
        out_specs=anywhere,
        scratch_shapes=[
            pltpu.VMEM((2, NB, 256), BF16),
            pltpu.VMEM((2, META, 128), I32),
            pltpu.VMEM((2, LIVE, 128), I32),
            pltpu.VMEM((2, TAB, 128), BF16),
            pltpu.VMEM((4, TAB // 2, 128), BF16),
            pltpu.VMEM((TAB // 2, 128), BF16),
            pltpu.VMEM((3, TAB // 8, 128), BF16),
            pltpu.VMEM((TAB, 128), F32),
            dma((7,)), dma((2, 3, 2)), dma((4, 3)), dma((3, 3)), dma((3, 3)), dma((3, 4)), dma((3, 4)),
        ],
        compiler_params=pltpu.CompilerParams(
            collective_id=1, has_side_effects=True, vmem_limit_bytes=62 * 1024 * 1024
        ),
        cost_estimate=pl.CostEstimate(flops=24_000_000_000, bytes_accessed=10_000_000, transcendentals=0),
        name="sketch_reduce",
    )(ghl, codes, spots)


def finish_kernel(
    table, med, info, across, mom, err, w_in, w_out,
    win_new, wout_new, mom_new, err_new,
    tabv, medv, infov, acrossv, momv, errv, winv, woutv, winn, woutn, momn, errn, sem, out_sem,
):
    pairs = [(mom.at[:, j, :], momv.at[j]) for j in range(ROWS)] + [(err.at[:, j, :], errv.at[j]) for j in range(ROWS)]
    pairs += [(table, tabv), (info, infov), (med, medv), (across, acrossv), (w_in, winv), (w_out, woutv)]
    loads = [pltpu.make_async_copy(src, dst, sem.at[n]) for n, (src, dst) in enumerate(pairs)]
    for load in loads:
        load.start()
    stores = []

    def store(src, dst):
        stores.append(pltpu.make_async_copy(src, dst, out_sem.at[len(stores)]))
        stores[-1].start()

    loads[10].wait()
    for j in range(ROWS):
        loads[j].wait()
        momn[j] = DECAY * momv[j] + tabv[j * COUNT : (j + 1) * COUNT, :]
        store(momn.at[j], mom_new.at[:, j, :])
    for load in loads[11:14]:
        load.wait()
    codes = infov[...]
    update = medv[...] + LEARN * tabv[LISTED:, :]
    kept = split2(jnp.where(codes[:, ROWS : ROWS + 1] == 1, update, 0.0))
    for j in range(ROWS):
        loads[5 + j].wait()
        gone = tn(signed_hit(codes[:, j : j + 1]), kept)
        errn[j] = errv[j] + LEARN * momn[j] - (gone[:, :128] + gone[:, 128:])
        store(errn.at[j], err_new.at[:, j, :])
    places = acrossv[0:1, :]

    def delta(start, rows):
        hit = jnp.where(iota((rows, LIVE), 0) + start == places, 1.0, 0.0).astype(BF16)
        got = nn(hit, kept)
        return got[:, :128] + got[:, 128:]

    loads[14].wait()
    for c in range(4):
        rows = pl.ds(c * 512, 512)
        for h in range(2):
            at = slice(h * 128, (h + 1) * 128)
            winn[rows, at] = winv[rows, at].astype(F32) - delta(h * 2048 + c * 512, 512)
        store(winn.at[rows], win_new.at[rows])
    loads[15].wait()
    for c in range(4):
        for q in range(4 * c, 4 * c + 4):
            at = slice(q * 128, (q + 1) * 128)
            woutn[:, at] = woutv[:, at].astype(F32) - delta(4096 + q * 256, 256)
        at = pl.ds(c * 512, 512)
        store(woutn.at[:, at], wout_new.at[:, at])
    for copy in stores:
        copy.wait()


def run_finish(table, med, info, across, mom, err, w_in, w_out):
    anywhere = pl.BlockSpec(memory_space=pl.ANY)
    vmem = pltpu.VMEM
    deep = vmem((ROWS, COUNT, 128), F32)
    return pl.pallas_call(
        finish_kernel,
        out_shape=(
            jax.ShapeDtypeStruct(w_in.shape, F32),
            jax.ShapeDtypeStruct(w_out.shape, F32),
            jax.ShapeDtypeStruct(mom.shape, F32),
            jax.ShapeDtypeStruct(err.shape, F32),
        ),
        in_specs=[anywhere] * 8,
        out_specs=(anywhere,) * 4,
        scratch_shapes=[
            vmem((TAB, 128), F32), vmem((LIVE, 128), F32), vmem((LIVE, 128), I32), vmem((8, LIVE), I32),
            deep, deep, vmem(w_in.shape, BF16), vmem(w_out.shape, BF16), vmem(w_in.shape, F32), vmem(w_out.shape, F32),
            deep, deep, pltpu.SemaphoreType.DMA((16,)), pltpu.SemaphoreType.DMA((18,)),
        ],
        compiler_params=pltpu.CompilerParams(vmem_limit_bytes=62 * 1024 * 1024),
        cost_estimate=pl.CostEstimate(flops=3_000_000_000, bytes_accessed=16_000_000, transcendentals=0),
        name="finish",
    )(table, med, info, across, mom, err, w_in, w_out)


def per_device(
    tokens, cotangent, w_in, w_out, momentum, error, block_order, signs, heavy_blocks, heavy_count
):
    mom, err = by_bucket(momentum), by_bucket(error)
    ghl, codes, spots, med, info, across = run_main(
        tokens, cotangent, w_in, w_out, block_order, signs, heavy_blocks, heavy_count, mom, err
    )
    table = run_sketch(ghl, codes, spots)
    win_new, wout_new, mom_new, err_new = run_finish(table, med, info, across, mom, err, w_in, w_out)
    return win_new, wout_new, by_row(mom_new), by_row(err_new)


def by_bucket(table):
    return jnp.transpose(table.reshape(ROWS, COUNT, 128), (1, 0, 2))


def by_row(table):
    return jnp.transpose(table, (1, 0, 2)).reshape(ROWS, COUNT * 128)


def solution(mesh):
    placed = (
        P(("rep", "shard"), None),
        P(("rep", "shard"), None),
        P(None, "shard"),
        P("shard", None),
        P(None, "shard"),
        P(None, "shard"),
        P(None, "shard"),
        P(None, "shard"),
        P("rep", "shard"),
        P("rep", "shard"),
    )
    return jax.shard_map(
        per_device,
        mesh=mesh,
        in_specs=placed,
        out_specs=(P(None, "shard"), P("shard", None), P(None, "shard"), P(None, "shard")),
        check_vma=False,
    )
```

```python
import functools

import jax
import jax.numpy as jnp
from jax import lax
from jax.experimental import pallas as pl
from jax.experimental.pallas import tpu as pltpu
from jax.sharding import PartitionSpec as P

MESH = pl.DeviceIdType.MESH
F32, BF16, I32 = jnp.float32, jnp.bfloat16, jnp.int32
LEARN = 0.05
DECAY = 0.9
ROOT = 0.7978845608028654

NX, NY, NZ = 4, 4, 8
TOK = 104
CHIP = 2 * TOK
SUBS = ((0, 112), (112, 96))
DW, COLS = 2048, 256
NB = 8192
COUNT = 512
ROWS = 5
LIVE = 256
LISTED = ROWS * COUNT
TAB = LISTED + LIVE
PIECES = ((0, 1024), (1024, 1024), (2048, 768))
CODE = ROWS * 64
META = CODE + 64


def nt(a, b):
    return lax.dot_general(a, b, (((1,), (1,)), ((), ())), preferred_element_type=F32)


def tn(a, b):
    return lax.dot_general(a, b, (((0,), (0,)), ((), ())), preferred_element_type=F32)


def nn(a, b):
    return jnp.dot(a, b, preferred_element_type=F32)


def iota(shape, dim):
    return lax.broadcasted_iota(I32, shape, dim)


def split2(x):
    hi = x.astype(BF16)
    return jnp.concatenate([hi, (x - hi.astype(F32)).astype(BF16)], axis=1)


def place_of(block):
    rest = block - 4096
    return jnp.where(
        block < 4096, (block & 1) * 2048 + (block >> 1), 4096 + (rest & 15) * 256 + (rest >> 4)
    )


def gelu_pair(pre):
    tangent = jnp.tanh(ROOT * (pre + 0.044715 * pre * pre * pre))
    value = 0.5 * pre * (1.0 + tangent)
    slope = 0.5 * (1.0 + tangent) + 0.5 * pre * (1.0 - tangent * tangent) * ROOT * (
        1.0 + 0.134145 * pre * pre
    )
    return value, slope


def invert(ord_ref, sgn_ref, meta_ref):
    step = 1024
    for j in range(ROWS):

        def body(c, acc, j=j):
            at = pl.ds(pl.multiple_of(c * step, step), step)
            place = place_of(ord_ref[j : j + 1, at])
            sign = sgn_ref[j : j + 1, at]
            bucket = (c * step + iota((1, step), 1)) >> 4
            row = iota((128, step), 0)
            value = jnp.where(row < 64, bucket >> 1, (bucket & 1) * 2 + sign)
            left = jnp.where((row & 63) == (place >> 7), value, 0).astype(F32).astype(BF16)
            right = jnp.where(row == (place & 127), 1.0, 0.0).astype(BF16)
            return acc + nt(left, right)

        acc = lax.fori_loop(0, NB // step, body, jnp.zeros((128, 128), F32))
        meta_ref[j * 64 : (j + 1) * 64, :] = (acc[:64] * 4.0 + acc[64:]).astype(I32)


def compact(lists, along):
    full = jnp.concatenate([lists, jnp.zeros((120, 128), I32)], axis=0)
    shape = (LIVE, 128)
    slot, lane = iota(shape, 0), iota(shape, 1)
    wanted = jnp.where(slot < 128, slot & 15, jnp.where(slot < 176, slot - 112, 127))
    pick = jnp.where(lane == wanted, 1.0, 0.0).astype(BF16)
    pick_count = jnp.where(lane == 64, 1.0, 0.0).astype(BF16)
    high = (full >> 7).astype(F32).astype(BF16)
    low = (full & 127).astype(F32).astype(BF16)
    if along == 0:
        values = nt(pick, high) * 128.0 + nt(pick, low)
        counts = nt(pick_count, low)
        spot, rep, axis = slot, lane, 1
    else:
        values = nt(high, pick) * 128.0 + nt(low, pick)
        counts = nt(low, pick_count)
        spot, rep, axis = iota((128, LIVE), 1), iota((128, LIVE), 0), 0
    first = (spot < 128) & (rep == (spot >> 4)) & (counts > (spot & 15).astype(F32))
    later = (spot >= 128) & (spot < 176) & (rep < 8) & (counts > 63.5)
    hit = jnp.where(first | later, 1.0, 0.0)
    live = jnp.sum(hit, axis=axis, keepdims=True)
    block = jnp.sum(hit * values, axis=axis, keepdims=True).astype(I32)
    return jnp.where(live > 0.5, place_of(block), -1)


def lists_of(meta_ref, *lead):
    total = jnp.zeros((8, 128), I32)
    for r in range(8):
        total = total + meta_ref[(*lead, slice(CODE + 8 * r, CODE + 8 * r + 8), slice(None))]
    return total


def middle_value(values):
    values = list(values)
    total = len(values)
    for rounds in range(total):
        for i in range(rounds % 2, total - 1, 2):
            lower = jnp.minimum(values[i], values[i + 1])
            upper = jnp.maximum(values[i], values[i + 1])
            values[i] = lower
            values[i + 1] = upper
    return values[total // 2]


def prepare(meta, momv, errv, medv, infov, acrossv):
    lists = lists_of(meta)
    down, across = compact(lists, 0), compact(lists, 1)
    shape = (LIVE, LIVE)
    same = (down == across) & (across >= 0) & (iota(shape, 1) < iota(shape, 0))
    earlier = jnp.max(jnp.where(same, 1.0, 0.0), axis=1, keepdims=True)
    keep = jnp.where((down >= 0) & (earlier < 0.5), 1, 0)
    codes = meta[...]
    high = (codes >> 2).astype(F32).astype(BF16)
    low = (codes & 3).astype(F32).astype(BF16)
    lane = iota((LIVE, 128), 1)
    lane_hit = lane == (down & 127)
    info = jnp.where(lane == ROWS, keep, 0)
    found = []
    for j in range(ROWS):
        pick = jnp.where(iota((LIVE, META), 1) == (down >> 7) + j * 64, 1.0, 0.0)
        pick = jnp.where(down >= 0, pick, 0.0).astype(BF16)
        value = nn(pick, high) * 4.0 + nn(pick, low)
        code = jnp.sum(jnp.where(lane_hit, value, 0.0), axis=1, keepdims=True).astype(I32)
        info = jnp.where(lane == j, code, info)
        probe = errv[j] + LEARN * DECAY * momv[j]
        got = nn(signed_hit(code), split2(probe))
        found.append(got[:, :128] + got[:, 128:])
    medv[...] = middle_value(found)
    infov[...] = info
    acrossv[...] = jnp.broadcast_to(across, acrossv.shape)


def signed_hit(code):
    sign = jnp.where((code & 1) == 1, 1.0, -1.0)
    return jnp.where(iota((LIVE, COUNT), 1) == (code >> 1), sign, 0.0).astype(BF16)


def main_kernel(
    tok_ref, cot_ref, win_ref, wout_ref, ord_ref, sgn_ref, lst_ref, cnt_ref, mom_ref, err_ref,
    ghl_ref, codes_ref, spots_ref, med_ref, info_ref, across_ref,
    own, land, buf, wi, wo, gin, gout, ordv, sgnv, meta, meta2, ghl,
    momv, errv, medv, infov, acrossv, spots, lstv,
    lsem, land_sem, ring_s, ring_r, sib_s, sib_r, w_s, w_r, list_s, list_r, meta_s, meta_r,
):
    rep, shard = lax.axis_index("rep"), lax.axis_index("shard")
    y, core = rep // 2, rep % 2
    x, z = shard // NZ, shard % NZ
    other = 1 - core

    def dev(dx=0, dy=0, dz=0, to=None):
        c = core if to is None else to
        return {
            "rep": lax.rem(y + dy + NY, NY) * 2 + c,
            "shard": lax.rem(x + dx + NX, NX) * NZ + lax.rem(z + dz + NZ, NZ),
        }

    def remote(src, dst, send, recv, device):
        return pltpu.make_async_remote_copy(
            src_ref=src, dst_ref=dst, send_sem=send, recv_sem=recv, device_id=device, device_id_type=MESH
        )

    def on_core(c, *actions):
        @pl.when(core == c)
        def _():
            for action in actions:
                action()

    own_tok = pltpu.make_async_copy(tok_ref, own, lsem.at[0])
    own_cot = pltpu.make_async_copy(cot_ref, own, lsem.at[0])
    loads = [
        pltpu.make_async_copy(lst_ref, lstv, lsem.at[1]),
        pltpu.make_async_copy(ord_ref, ordv, lsem.at[2]),
        pltpu.make_async_copy(sgn_ref, sgnv, lsem.at[3]),
    ]
    tables = [pltpu.make_async_copy(mom_ref.at[:, j, :], momv.at[j], lsem.at[6 + j]) for j in range(ROWS)]
    tables += [pltpu.make_async_copy(err_ref.at[:, j, :], errv.at[j], lsem.at[11 + j]) for j in range(ROWS)]
    own_wi = pltpu.make_async_copy(win_ref, wi.at[:, pl.ds(0, COLS)], lsem.at[4])
    own_wo = pltpu.make_async_copy(wout_ref, wo.at[pl.ds(0, COLS)], lsem.at[5])
    on_core(0, own_tok.start)
    on_core(1, own_cot.start)
    for load in loads:
        load.start()

    barrier = pltpu.get_barrier_semaphore()
    partners = [dev(dz=1), dev(dz=-1)]
    partners += [dev(dx=d, to=c) for d in (1, -1, 2) for c in (0, 1)]
    partners += [dev(dy=d, to=c) for d in (1, 2, 3) for c in (0, 1)] + [dev(to=other)]
    for partner in partners:
        pl.semaphore_signal(barrier, inc=1, device_id=partner, device_id_type=MESH)
    pl.semaphore_wait(barrier, len(partners))

    give_cot = remote(cot_ref, land, land_sem.at[0], land_sem.at[1], dev(to=other))
    give_tok = remote(tok_ref, land, land_sem.at[0], land_sem.at[1], dev(to=other))
    on_core(0, give_cot.start)
    on_core(1, give_tok.start)

    toward = jnp.where(core == 0, -1, 1)
    lower, upper = pl.ds(0, COLS), pl.ds(COLS, COLS)
    landing = pl.ds(pl.multiple_of(other * COLS, COLS), COLS)
    w_in_first = remote(win_ref, wi.at[:, landing], w_s.at[0], w_r.at[0], dev(dx=toward))
    w_out_first = remote(wout_ref, wo.at[landing], w_s.at[1], w_r.at[1], dev(dx=toward))
    w_in_next = remote(wi.at[:, upper], wi.at[:, upper], w_s.at[2], w_r.at[2], dev(dx=-1, to=1))
    w_out_next = remote(wo.at[lower], wo.at[upper], w_s.at[3], w_r.at[3], dev(dx=1, to=1))
    on_core(0, w_in_first.start, w_out_first.start, own_wi.start, own_wo.start)
    on_core(1, w_out_first.start, w_in_first.start)

    loads[0].wait()
    listed = jnp.concatenate([lstv[...], jnp.full(lstv.shape, cnt_ref[0, 0], I32)], axis=1)
    meta[pl.ds(pl.multiple_of(CODE + 8 * rep, 8), 8), :] = jnp.where(iota((8, 128), 0) == rep, listed, 0)
    list_row = meta.at[pl.ds(pl.multiple_of(CODE + 8 * rep, 8), 8)]
    peers = [(0, 1), (1, 0), (1, 1), (2, 0), (2, 1), (3, 0), (3, 1)]
    peers = [(n, dev(dy=d, to=other if flip else core)) for n, (d, flip) in enumerate(peers)]
    list_copies = [remote(list_row, list_row, list_s.at[n], list_r.at[n], peer) for n, peer in peers]
    for copy in list_copies:
        copy.start()

    on_core(0, own_tok.wait, give_cot.wait)
    on_core(1, own_cot.wait, give_tok.wait)
    for c in range(4):
        at = slice(c * 512, (c + 1) * 512)
        mine, theirs = own[:, at].astype(F32), land[:, at].astype(F32)
        first, second = jnp.where(core == 0, mine, theirs), jnp.where(core == 0, theirs, mine)
        buf[core, 0:CHIP, at] = jnp.concatenate([first, second], axis=0).astype(BF16)

    def turn_of(way, sub):
        return sub if way == 0 else 1 - sub

    def unit_of(hops, turn):
        return 0 if hops == 0 else 2 * hops - 1 + turn

    def rows_of(unit, sub):
        return pl.ds(unit * CHIP + SUBS[sub][0], SUBS[sub][1])

    def ring(way, hops, sub):
        turn = turn_of(way, sub)
        return remote(
            buf.at[core, rows_of(unit_of(hops, turn), sub)],
            buf.at[core, rows_of(unit_of(hops + 1, turn), sub)],
            ring_s.at[way, hops, sub], ring_r.at[way, hops, sub],
            dev(dz=1 if way == 0 else -1),
        )

    def sibling(unit, sub):
        at = buf.at[core, rows_of(unit, sub)]
        return remote(at, at, sib_s.at[unit, sub], sib_r.at[unit, sub], dev(to=other))

    for turn in (0, 1):
        ring(0, 0, turn).start()
        ring(1, 0, 1 - turn).start()
    for sub in (0, 1):
        sibling(0, sub).start()
    for load in tables:
        load.start()

    def arrive(hops, turn):
        for way in (0, 1):
            sub = turn if way == 0 else 1 - turn
            ring(way, hops - 1, sub).wait_recv()
            if hops < 3 or (hops == 3 and turn == 0):
                ring(way, hops, sub).start()
            sibling(unit_of(hops, turn), sub).start()

    loads[1].wait()
    loads[2].wait()
    invert(ordv, sgnv, meta)
    for copy in list_copies:
        copy.wait_recv()
    meta_first = remote(meta, meta2.at[other], meta_s.at[0], meta_r.at[0], dev(dx=toward))
    meta_next = remote(meta, meta2.at[1], meta_s.at[1], meta_r.at[1], dev(dx=2))
    meta_first.start()
    on_core(1, meta_next.start)

    @pl.when(core == 0)
    def _():
        meta2[0] = meta[...]

    gin[...] = jnp.zeros_like(gin)
    gout[...] = jnp.zeros_like(gout)

    arrive(1, 0)
    on_core(0, w_in_first.wait_recv, w_in_next.start)
    on_core(1, w_out_first.wait_recv, w_out_next.start)
    arrive(1, 1)
    for load in tables:
        load.wait()
    prepare(meta, momv, errv, medv, infov, acrossv)
    ready = [
        pltpu.make_async_copy(medv, med_ref, lsem.at[16]),
        pltpu.make_async_copy(infov, info_ref, lsem.at[17]),
        pltpu.make_async_copy(acrossv, across_ref, lsem.at[18]),
    ]
    for copy in ready:
        copy.start()
    meta_first.wait_recv()
    on_core(1, meta_next.wait_recv)
    for k in (0, 1):
        spots[k] = jnp.broadcast_to(compact(lists_of(meta2, k), 0), (LIVE, 128))
    ready += [
        pltpu.make_async_copy(meta2, codes_ref, lsem.at[21]),
        pltpu.make_async_copy(spots, spots_ref, lsem.at[22]),
    ]
    for copy in ready[3:]:
        copy.start()
    arrive(2, 0)
    on_core(0, w_out_first.wait_recv, own_wi.wait, own_wo.wait)
    on_core(1, w_in_first.wait_recv, w_in_next.wait_recv, w_out_next.wait_recv)

    def wait_sibling(*units):
        for unit in units:
            for sub in (0, 1):
                sibling(unit, sub).wait_recv()

    out_first = pltpu.make_async_copy(ghl.at[:, pl.ds(0, 4096)], ghl_ref.at[:, pl.ds(0, 4096)], lsem.at[19])
    out_last = pltpu.make_async_copy(ghl.at[:, pl.ds(4096, 4096)], ghl_ref.at[:, pl.ds(4096, 4096)], lsem.at[20])
    ready += [out_first, out_last]

    def work(i, carry):
        @pl.when(i == 0)
        def _():
            wait_sibling(0, 1, 2, 3)

        @pl.when(i == 2)
        def _():
            arrive(2, 1)

        @pl.when(i == 4)
        def _():
            wait_sibling(4)
            arrive(3, 0)

        @pl.when(i == 5)
        def _():
            wait_sibling(5)

        @pl.when(i == 6)
        def _():
            arrive(3, 1)
            wait_sibling(6)

        @pl.when(i == 7)
        def _():
            ring(0, 3, 0).wait_recv()
            sibling(7, 0).start()
            ring(1, 3, 1).wait_recv()
            sibling(7, 1).start()
            wait_sibling(7)

        rows = pl.ds(pl.multiple_of(i * CHIP, 16), CHIP)
        value, slope = gelu_pair(nn(buf[0, rows, :], wi[...]))
        back = nt(buf[1, rows, :], wo[...])
        hidden = value.astype(BF16)
        grad = (back * slope).astype(BF16)
        for c in range(4):
            at = slice(c * 512, (c + 1) * 512)
            gin[at, :] += tn(buf[0, rows, at], grad)
            gout[:, at] += tn(hidden, buf[1, rows, at])
        return carry

    lax.fori_loop(0, NZ, work, 0)

    def split_in(r, carry):
        rows = pl.ds(pl.multiple_of(r * 256, 256), 256)
        for k in range(2):
            for h in range(2):
                at = slice(k * COLS + h * 128, k * COLS + (h + 1) * 128)
                ghl[k, pl.ds(pl.multiple_of(h * 2048 + r * 256, 256), 256), :] = split2(gin[rows, at])
        return carry

    def split_out(q, carry):
        at = pl.ds(pl.multiple_of(q * 128, 128), 128)
        for k in range(2):
            rows = pl.ds(pl.multiple_of(4096 + q * 256, 256), 256)
            ghl[k, rows, :] = split2(gout[k * COLS : (k + 1) * COLS, at])
        return carry

    lax.fori_loop(0, 8, split_in, 0)
    out_first.start()
    lax.fori_loop(0, 16, split_out, 0)
    out_last.start()

    for copy in list_copies + [w_in_first, w_out_first, meta_first]:
        copy.wait_send()
    for way in (0, 1):
        for hops in range(4):
            for sub in (0, 1):
                if hops < 3 or sub == way:
                    ring(way, hops, sub).wait_send()
    for unit in range(NZ):
        for sub in (0, 1):
            sibling(unit, sub).wait_send()
    on_core(0, w_in_next.wait_send)
    on_core(1, w_out_next.wait_send, meta_next.wait_send)
    for copy in ready:
        copy.wait()


def sketch_kernel(
    ghl_ref, codes_ref, spots_ref, table_ref,
    ghl, codes, spots, outb, recvx, yb, recvy, tot, lsem, x_s, x_r, y_s, y_r, a_s, a_r,
):
    rep, shard = lax.axis_index("rep"), lax.axis_index("shard")
    y, core = rep // 2, rep % 2
    x, z = shard // NZ, shard % NZ
    other = 1 - core

    def dev(dx=0, dy=0, dz=0, to=None):
        c = core if to is None else to
        return {
            "rep": lax.rem(y + dy + NY, NY) * 2 + c,
            "shard": lax.rem(x + dx + NX, NX) * NZ + lax.rem(z + dz + NZ, NZ),
        }

    def remote(src, dst, send, recv, device):
        return pltpu.make_async_remote_copy(
            src_ref=src, dst_ref=dst, send_sem=send, recv_sem=recv, device_id=device, device_id_type=MESH
        )

    def on_core(c, *actions):
        @pl.when(core == c)
        def _():
            for action in actions:
                action()

    loads = [
        pltpu.make_async_copy(codes_ref, codes, lsem.at[0]),
        pltpu.make_async_copy(spots_ref, spots, lsem.at[1]),
        pltpu.make_async_copy(ghl_ref.at[1], ghl.at[1], lsem.at[2]),
        pltpu.make_async_copy(ghl_ref.at[0], ghl.at[0], lsem.at[3]),
    ]
    for load in loads:
        load.start()
    barrier = pltpu.get_barrier_semaphore()
    partners = [dev(dx=d, to=c) for d in (1, -1, 2) for c in (0, 1)]
    partners += [dev(dy=d) for d in (1, 2, 3)] + [dev(to=other)]
    for partner in partners:
        pl.semaphore_signal(barrier, inc=1, device_id=partner, device_id_type=MESH)
    pl.semaphore_wait(barrier, len(partners))
    loads[0].wait()
    loads[1].wait()

    def spread(code):
        code = jnp.broadcast_to(code, (16, 128))
        bucket = (code >> 1).astype(F32)
        return jnp.where((code & 1) == 1, 1.0, -1.0).astype(BF16), [(bucket - 256.0 * h).astype(BF16) for h in (0, 1)]

    def one_hot(spread_code, quarter):
        sign, spot = spread_code[0], spread_code[1][quarter // 2]
        ramp = iota((256, 128), 0).astype(F32).astype(BF16)
        first = 8 * (quarter % 2)
        hits = [spot == ramp[g * 16 : (g + 1) * 16] for g in range(first, first + 8)]
        return jnp.concatenate([jnp.where(hit, sign, jnp.zeros_like(sign)) for hit in hits], axis=0)

    def sketch(k, work, midway):
        per = NB // 512
        used = sorted({j for j, _ in work if j is not None})

        def run(*sums):
            def push(unit, index, register):
                at = pl.ds(pl.multiple_of((unit * per + index) * 256, 256), 256)
                pltpu.matmul_push_rhs(ghl[k, at, :], register, unit)

            def chunk(t, carry):
                @pl.when(t == 3)
                def _():
                    midway()

                wide = [
                    {
                        j: codes[k, pl.ds(pl.multiple_of(j * 64 + 2 * unit * per + (t // 2) * 8, 8), 8), :]
                        for j in used
                    }
                    for unit in (0, 1)
                ]
                odd = lax.rem(t, 2) == 1
                found = [{j: jnp.where(odd, v[4:8], v[0:4]) for j, v in each.items()} for each in wide]
                for i in (0, 1):
                    for unit in (0, 1):
                        push(unit, 2 * t + 1 if i == 0 else lax.rem(2 * t + 2, per), 1 - i)
                    rows = [
                        {j: [spread(found[unit][j][2 * i + n : 2 * i + n + 1, :]) for n in (0, 1)] for j in used}
                        for unit in (0, 1)
                    ]
                    for c, (j, q) in enumerate(work):
                        for unit in (0, 1):
                            if j is None:
                                spot = spots[k, q * 128 : (q + 1) * 128, :] - (unit * per + 2 * t + i) * 256
                                lane = iota((128, 128), 1)
                                hot = [jnp.where(spot == lane + 128 * n, 1.0, 0.0).astype(BF16) for n in (0, 1)]
                            else:
                                hot = [one_hot(rows[unit][j][n], q) for n in (0, 1)]
                            pltpu.matmul_acc_lhs(
                                sums[2 * c + unit],
                                jnp.concatenate(hot, axis=1),
                                load_staged_rhs=i if c == 0 else None,
                            )
                return carry

            for unit in (0, 1):
                push(unit, 0, 0)
            lax.fori_loop(0, per // 2, chunk, 0)
            for unit in (0, 1):
                pltpu.matmul_acc_lhs(sums[unit], jnp.zeros((128, 256), BF16), load_staged_rhs=0)
            for c, (j, q) in enumerate(work):
                total = pltpu.matmul_pop(sums[2 * c]) + pltpu.matmul_pop(sums[2 * c + 1])
                start = q * 128 + (LISTED if j is None else j * COUNT)
                outb[k, start : start + 128, :] = (total[:, :128] + total[:, 128:]).astype(BF16)

        pl.run_scoped(run, *[pltpu.ACC(mxu_id=unit)((128, 256), F32) for _ in work for unit in (0, 1)])

    def whole(*rows):
        return [(j, q) for j in rows for q in range(4)]

    def half_of(p):
        return PIECES[p][0] // 2, PIECES[p][1] // 2

    def quarter_of(p):
        return PIECES[p][0] // 8, PIECES[p][1] // 8

    def x_copy(k, p, h, slot, device):
        start, rows = half_of(p)
        return remote(
            outb.at[k, pl.ds(PIECES[p][0] + h * rows, rows)], recvx.at[slot, pl.ds(start, rows)],
            x_s.at[k, p, h], x_r.at[slot, p], device,
        )

    x_far = [[x_copy(1, p, h, 1 + 2 * core, dev(dx=1 + core, to=h)) for h in (0, 1)] for p in range(3)]
    x_near = [[x_copy(0, p, h, 2, dev(dx=-1, to=h)) for h in (0, 1)] for p in range(3)]
    x_home = [x_copy(0, p, 1, 0, dev(to=1)) for p in range(3)]

    def x_far_start(p):
        for copy in x_far[p]:
            copy.start()

    def x_near_start(p):
        start, rows = half_of(p)
        on_core(1, *[copy.start for copy in x_near[p]])

        @pl.when(core == 0)
        def _():
            x_home[p].start()
            recvx[0, start : start + rows, :] = outb[0, PIECES[p][0] : PIECES[p][0] + rows, :]

    def my_quarter(p):
        rows = PIECES[p][1] // 8
        return pl.ds(pl.multiple_of(PIECES[p][0] + core * (4 * rows) + y * rows, 16), rows)

    def y_copy(p, d):
        start, rows = quarter_of(p)
        there = pl.ds(pl.multiple_of(4 * start + lax.rem(y + d, NY) * rows, 16), rows)
        return remote(yb.at[there], recvy.at[d - 1, pl.ds(start, rows)], y_s.at[p, d - 1], y_r.at[p, d - 1], dev(dy=d))

    def y_start(p):
        start, rows = half_of(p)
        on_core(1, x_copy(0, p, 1, 0, dev(to=1)).wait_recv)
        for slot in (1, 2, 3):
            x_copy(1, p, 0, slot, dev(dx=1)).wait_recv()
        part = recvx[0, start : start + rows, :].astype(F32)
        for slot in (1, 2, 3):
            part = part + recvx[slot, start : start + rows, :].astype(F32)
        yb[start : start + rows, :] = part.astype(BF16)
        tot[pl.ds(pl.multiple_of(PIECES[p][0] + core * rows, 16), rows), :] = part
        for d in (1, 2, 3):
            y_copy(p, d).start()

    def a_copy(p, d):
        at = tot.at[my_quarter(p)]
        return remote(at, at, a_s.at[p, d - 1], a_r.at[p, d - 1], dev(dy=d))

    def a_start(p):
        start, rows = quarter_of(p)
        total = tot[my_quarter(p), :]
        for d in (1, 2, 3):
            y_copy(p, d).wait_recv()
            total = total + recvy[d - 1, start : start + rows, :].astype(F32)
        tot[my_quarter(p), :] = total
        for d in (1, 2, 3):
            a_copy(p, d).start()

    def e_copy(p):
        rows = PIECES[p][1] // 2
        at = tot.at[pl.ds(pl.multiple_of(PIECES[p][0] + core * rows, 16), rows)]
        return remote(at, at, a_s.at[p, 3], a_r.at[p, 3], dev(to=other))

    def e_start(p):
        for d in (1, 2, 3):
            a_copy(p, d).wait_recv()
        e_copy(p).start()

    def piece_out(p):
        at = pl.ds(*PIECES[p])
        return pltpu.make_async_copy(tot.at[at], table_ref.at[at], lsem.at[4 + p])

    def e_finish(p):
        e_copy(p).wait_recv()
        piece_out(p).start()

    passes = (whole(0, 1), whole(2, 3), whole(4) + [(None, 0), (None, 1)])
    midway = ((), ((y_start, 0),), ((y_start, 1), (e_start, 0)))
    loads[2].wait()

    def shard_pass(turn, carry):
        @pl.when(turn == 1)
        def _():
            loads[3].wait()

        for p in range(3):

            def between(p=p):
                @pl.when(turn == 1)
                def _():
                    for action, piece in midway[p]:
                        action(piece)

            sketch(1 - turn, passes[p], between)

            @pl.when(turn == 0)
            def _(p=p):
                x_far_start(p)

            @pl.when(turn == 1)
            def _(p=p):
                x_near_start(p)
                if p > 0:
                    a_start(p - 1)

        return carry

    lax.fori_loop(0, 2, shard_pass, 0)
    e_finish(0)
    y_start(2)
    e_start(1)
    a_start(2)
    e_finish(1)
    e_start(2)
    e_finish(2)

    for p in range(3):
        for copy in x_far[p] + [y_copy(p, d) for d in (1, 2, 3)] + [a_copy(p, d) for d in (1, 2, 3)] + [e_copy(p)]:
            copy.wait_send()
    on_core(0, *[copy.wait_send for copy in x_home])
    on_core(1, *[c.wait_send for p in range(3) for c in x_near[p]])
    for p in range(3):
        piece_out(p).wait()


def run_main(*args):
    anywhere = pl.BlockSpec(memory_space=pl.ANY)
    dma = pltpu.SemaphoreType.DMA
    return pl.pallas_call(
        main_kernel,
        out_shape=(
            jax.ShapeDtypeStruct((2, NB, 256), BF16),
            jax.ShapeDtypeStruct((2, META, 128), I32),
            jax.ShapeDtypeStruct((2, LIVE, 128), I32),
            jax.ShapeDtypeStruct((LIVE, 128), F32),
            jax.ShapeDtypeStruct((LIVE, 128), I32),
            jax.ShapeDtypeStruct((8, LIVE), I32),
        ),
        in_specs=[anywhere] * 7 + [pl.BlockSpec(memory_space=pltpu.SMEM)] + [anywhere] * 2,
        out_specs=(anywhere,) * 6,
        scratch_shapes=[
            pltpu.VMEM((TOK, DW), BF16),
            pltpu.VMEM((TOK, DW), BF16),
            pltpu.VMEM((2, NZ * CHIP, DW), BF16),
            pltpu.VMEM((DW, 2 * COLS), BF16),
            pltpu.VMEM((2 * COLS, DW), BF16),
            pltpu.VMEM((DW, 2 * COLS), F32),
            pltpu.VMEM((2 * COLS, DW), F32),
            pltpu.VMEM((ROWS, NB), I32),
            pltpu.VMEM((ROWS, NB), I32),
            pltpu.VMEM((META, 128), I32),
            pltpu.VMEM((2, META, 128), I32),
            pltpu.VMEM((2, NB, 256), BF16),
            pltpu.VMEM((ROWS, COUNT, 128), F32),
            pltpu.VMEM((ROWS, COUNT, 128), F32),
            pltpu.VMEM((LIVE, 128), F32),
            pltpu.VMEM((LIVE, 128), I32),
            pltpu.VMEM((8, LIVE), I32),
            pltpu.VMEM((2, LIVE, 128), I32),
            pltpu.VMEM((1, 64), I32),
            dma((23,)), dma((2,)),
            dma((2, 4, 2)), dma((2, 4, 2)), dma((NZ, 2)), dma((NZ, 2)), dma((4,)), dma((4,)),
            dma((7,)), dma((7,)), dma((2,)), dma((2,)),
        ],
        compiler_params=pltpu.CompilerParams(
            collective_id=0, has_side_effects=True, vmem_limit_bytes=62 * 1024 * 1024
        ),
        cost_estimate=pl.CostEstimate(flops=15_000_000_000, bytes_accessed=20_000_000, transcendentals=2_000_000),
        name="gather_grad",
    )(*args)


def run_sketch(ghl, codes, spots):
    anywhere = pl.BlockSpec(memory_space=pl.ANY)
    dma = pltpu.SemaphoreType.DMA
    return pl.pallas_call(
        sketch_kernel,
        out_shape=jax.ShapeDtypeStruct((TAB, 128), F32),
        in_specs=[anywhere] * 3,
        out_specs=anywhere,
        scratch_shapes=[
            pltpu.VMEM((2, NB, 256), BF16),
            pltpu.VMEM((2, META, 128), I32),
            pltpu.VMEM((2, LIVE, 128), I32),
            pltpu.VMEM((2, TAB, 128), BF16),
            pltpu.VMEM((4, TAB // 2, 128), BF16),
            pltpu.VMEM((TAB // 2, 128), BF16),
            pltpu.VMEM((3, TAB // 8, 128), BF16),
            pltpu.VMEM((TAB, 128), F32),
            dma((7,)), dma((2, 3, 2)), dma((4, 3)), dma((3, 3)), dma((3, 3)), dma((3, 4)), dma((3, 4)),
        ],
        compiler_params=pltpu.CompilerParams(
            collective_id=1, has_side_effects=True, vmem_limit_bytes=62 * 1024 * 1024
        ),
        cost_estimate=pl.CostEstimate(flops=24_000_000_000, bytes_accessed=10_000_000, transcendentals=0),
        name="sketch_reduce",
    )(ghl, codes, spots)


def finish_kernel(
    table, med, info, across, mom, err, w_in, w_out,
    win_new, wout_new, mom_new, err_new,
    tabv, medv, infov, acrossv, momv, errv, winv, woutv, winn, woutn, momn, errn, sem, out_sem,
):
    pairs = [(info, infov), (med, medv), (table, tabv), (across, acrossv), (w_in, winv), (w_out, woutv)]
    for j in range(ROWS):
        pairs += [(mom.at[:, j, :], momv.at[j]), (err.at[:, j, :], errv.at[j])]
    loads = [pltpu.make_async_copy(src, dst, sem.at[n]) for n, (src, dst) in enumerate(pairs)]
    for load in loads:
        load.start()
    stores = []

    def store(src, dst):
        stores.append(pltpu.make_async_copy(src, dst, out_sem.at[len(stores)]))
        stores[-1].start()

    for load in loads[:4]:
        load.wait()
    codes = infov[...]
    update = medv[...] + LEARN * tabv[LISTED:, :]
    kept = split2(jnp.where(codes[:, ROWS : ROWS + 1] == 1, update, 0.0))
    places = acrossv[0:1, :]

    def delta(start, rows):
        hit = jnp.where(iota((rows, LIVE), 0) + start == places, 1.0, 0.0).astype(BF16)
        got = nn(hit, kept)
        return got[:, :128] + got[:, 128:]

    loads[4].wait()
    for c in range(4):
        rows = pl.ds(c * 512, 512)
        for h in range(2):
            at = slice(h * 128, (h + 1) * 128)
            winn[rows, at] = winv[rows, at].astype(F32) - delta(h * 2048 + c * 512, 512)
        store(winn.at[rows], win_new.at[rows])
    loads[5].wait()
    for c in range(4):
        for q in range(4 * c, 4 * c + 4):
            at = slice(q * 128, (q + 1) * 128)
            woutn[:, at] = woutv[:, at].astype(F32) - delta(4096 + q * 256, 256)
        at = pl.ds(c * 512, 512)
        store(woutn.at[:, at], wout_new.at[:, at])
    for j in range(ROWS):
        loads[6 + 2 * j].wait()
        loads[7 + 2 * j].wait()
        fresh = DECAY * momv[j] + tabv[j * COUNT : (j + 1) * COUNT, :]
        momn[j] = fresh
        store(momn.at[j], mom_new.at[:, j, :])
        gone = tn(signed_hit(codes[:, j : j + 1]), kept)
        errn[j] = errv[j] + LEARN * fresh - (gone[:, :128] + gone[:, 128:])
        store(errn.at[j], err_new.at[:, j, :])
    for copy in stores:
        copy.wait()


def run_finish(table, med, info, across, mom, err, w_in, w_out):
    anywhere = pl.BlockSpec(memory_space=pl.ANY)
    vmem = pltpu.VMEM
    deep = vmem((ROWS, COUNT, 128), F32)
    return pl.pallas_call(
        finish_kernel,
        out_shape=(
            jax.ShapeDtypeStruct(w_in.shape, F32),
            jax.ShapeDtypeStruct(w_out.shape, F32),
            jax.ShapeDtypeStruct(mom.shape, F32),
            jax.ShapeDtypeStruct(err.shape, F32),
        ),
        in_specs=[anywhere] * 8,
        out_specs=(anywhere,) * 4,
        scratch_shapes=[
            vmem((TAB, 128), F32), vmem((LIVE, 128), F32), vmem((LIVE, 128), I32), vmem((8, LIVE), I32),
            deep, deep, vmem(w_in.shape, BF16), vmem(w_out.shape, BF16), vmem(w_in.shape, F32), vmem(w_out.shape, F32),
            deep, deep, pltpu.SemaphoreType.DMA((16,)), pltpu.SemaphoreType.DMA((18,)),
        ],
        compiler_params=pltpu.CompilerParams(vmem_limit_bytes=62 * 1024 * 1024),
        cost_estimate=pl.CostEstimate(flops=3_000_000_000, bytes_accessed=16_000_000, transcendentals=0),
        name="finish",
    )(table, med, info, across, mom, err, w_in, w_out)


def per_device(
    tokens, cotangent, w_in, w_out, momentum, error, block_order, signs, heavy_blocks, heavy_count
):
    mom, err = by_bucket(momentum), by_bucket(error)
    ghl, codes, spots, med, info, across = run_main(
        tokens, cotangent, w_in, w_out, block_order, signs, heavy_blocks, heavy_count, mom, err
    )
    table = run_sketch(ghl, codes, spots)
    win_new, wout_new, mom_new, err_new = run_finish(table, med, info, across, mom, err, w_in, w_out)
    return win_new, wout_new, by_row(mom_new), by_row(err_new)


def by_bucket(table):
    return jnp.transpose(table.reshape(ROWS, COUNT, 128), (1, 0, 2))


def by_row(table):
    return jnp.transpose(table, (1, 0, 2)).reshape(ROWS, COUNT * 128)


def solution(mesh):
    placed = (
        P(("rep", "shard"), None),
        P(("rep", "shard"), None),
        P(None, "shard"),
        P("shard", None),
        P(None, "shard"),
        P(None, "shard"),
        P(None, "shard"),
        P(None, "shard"),
        P("rep", "shard"),
        P("rep", "shard"),
    )
    return jax.shard_map(
        per_device,
        mesh=mesh,
        in_specs=placed,
        out_specs=(P(None, "shard"), P("shard", None), P(None, "shard"), P(None, "shard")),
        check_vma=False,
    )
```

```python
import functools

import jax
import jax.numpy as jnp
from jax import lax
from jax.experimental import pallas as pl
from jax.experimental.pallas import tpu as pltpu
from jax.sharding import PartitionSpec as P

MESH = pl.DeviceIdType.MESH
F32, BF16, I32 = jnp.float32, jnp.bfloat16, jnp.int32
LEARN = 0.05
DECAY = 0.9
ROOT = 0.7978845608028654

NX, NY, NZ = 4, 4, 8
TOK = 104
CHIP = 2 * TOK
SUBS = ((0, 112), (112, 96))
DW, COLS = 2048, 256
NB = 8192
COUNT = 512
ROWS = 5
LIVE = 256
LISTED = ROWS * COUNT
TAB = LISTED + LIVE
PIECES = ((0, 1024), (1024, 1024), (2048, 768))
CODE = ROWS * 64
META = CODE + 64


def nt(a, b):
    return lax.dot_general(a, b, (((1,), (1,)), ((), ())), preferred_element_type=F32)


def tn(a, b):
    return lax.dot_general(a, b, (((0,), (0,)), ((), ())), preferred_element_type=F32)


def nn(a, b):
    return jnp.dot(a, b, preferred_element_type=F32)


def iota(shape, dim):
    return lax.broadcasted_iota(I32, shape, dim)


def split2(x):
    hi = x.astype(BF16)
    return jnp.concatenate([hi, (x - hi.astype(F32)).astype(BF16)], axis=1)


def place_of(block):
    rest = block - 4096
    return jnp.where(
        block < 4096, (block & 1) * 2048 + (block >> 1), 4096 + (rest & 15) * 256 + (rest >> 4)
    )


def gelu_pair(pre):
    tangent = jnp.tanh(ROOT * (pre + 0.044715 * pre * pre * pre))
    value = 0.5 * pre * (1.0 + tangent)
    slope = 0.5 * (1.0 + tangent) + 0.5 * pre * (1.0 - tangent * tangent) * ROOT * (
        1.0 + 0.134145 * pre * pre
    )
    return value, slope


def invert(ord_ref, sgn_ref, meta_ref):
    step = 1024
    for j in range(ROWS):

        def body(c, acc, j=j):
            at = pl.ds(pl.multiple_of(c * step, step), step)
            place = place_of(ord_ref[j : j + 1, at])
            sign = sgn_ref[j : j + 1, at]
            bucket = (c * step + iota((1, step), 1)) >> 4
            row = iota((128, step), 0)
            value = jnp.where(row < 64, bucket >> 1, (bucket & 1) * 2 + sign)
            left = jnp.where((row & 63) == (place >> 7), value, 0).astype(F32).astype(BF16)
            right = jnp.where(row == (place & 127), 1.0, 0.0).astype(BF16)
            return acc + nt(left, right)

        acc = lax.fori_loop(0, NB // step, body, jnp.zeros((128, 128), F32))
        meta_ref[j * 64 : (j + 1) * 64, :] = (acc[:64] * 4.0 + acc[64:]).astype(I32)


def compact(lists, along):
    full = jnp.concatenate([lists, jnp.zeros((120, 128), I32)], axis=0)
    shape = (LIVE, 128)
    slot, lane = iota(shape, 0), iota(shape, 1)
    wanted = jnp.where(slot < 128, slot & 15, jnp.where(slot < 176, slot - 112, 127))
    pick = jnp.where(lane == wanted, 1.0, 0.0).astype(BF16)
    pick_count = jnp.where(lane == 64, 1.0, 0.0).astype(BF16)
    high = (full >> 7).astype(F32).astype(BF16)
    low = (full & 127).astype(F32).astype(BF16)
    if along == 0:
        values = nt(pick, high) * 128.0 + nt(pick, low)
        counts = nt(pick_count, low)
        spot, rep, axis = slot, lane, 1
    else:
        values = nt(high, pick) * 128.0 + nt(low, pick)
        counts = nt(low, pick_count)
        spot, rep, axis = iota((128, LIVE), 1), iota((128, LIVE), 0), 0
    first = (spot < 128) & (rep == (spot >> 4)) & (counts > (spot & 15).astype(F32))
    later = (spot >= 128) & (spot < 176) & (rep < 8) & (counts > 63.5)
    hit = jnp.where(first | later, 1.0, 0.0)
    live = jnp.sum(hit, axis=axis, keepdims=True)
    block = jnp.sum(hit * values, axis=axis, keepdims=True).astype(I32)
    return jnp.where(live > 0.5, place_of(block), -1)


def lists_of(meta_ref, *lead):
    total = jnp.zeros((8, 128), I32)
    for r in range(8):
        total = total + meta_ref[(*lead, slice(CODE + 8 * r, CODE + 8 * r + 8), slice(None))]
    return total


def middle_value(values):
    values = list(values)
    total = len(values)
    for rounds in range(total):
        for i in range(rounds % 2, total - 1, 2):
            lower = jnp.minimum(values[i], values[i + 1])
            upper = jnp.maximum(values[i], values[i + 1])
            values[i] = lower
            values[i + 1] = upper
    return values[total // 2]


def prepare(meta, momv, errv, medv, infov, acrossv):
    lists = lists_of(meta)
    down, across = compact(lists, 0), compact(lists, 1)
    shape = (LIVE, LIVE)
    same = (down == across) & (across >= 0) & (iota(shape, 1) < iota(shape, 0))
    earlier = jnp.max(jnp.where(same, 1.0, 0.0), axis=1, keepdims=True)
    keep = jnp.where((down >= 0) & (earlier < 0.5), 1, 0)
    codes = meta[...]
    high = (codes >> 2).astype(F32).astype(BF16)
    low = (codes & 3).astype(F32).astype(BF16)
    lane = iota((LIVE, 128), 1)
    lane_hit = lane == (down & 127)
    info = jnp.where(lane == ROWS, keep, 0)
    found = []
    for j in range(ROWS):
        pick = jnp.where(iota((LIVE, META), 1) == (down >> 7) + j * 64, 1.0, 0.0)
        pick = jnp.where(down >= 0, pick, 0.0).astype(BF16)
        value = nn(pick, high) * 4.0 + nn(pick, low)
        code = jnp.sum(jnp.where(lane_hit, value, 0.0), axis=1, keepdims=True).astype(I32)
        info = jnp.where(lane == j, code, info)
        probe = errv[j] + LEARN * DECAY * momv[j]
        got = nn(signed_hit(code), split2(probe))
        found.append(got[:, :128] + got[:, 128:])
    medv[...] = middle_value(found)
    infov[...] = info
    acrossv[...] = jnp.broadcast_to(across, acrossv.shape)


def signed_hit(code):
    sign = jnp.where((code & 1) == 1, 1.0, -1.0)
    return jnp.where(iota((LIVE, COUNT), 1) == (code >> 1), sign, 0.0).astype(BF16)


def main_kernel(
    tok_ref, cot_ref, win_ref, wout_ref, ord_ref, sgn_ref, lst_ref, cnt_ref, mom_ref, err_ref,
    ghl_ref, codes_ref, spots_ref, med_ref, info_ref, across_ref,
    own, land, buf, wi, wo, gin, gout, ordv, sgnv, meta, meta2, ghl,
    momv, errv, medv, infov, acrossv, spots, lstv,
    lsem, land_sem, ring_s, ring_r, sib_s, sib_r, w_s, w_r, list_s, list_r, meta_s, meta_r,
):
    rep, shard = lax.axis_index("rep"), lax.axis_index("shard")
    y, core = rep // 2, rep % 2
    x, z = shard // NZ, shard % NZ
    other = 1 - core

    def dev(dx=0, dy=0, dz=0, to=None):
        c = core if to is None else to
        return {
            "rep": lax.rem(y + dy + NY, NY) * 2 + c,
            "shard": lax.rem(x + dx + NX, NX) * NZ + lax.rem(z + dz + NZ, NZ),
        }

    def remote(src, dst, send, recv, device):
        return pltpu.make_async_remote_copy(
            src_ref=src, dst_ref=dst, send_sem=send, recv_sem=recv, device_id=device, device_id_type=MESH
        )

    def on_core(c, *actions):
        @pl.when(core == c)
        def _():
            for action in actions:
                action()

    own_tok = pltpu.make_async_copy(tok_ref, own, lsem.at[0])
    own_cot = pltpu.make_async_copy(cot_ref, own, lsem.at[0])
    loads = [
        pltpu.make_async_copy(lst_ref, lstv, lsem.at[1]),
        pltpu.make_async_copy(ord_ref, ordv, lsem.at[2]),
        pltpu.make_async_copy(sgn_ref, sgnv, lsem.at[3]),
    ]
    tables = [pltpu.make_async_copy(mom_ref.at[:, j, :], momv.at[j], lsem.at[6 + j]) for j in range(ROWS)]
    tables += [pltpu.make_async_copy(err_ref.at[:, j, :], errv.at[j], lsem.at[11 + j]) for j in range(ROWS)]
    own_wi = pltpu.make_async_copy(win_ref, wi.at[:, pl.ds(0, COLS)], lsem.at[4])
    own_wo = pltpu.make_async_copy(wout_ref, wo.at[pl.ds(0, COLS)], lsem.at[5])
    on_core(0, own_tok.start)
    on_core(1, own_cot.start)
    for load in loads:
        load.start()

    barrier = pltpu.get_barrier_semaphore()
    partners = [dev(dz=1), dev(dz=-1)]
    partners += [dev(dx=d, to=c) for d in (1, -1, 2) for c in (0, 1)]
    partners += [dev(dy=d, to=c) for d in (1, 2, 3) for c in (0, 1)] + [dev(to=other)]
    for partner in partners:
        pl.semaphore_signal(barrier, inc=1, device_id=partner, device_id_type=MESH)
    pl.semaphore_wait(barrier, len(partners))

    give_cot = remote(cot_ref, land, land_sem.at[0], land_sem.at[1], dev(to=other))
    give_tok = remote(tok_ref, land, land_sem.at[0], land_sem.at[1], dev(to=other))
    on_core(0, give_cot.start)
    on_core(1, give_tok.start)

    toward = jnp.where(core == 0, -1, 1)
    lower, upper = pl.ds(0, COLS), pl.ds(COLS, COLS)
    landing = pl.ds(pl.multiple_of(other * COLS, COLS), COLS)
    w_in_first = remote(win_ref, wi.at[:, landing], w_s.at[0], w_r.at[0], dev(dx=toward))
    w_out_first = remote(wout_ref, wo.at[landing], w_s.at[1], w_r.at[1], dev(dx=toward))
    w_in_next = remote(wi.at[:, upper], wi.at[:, upper], w_s.at[2], w_r.at[2], dev(dx=-1, to=1))
    w_out_next = remote(wo.at[lower], wo.at[upper], w_s.at[3], w_r.at[3], dev(dx=1, to=1))
    on_core(0, w_in_first.start, w_out_first.start, own_wi.start, own_wo.start)
    on_core(1, w_out_first.start, w_in_first.start)

    loads[0].wait()
    listed = jnp.concatenate([lstv[...], jnp.full(lstv.shape, cnt_ref[0, 0], I32)], axis=1)
    meta[pl.ds(pl.multiple_of(CODE + 8 * rep, 8), 8), :] = jnp.where(iota((8, 128), 0) == rep, listed, 0)
    list_row = meta.at[pl.ds(pl.multiple_of(CODE + 8 * rep, 8), 8)]
    peers = [(0, 1), (1, 0), (1, 1), (2, 0), (2, 1), (3, 0), (3, 1)]
    peers = [(n, dev(dy=d, to=other if flip else core)) for n, (d, flip) in enumerate(peers)]
    list_copies = [remote(list_row, list_row, list_s.at[n], list_r.at[n], peer) for n, peer in peers]
    for copy in list_copies:
        copy.start()

    on_core(0, own_tok.wait, give_cot.wait)
    on_core(1, own_cot.wait, give_tok.wait)
    for c in range(4):
        at = slice(c * 512, (c + 1) * 512)
        mine, theirs = own[:, at].astype(F32), land[:, at].astype(F32)
        first, second = jnp.where(core == 0, mine, theirs), jnp.where(core == 0, theirs, mine)
        buf[core, 0:CHIP, at] = jnp.concatenate([first, second], axis=0).astype(BF16)

    def turn_of(way, sub):
        return sub if way == 0 else 1 - sub

    def unit_of(hops, turn):
        return 0 if hops == 0 else 2 * hops - 1 + turn

    def rows_of(unit, sub):
        return pl.ds(unit * CHIP + SUBS[sub][0], SUBS[sub][1])

    def ring(way, hops, sub):
        turn = turn_of(way, sub)
        return remote(
            buf.at[core, rows_of(unit_of(hops, turn), sub)],
            buf.at[core, rows_of(unit_of(hops + 1, turn), sub)],
            ring_s.at[way, hops, sub], ring_r.at[way, hops, sub],
            dev(dz=1 if way == 0 else -1),
        )

    def sibling(unit, sub):
        at = buf.at[core, rows_of(unit, sub)]
        return remote(at, at, sib_s.at[unit, sub], sib_r.at[unit, sub], dev(to=other))

    for turn in (0, 1):
        ring(0, 0, turn).start()
        ring(1, 0, 1 - turn).start()
    for sub in (0, 1):
        sibling(0, sub).start()
    for load in tables:
        load.start()

    def arrive(hops, turn):
        for way in (0, 1):
            sub = turn if way == 0 else 1 - turn
            ring(way, hops - 1, sub).wait_recv()
            if hops < 3 or (hops == 3 and turn == 0):
                ring(way, hops, sub).start()
            sibling(unit_of(hops, turn), sub).start()

    loads[1].wait()
    loads[2].wait()
    invert(ordv, sgnv, meta)
    for copy in list_copies:
        copy.wait_recv()
    meta_first = remote(meta, meta2.at[other], meta_s.at[0], meta_r.at[0], dev(dx=toward))
    meta_next = remote(meta, meta2.at[1], meta_s.at[1], meta_r.at[1], dev(dx=2))
    meta_first.start()
    on_core(1, meta_next.start)

    @pl.when(core == 0)
    def _():
        meta2[0] = meta[...]

    gin[...] = jnp.zeros_like(gin)
    gout[...] = jnp.zeros_like(gout)

    arrive(1, 0)
    on_core(0, w_in_first.wait_recv, w_in_next.start)
    on_core(1, w_out_first.wait_recv, w_out_next.start)
    arrive(1, 1)
    for load in tables:
        load.wait()
    prepare(meta, momv, errv, medv, infov, acrossv)
    ready = [
        pltpu.make_async_copy(medv, med_ref, lsem.at[16]),
        pltpu.make_async_copy(infov, info_ref, lsem.at[17]),
        pltpu.make_async_copy(acrossv, across_ref, lsem.at[18]),
    ]
    for copy in ready:
        copy.start()
    meta_first.wait_recv()
    on_core(1, meta_next.wait_recv)
    for k in (0, 1):
        spots[k] = jnp.broadcast_to(compact(lists_of(meta2, k), 0), (LIVE, 128))
    ready += [
        pltpu.make_async_copy(meta2, codes_ref, lsem.at[21]),
        pltpu.make_async_copy(spots, spots_ref, lsem.at[22]),
    ]
    for copy in ready[3:]:
        copy.start()
    arrive(2, 0)
    on_core(0, w_out_first.wait_recv, own_wi.wait, own_wo.wait)
    on_core(1, w_in_first.wait_recv, w_in_next.wait_recv, w_out_next.wait_recv)

    def wait_sibling(*units):
        for unit in units:
            for sub in (0, 1):
                sibling(unit, sub).wait_recv()

    out_first = pltpu.make_async_copy(ghl.at[:, pl.ds(0, 4096)], ghl_ref.at[:, pl.ds(0, 4096)], lsem.at[19])
    out_last = pltpu.make_async_copy(ghl.at[:, pl.ds(4096, 4096)], ghl_ref.at[:, pl.ds(4096, 4096)], lsem.at[20])
    ready += [out_first, out_last]

    def work(start, count, last=False):
        rows = pl.ds(start, count)
        value, slope = gelu_pair(nn(buf[0, rows, :], wi[...]))
        back = nt(buf[1, rows, :], wo[...])
        hidden = value.astype(BF16)
        grad = (back * slope).astype(BF16)
        for c in range(4):
            at = slice(c * 512, (c + 1) * 512)
            total = gin[at, :] + tn(buf[0, rows, at], grad)
            if not last:
                gin[at, :] = total
                continue
            for k in range(2):
                for h in range(2):
                    part = total[:, k * COLS + h * 128 : k * COLS + (h + 1) * 128]
                    ghl[k, h * 2048 + c * 512 : h * 2048 + (c + 1) * 512, :] = split2(part)
        if last:
            out_first.start()
        for c in range(4):
            at = slice(c * 512, (c + 1) * 512)
            total = gout[:, at] + tn(hidden, buf[1, rows, at])
            if not last:
                gout[:, at] = total
                continue
            for k in range(2):
                for q in range(4 * c, 4 * c + 4):
                    part = total[k * COLS : (k + 1) * COLS, (q - 4 * c) * 128 : (q - 4 * c + 1) * 128]
                    ghl[k, 4096 + q * 256 : 4352 + q * 256, :] = split2(part)

    def work_pair(i, carry):
        @pl.when(i == 0)
        def _():
            wait_sibling(0, 1)

        @pl.when(i == 1)
        def _():
            wait_sibling(2, 3)

        @pl.when(i == 2)
        def _():
            arrive(2, 1)
            arrive(3, 0)
            wait_sibling(4, 5)

        work(pl.multiple_of(i * (2 * CHIP), 16), 2 * CHIP)
        return carry

    lax.fori_loop(0, 3, work_pair, 0)
    arrive(3, 1)
    wait_sibling(6)
    work(6 * CHIP, CHIP)
    ring(0, 3, 0).wait_recv()
    sibling(7, 0).start()
    ring(1, 3, 1).wait_recv()
    sibling(7, 1).start()
    wait_sibling(7)
    work(7 * CHIP, CHIP, last=True)
    out_last.start()

    for copy in list_copies + [w_in_first, w_out_first, meta_first]:
        copy.wait_send()
    for way in (0, 1):
        for hops in range(4):
            for sub in (0, 1):
                if hops < 3 or sub == way:
                    ring(way, hops, sub).wait_send()
    for unit in range(NZ):
        for sub in (0, 1):
            sibling(unit, sub).wait_send()
    on_core(0, w_in_next.wait_send)
    on_core(1, w_out_next.wait_send, meta_next.wait_send)
    for copy in ready:
        copy.wait()


def sketch_kernel(
    ghl_ref, codes_ref, spots_ref, table_ref,
    ghl, codes, spots, outb, recvx, yb, recvy, tot, lsem, x_s, x_r, y_s, y_r, a_s, a_r,
):
    rep, shard = lax.axis_index("rep"), lax.axis_index("shard")
    y, core = rep // 2, rep % 2
    x, z = shard // NZ, shard % NZ
    other = 1 - core

    def dev(dx=0, dy=0, dz=0, to=None):
        c = core if to is None else to
        return {
            "rep": lax.rem(y + dy + NY, NY) * 2 + c,
            "shard": lax.rem(x + dx + NX, NX) * NZ + lax.rem(z + dz + NZ, NZ),
        }

    def remote(src, dst, send, recv, device):
        return pltpu.make_async_remote_copy(
            src_ref=src, dst_ref=dst, send_sem=send, recv_sem=recv, device_id=device, device_id_type=MESH
        )

    def on_core(c, *actions):
        @pl.when(core == c)
        def _():
            for action in actions:
                action()

    loads = [
        pltpu.make_async_copy(codes_ref, codes, lsem.at[0]),
        pltpu.make_async_copy(spots_ref, spots, lsem.at[1]),
        pltpu.make_async_copy(ghl_ref.at[1], ghl.at[1], lsem.at[2]),
        pltpu.make_async_copy(ghl_ref.at[0], ghl.at[0], lsem.at[3]),
    ]
    for load in loads:
        load.start()
    barrier = pltpu.get_barrier_semaphore()
    partners = [dev(dx=d, to=c) for d in (1, -1, 2) for c in (0, 1)]
    partners += [dev(dy=d) for d in (1, 2, 3)] + [dev(to=other)]
    for partner in partners:
        pl.semaphore_signal(barrier, inc=1, device_id=partner, device_id_type=MESH)
    pl.semaphore_wait(barrier, len(partners))
    loads[0].wait()
    loads[1].wait()

    def spread(code):
        code = jnp.broadcast_to(code, (16, 128))
        bucket = (code >> 1).astype(F32)
        return jnp.where((code & 1) == 1, 1.0, -1.0).astype(BF16), [(bucket - 256.0 * h).astype(BF16) for h in (0, 1)]

    def one_hot(spread_code, quarter):
        sign, spot = spread_code[0], spread_code[1][quarter // 2]
        ramp = iota((256, 128), 0).astype(F32).astype(BF16)
        first = 8 * (quarter % 2)
        hits = [spot == ramp[g * 16 : (g + 1) * 16] for g in range(first, first + 8)]
        return jnp.concatenate([jnp.where(hit, sign, jnp.zeros_like(sign)) for hit in hits], axis=0)

    def sketch(k, work):
        step = 4
        per = NB // 512
        used = sorted({j for j, _ in work if j is not None})

        def run(*sums):
            def chunk(t, carry):
                first = [unit * per + t * step for unit in (0, 1)]

                def tile(unit, i):
                    return ghl[k, pl.ds(pl.multiple_of((first[unit] + i) * 256, 256), 256), :]

                found = [
                    {j: codes[k, pl.ds(pl.multiple_of(j * 64 + 2 * first[unit], 8), 2 * step), :] for j in used}
                    for unit in (0, 1)
                ]
                for unit in (0, 1):
                    pltpu.matmul_push_rhs(tile(unit, 0), 0, unit)
                for i in range(step):
                    if i + 1 < step:
                        for unit in (0, 1):
                            pltpu.matmul_push_rhs(tile(unit, i + 1), (i + 1) % 2, unit)
                    rows = [
                        {j: [spread(found[unit][j][2 * i + n : 2 * i + n + 1, :]) for n in (0, 1)] for j in used}
                        for unit in (0, 1)
                    ]
                    for c, (j, q) in enumerate(work):
                        for unit in (0, 1):
                            if j is None:
                                spot = spots[k, q * 128 : (q + 1) * 128, :] - (first[unit] + i) * 256
                                lane = iota((128, 128), 1)
                                hot = [jnp.where(spot == lane + 128 * n, 1.0, 0.0).astype(BF16) for n in (0, 1)]
                            else:
                                hot = [one_hot(rows[unit][j][n], q) for n in (0, 1)]
                            pltpu.matmul_acc_lhs(
                                sums[2 * c + unit],
                                jnp.concatenate(hot, axis=1),
                                load_staged_rhs=i % 2 if c == 0 else None,
                            )
                return carry

            lax.fori_loop(0, per // step, chunk, 0)
            for c, (j, q) in enumerate(work):
                total = pltpu.matmul_pop(sums[2 * c]) + pltpu.matmul_pop(sums[2 * c + 1])
                start = q * 128 + (LISTED if j is None else j * COUNT)
                outb[k, start : start + 128, :] = (total[:, :128] + total[:, 128:]).astype(BF16)

        pl.run_scoped(run, *[pltpu.ACC(mxu_id=unit)((128, 256), F32) for _ in work for unit in (0, 1)])

    def whole(*rows):
        return [(j, q) for j in rows for q in range(4)]

    def half_of(p):
        return PIECES[p][0] // 2, PIECES[p][1] // 2

    def quarter_of(p):
        return PIECES[p][0] // 8, PIECES[p][1] // 8

    def x_copy(k, p, h, slot, device):
        start, rows = half_of(p)
        return remote(
            outb.at[k, pl.ds(PIECES[p][0] + h * rows, rows)], recvx.at[slot, pl.ds(start, rows)],
            x_s.at[k, p, h], x_r.at[slot, p], device,
        )

    x_far = [[x_copy(1, p, h, 1 + 2 * core, dev(dx=1 + core, to=h)) for h in (0, 1)] for p in range(3)]
    x_near = [[x_copy(0, p, h, 2, dev(dx=-1, to=h)) for h in (0, 1)] for p in range(3)]
    x_home = [x_copy(0, p, 1, 0, dev(to=1)) for p in range(3)]

    def x_far_start(p):
        for copy in x_far[p]:
            copy.start()

    def x_near_start(p):
        start, rows = half_of(p)
        on_core(1, *[copy.start for copy in x_near[p]])

        @pl.when(core == 0)
        def _():
            x_home[p].start()
            recvx[0, start : start + rows, :] = outb[0, PIECES[p][0] : PIECES[p][0] + rows, :]

    def my_quarter(p):
        rows = PIECES[p][1] // 8
        return pl.ds(pl.multiple_of(PIECES[p][0] + core * (4 * rows) + y * rows, 16), rows)

    def y_copy(p, d):
        start, rows = quarter_of(p)
        there = pl.ds(pl.multiple_of(4 * start + lax.rem(y + d, NY) * rows, 16), rows)
        return remote(yb.at[there], recvy.at[d - 1, pl.ds(start, rows)], y_s.at[p, d - 1], y_r.at[p, d - 1], dev(dy=d))

    def y_start(p):
        start, rows = half_of(p)
        on_core(1, x_copy(0, p, 1, 0, dev(to=1)).wait_recv)
        for slot in (1, 2, 3):
            x_copy(1, p, 0, slot, dev(dx=1)).wait_recv()
        part = recvx[0, start : start + rows, :].astype(F32)
        for slot in (1, 2, 3):
            part = part + recvx[slot, start : start + rows, :].astype(F32)
        yb[start : start + rows, :] = part.astype(BF16)
        tot[pl.ds(pl.multiple_of(PIECES[p][0] + core * rows, 16), rows), :] = part
        for d in (1, 2, 3):
            y_copy(p, d).start()

    def a_copy(p, d):
        at = tot.at[my_quarter(p)]
        return remote(at, at, a_s.at[p, d - 1], a_r.at[p, d - 1], dev(dy=d))

    def a_start(p):
        start, rows = quarter_of(p)
        total = tot[my_quarter(p), :]
        for d in (1, 2, 3):
            y_copy(p, d).wait_recv()
            total = total + recvy[d - 1, start : start + rows, :].astype(F32)
        tot[my_quarter(p), :] = total
        for d in (1, 2, 3):
            a_copy(p, d).start()

    def e_copy(p):
        rows = PIECES[p][1] // 2
        at = tot.at[pl.ds(pl.multiple_of(PIECES[p][0] + core * rows, 16), rows)]
        return remote(at, at, a_s.at[p, 3], a_r.at[p, 3], dev(to=other))

    def e_start(p):
        for d in (1, 2, 3):
            a_copy(p, d).wait_recv()
        e_copy(p).start()

    def piece_out(p):
        at = pl.ds(*PIECES[p])
        return pltpu.make_async_copy(tot.at[at], table_ref.at[at], lsem.at[4 + p])

    def e_finish(p):
        e_copy(p).wait_recv()
        piece_out(p).start()

    passes = (whole(0, 1), whole(2, 3), whole(4) + [(None, 0), (None, 1)])
    loads[2].wait()
    sketch(1, passes[0])
    x_far_start(0)
    loads[3].wait()
    sketch(0, passes[0])
    x_near_start(0)
    sketch(1, passes[1])
    x_far_start(1)
    y_start(0)
    sketch(0, passes[1])
    x_near_start(1)
    a_start(0)
    sketch(1, passes[2])
    x_far_start(2)
    y_start(1)
    e_start(0)
    sketch(0, passes[2])
    x_near_start(2)
    a_start(1)
    e_finish(0)
    y_start(2)
    e_start(1)
    a_start(2)
    e_finish(1)
    e_start(2)
    e_finish(2)

    for p in range(3):
        for copy in x_far[p] + [y_copy(p, d) for d in (1, 2, 3)] + [a_copy(p, d) for d in (1, 2, 3)] + [e_copy(p)]:
            copy.wait_send()
    on_core(0, *[copy.wait_send for copy in x_home])
    on_core(1, *[c.wait_send for p in range(3) for c in x_near[p]])
    for p in range(3):
        piece_out(p).wait()


def run_main(*args):
    anywhere = pl.BlockSpec(memory_space=pl.ANY)
    dma = pltpu.SemaphoreType.DMA
    return pl.pallas_call(
        main_kernel,
        out_shape=(
            jax.ShapeDtypeStruct((2, NB, 256), BF16),
            jax.ShapeDtypeStruct((2, META, 128), I32),
            jax.ShapeDtypeStruct((2, LIVE, 128), I32),
            jax.ShapeDtypeStruct((LIVE, 128), F32),
            jax.ShapeDtypeStruct((LIVE, 128), I32),
            jax.ShapeDtypeStruct((8, LIVE), I32),
        ),
        in_specs=[anywhere] * 7 + [pl.BlockSpec(memory_space=pltpu.SMEM)] + [anywhere] * 2,
        out_specs=(anywhere,) * 6,
        scratch_shapes=[
            pltpu.VMEM((TOK, DW), BF16),
            pltpu.VMEM((TOK, DW), BF16),
            pltpu.VMEM((2, NZ * CHIP, DW), BF16),
            pltpu.VMEM((DW, 2 * COLS), BF16),
            pltpu.VMEM((2 * COLS, DW), BF16),
            pltpu.VMEM((DW, 2 * COLS), F32),
            pltpu.VMEM((2 * COLS, DW), F32),
            pltpu.VMEM((ROWS, NB), I32),
            pltpu.VMEM((ROWS, NB), I32),
            pltpu.VMEM((META, 128), I32),
            pltpu.VMEM((2, META, 128), I32),
            pltpu.VMEM((2, NB, 256), BF16),
            pltpu.VMEM((ROWS, COUNT, 128), F32),
            pltpu.VMEM((ROWS, COUNT, 128), F32),
            pltpu.VMEM((LIVE, 128), F32),
            pltpu.VMEM((LIVE, 128), I32),
            pltpu.VMEM((8, LIVE), I32),
            pltpu.VMEM((2, LIVE, 128), I32),
            pltpu.VMEM((1, 64), I32),
            dma((23,)), dma((2,)),
            dma((2, 4, 2)), dma((2, 4, 2)), dma((NZ, 2)), dma((NZ, 2)), dma((4,)), dma((4,)),
            dma((7,)), dma((7,)), dma((2,)), dma((2,)),
        ],
        compiler_params=pltpu.CompilerParams(
            collective_id=0, has_side_effects=True, vmem_limit_bytes=62 * 1024 * 1024
        ),
        cost_estimate=pl.CostEstimate(flops=15_000_000_000, bytes_accessed=20_000_000, transcendentals=2_000_000),
        name="gather_grad",
    )(*args)


def run_sketch(ghl, codes, spots):
    anywhere = pl.BlockSpec(memory_space=pl.ANY)
    dma = pltpu.SemaphoreType.DMA
    return pl.pallas_call(
        sketch_kernel,
        out_shape=jax.ShapeDtypeStruct((TAB, 128), F32),
        in_specs=[anywhere] * 3,
        out_specs=anywhere,
        scratch_shapes=[
            pltpu.VMEM((2, NB, 256), BF16),
            pltpu.VMEM((2, META, 128), I32),
            pltpu.VMEM((2, LIVE, 128), I32),
            pltpu.VMEM((2, TAB, 128), BF16),
            pltpu.VMEM((4, TAB // 2, 128), BF16),
            pltpu.VMEM((TAB // 2, 128), BF16),
            pltpu.VMEM((3, TAB // 8, 128), BF16),
            pltpu.VMEM((TAB, 128), F32),
            dma((7,)), dma((2, 3, 2)), dma((4, 3)), dma((3, 3)), dma((3, 3)), dma((3, 4)), dma((3, 4)),
        ],
        compiler_params=pltpu.CompilerParams(
            collective_id=1, has_side_effects=True, vmem_limit_bytes=62 * 1024 * 1024
        ),
        cost_estimate=pl.CostEstimate(flops=24_000_000_000, bytes_accessed=10_000_000, transcendentals=0),
        name="sketch_reduce",
    )(ghl, codes, spots)


def finish_kernel(
    table, med, info, across, mom, err, w_in, w_out,
    win_new, wout_new, mom_new, err_new,
    tabv, medv, infov, acrossv, momv, errv, winv, woutv, winn, woutn, momn, errn, sem, out_sem,
):
    pairs = [(info, infov), (med, medv), (table, tabv), (across, acrossv), (w_in, winv), (w_out, woutv)]
    for j in range(ROWS):
        pairs += [(mom.at[:, j, :], momv.at[j]), (err.at[:, j, :], errv.at[j])]
    loads = [pltpu.make_async_copy(src, dst, sem.at[n]) for n, (src, dst) in enumerate(pairs)]
    for load in loads:
        load.start()
    stores = []

    def store(src, dst):
        stores.append(pltpu.make_async_copy(src, dst, out_sem.at[len(stores)]))
        stores[-1].start()

    for load in loads[:4]:
        load.wait()
    codes = infov[...]
    update = medv[...] + LEARN * tabv[LISTED:, :]
    kept = split2(jnp.where(codes[:, ROWS : ROWS + 1] == 1, update, 0.0))
    places = acrossv[0:1, :]

    def delta(start, rows):
        hit = jnp.where(iota((rows, LIVE), 0) + start == places, 1.0, 0.0).astype(BF16)
        got = nn(hit, kept)
        return got[:, :128] + got[:, 128:]

    loads[4].wait()
    for c in range(4):
        rows = pl.ds(c * 512, 512)
        for h in range(2):
            at = slice(h * 128, (h + 1) * 128)
            winn[rows, at] = winv[rows, at].astype(F32) - delta(h * 2048 + c * 512, 512)
        store(winn.at[rows], win_new.at[rows])
    loads[5].wait()
    for c in range(4):
        for q in range(4 * c, 4 * c + 4):
            at = slice(q * 128, (q + 1) * 128)
            woutn[:, at] = woutv[:, at].astype(F32) - delta(4096 + q * 256, 256)
        at = pl.ds(c * 512, 512)
        store(woutn.at[:, at], wout_new.at[:, at])
    for j in range(ROWS):
        loads[6 + 2 * j].wait()
        loads[7 + 2 * j].wait()
        fresh = DECAY * momv[j] + tabv[j * COUNT : (j + 1) * COUNT, :]
        momn[j] = fresh
        store(momn.at[j], mom_new.at[:, j, :])
        gone = tn(signed_hit(codes[:, j : j + 1]), kept)
        errn[j] = errv[j] + LEARN * fresh - (gone[:, :128] + gone[:, 128:])
        store(errn.at[j], err_new.at[:, j, :])
    for copy in stores:
        copy.wait()


def run_finish(table, med, info, across, mom, err, w_in, w_out):
    anywhere = pl.BlockSpec(memory_space=pl.ANY)
    vmem = pltpu.VMEM
    deep = vmem((ROWS, COUNT, 128), F32)
    return pl.pallas_call(
        finish_kernel,
        out_shape=(
            jax.ShapeDtypeStruct(w_in.shape, F32),
            jax.ShapeDtypeStruct(w_out.shape, F32),
            jax.ShapeDtypeStruct(mom.shape, F32),
            jax.ShapeDtypeStruct(err.shape, F32),
        ),
        in_specs=[anywhere] * 8,
        out_specs=(anywhere,) * 4,
        scratch_shapes=[
            vmem((TAB, 128), F32), vmem((LIVE, 128), F32), vmem((LIVE, 128), I32), vmem((8, LIVE), I32),
            deep, deep, vmem(w_in.shape, BF16), vmem(w_out.shape, BF16), vmem(w_in.shape, F32), vmem(w_out.shape, F32),
            deep, deep, pltpu.SemaphoreType.DMA((16,)), pltpu.SemaphoreType.DMA((18,)),
        ],
        compiler_params=pltpu.CompilerParams(vmem_limit_bytes=62 * 1024 * 1024),
        cost_estimate=pl.CostEstimate(flops=3_000_000_000, bytes_accessed=16_000_000, transcendentals=0),
        name="finish",
    )(table, med, info, across, mom, err, w_in, w_out)


def per_device(
    tokens, cotangent, w_in, w_out, momentum, error, block_order, signs, heavy_blocks, heavy_count
):
    mom, err = by_bucket(momentum), by_bucket(error)
    ghl, codes, spots, med, info, across = run_main(
        tokens, cotangent, w_in, w_out, block_order, signs, heavy_blocks, heavy_count, mom, err
    )
    table = run_sketch(ghl, codes, spots)
    win_new, wout_new, mom_new, err_new = run_finish(table, med, info, across, mom, err, w_in, w_out)
    return win_new, wout_new, by_row(mom_new), by_row(err_new)


def by_bucket(table):
    return jnp.transpose(table.reshape(ROWS, COUNT, 128), (1, 0, 2))


def by_row(table):
    return jnp.transpose(table, (1, 0, 2)).reshape(ROWS, COUNT * 128)


def solution(mesh):
    placed = (
        P(("rep", "shard"), None),
        P(("rep", "shard"), None),
        P(None, "shard"),
        P("shard", None),
        P(None, "shard"),
        P(None, "shard"),
        P(None, "shard"),
        P(None, "shard"),
        P("rep", "shard"),
        P("rep", "shard"),
    )
    return jax.shard_map(
        per_device,
        mesh=mesh,
        in_specs=placed,
        out_specs=(P(None, "shard"), P("shard", None), P(None, "shard"), P(None, "shard")),
        check_vma=False,
    )
```

```python
import functools

import jax
import jax.numpy as jnp
from jax import lax
from jax.experimental import pallas as pl
from jax.experimental.pallas import tpu as pltpu
from jax.sharding import PartitionSpec as P

MESH = pl.DeviceIdType.MESH
F32, BF16, I32 = jnp.float32, jnp.bfloat16, jnp.int32
LEARN = 0.05
DECAY = 0.9
ROOT = 0.7978845608028654

NX, NY, NZ = 4, 4, 8
TOK = 104
CHIP = 2 * TOK
SUBS = ((0, 112), (112, 96))
DW, COLS = 2048, 256
NB = 8192
COUNT = 512
ROWS = 5
LIVE = 256
LISTED = ROWS * COUNT
TAB = LISTED + LIVE
PIECES = ((0, 1024), (1024, 1024), (2048, 768))
CODE = ROWS * 64
META = CODE + 64


def nt(a, b):
    return lax.dot_general(a, b, (((1,), (1,)), ((), ())), preferred_element_type=F32)


def tn(a, b):
    return lax.dot_general(a, b, (((0,), (0,)), ((), ())), preferred_element_type=F32)


def nn(a, b):
    return jnp.dot(a, b, preferred_element_type=F32)


def iota(shape, dim):
    return lax.broadcasted_iota(I32, shape, dim)


def split2(x):
    hi = x.astype(BF16)
    return jnp.concatenate([hi, (x - hi.astype(F32)).astype(BF16)], axis=1)


def place_of(block):
    rest = block - 4096
    return jnp.where(
        block < 4096, (block & 1) * 2048 + (block >> 1), 4096 + (rest & 15) * 256 + (rest >> 4)
    )


def gelu_pair(pre):
    tangent = jnp.tanh(ROOT * (pre + 0.044715 * pre * pre * pre))
    value = 0.5 * pre * (1.0 + tangent)
    slope = 0.5 * (1.0 + tangent) + 0.5 * pre * (1.0 - tangent * tangent) * ROOT * (
        1.0 + 0.134145 * pre * pre
    )
    return value, slope


def invert(ord_ref, sgn_ref, meta_ref):
    step = 1024
    for j in range(ROWS):

        def body(c, acc, j=j):
            at = pl.ds(pl.multiple_of(c * step, step), step)
            place = place_of(ord_ref[j : j + 1, at])
            sign = sgn_ref[j : j + 1, at]
            bucket = (c * step + iota((1, step), 1)) >> 4
            row = iota((128, step), 0)
            value = jnp.where(row < 64, bucket >> 1, (bucket & 1) * 2 + sign)
            left = jnp.where((row & 63) == (place >> 7), value, 0).astype(F32).astype(BF16)
            right = jnp.where(row == (place & 127), 1.0, 0.0).astype(BF16)
            return acc + nt(left, right)

        acc = lax.fori_loop(0, NB // step, body, jnp.zeros((128, 128), F32))
        meta_ref[j * 64 : (j + 1) * 64, :] = (acc[:64] * 4.0 + acc[64:]).astype(I32)


def compact(lists, along):
    full = jnp.concatenate([lists, jnp.zeros((120, 128), I32)], axis=0)
    shape = (LIVE, 128)
    slot, lane = iota(shape, 0), iota(shape, 1)
    wanted = jnp.where(slot < 128, slot & 15, jnp.where(slot < 176, slot - 112, 127))
    pick = jnp.where(lane == wanted, 1.0, 0.0).astype(BF16)
    pick_count = jnp.where(lane == 64, 1.0, 0.0).astype(BF16)
    high = (full >> 7).astype(F32).astype(BF16)
    low = (full & 127).astype(F32).astype(BF16)
    if along == 0:
        values = nt(pick, high) * 128.0 + nt(pick, low)
        counts = nt(pick_count, low)
        spot, rep, axis = slot, lane, 1
    else:
        values = nt(high, pick) * 128.0 + nt(low, pick)
        counts = nt(low, pick_count)
        spot, rep, axis = iota((128, LIVE), 1), iota((128, LIVE), 0), 0
    first = (spot < 128) & (rep == (spot >> 4)) & (counts > (spot & 15).astype(F32))
    later = (spot >= 128) & (spot < 176) & (rep < 8) & (counts > 63.5)
    hit = jnp.where(first | later, 1.0, 0.0)
    live = jnp.sum(hit, axis=axis, keepdims=True)
    block = jnp.sum(hit * values, axis=axis, keepdims=True).astype(I32)
    return jnp.where(live > 0.5, place_of(block), -1)


def lists_of(meta_ref, *lead):
    total = jnp.zeros((8, 128), I32)
    for r in range(8):
        total = total + meta_ref[(*lead, slice(CODE + 8 * r, CODE + 8 * r + 8), slice(None))]
    return total


def middle_value(values):
    values = list(values)
    total = len(values)
    for rounds in range(total):
        for i in range(rounds % 2, total - 1, 2):
            lower = jnp.minimum(values[i], values[i + 1])
            upper = jnp.maximum(values[i], values[i + 1])
            values[i] = lower
            values[i + 1] = upper
    return values[total // 2]


def prepare(meta, momv, errv, medv, infov, acrossv):
    lists = lists_of(meta)
    down, across = compact(lists, 0), compact(lists, 1)
    shape = (LIVE, LIVE)
    same = (down == across) & (across >= 0) & (iota(shape, 1) < iota(shape, 0))
    earlier = jnp.max(jnp.where(same, 1.0, 0.0), axis=1, keepdims=True)
    keep = jnp.where((down >= 0) & (earlier < 0.5), 1, 0)
    codes = meta[...]
    high = (codes >> 2).astype(F32).astype(BF16)
    low = (codes & 3).astype(F32).astype(BF16)
    lane = iota((LIVE, 128), 1)
    lane_hit = lane == (down & 127)
    info = jnp.where(lane == ROWS, keep, 0)
    found = []
    for j in range(ROWS):
        pick = jnp.where(iota((LIVE, META), 1) == (down >> 7) + j * 64, 1.0, 0.0)
        pick = jnp.where(down >= 0, pick, 0.0).astype(BF16)
        value = nn(pick, high) * 4.0 + nn(pick, low)
        code = jnp.sum(jnp.where(lane_hit, value, 0.0), axis=1, keepdims=True).astype(I32)
        info = jnp.where(lane == j, code, info)
        probe = errv[j] + LEARN * DECAY * momv[j]
        got = nn(signed_hit(code), split2(probe))
        found.append(got[:, :128] + got[:, 128:])
    medv[...] = middle_value(found)
    infov[...] = info
    acrossv[...] = jnp.broadcast_to(across, acrossv.shape)


def signed_hit(code):
    sign = jnp.where((code & 1) == 1, 1.0, -1.0)
    return jnp.where(iota((LIVE, COUNT), 1) == (code >> 1), sign, 0.0).astype(BF16)


def main_kernel(
    tok_ref, cot_ref, win_ref, wout_ref, ord_ref, sgn_ref, lst_ref, cnt_ref, mom_ref, err_ref,
    ghl_ref, codes_ref, spots_ref, med_ref, info_ref, across_ref,
    own, land, buf, wi, wo, gin, gout, ordv, sgnv, meta, meta2, ghl,
    momv, errv, medv, infov, acrossv, spots, lstv,
    lsem, land_sem, ring_s, ring_r, sib_s, sib_r, w_s, w_r, list_s, list_r, meta_s, meta_r,
):
    rep, shard = lax.axis_index("rep"), lax.axis_index("shard")
    y, core = rep // 2, rep % 2
    x, z = shard // NZ, shard % NZ
    other = 1 - core

    def dev(dx=0, dy=0, dz=0, to=None):
        c = core if to is None else to
        return {
            "rep": lax.rem(y + dy + NY, NY) * 2 + c,
            "shard": lax.rem(x + dx + NX, NX) * NZ + lax.rem(z + dz + NZ, NZ),
        }

    def remote(src, dst, send, recv, device):
        return pltpu.make_async_remote_copy(
            src_ref=src, dst_ref=dst, send_sem=send, recv_sem=recv, device_id=device, device_id_type=MESH
        )

    def on_core(c, *actions):
        @pl.when(core == c)
        def _():
            for action in actions:
                action()

    own_tok = pltpu.make_async_copy(tok_ref, own, lsem.at[0])
    own_cot = pltpu.make_async_copy(cot_ref, own, lsem.at[0])
    loads = [
        pltpu.make_async_copy(lst_ref, lstv, lsem.at[1]),
        pltpu.make_async_copy(ord_ref, ordv, lsem.at[2]),
        pltpu.make_async_copy(sgn_ref, sgnv, lsem.at[3]),
    ]
    tables = [pltpu.make_async_copy(mom_ref.at[:, j, :], momv.at[j], lsem.at[6 + j]) for j in range(ROWS)]
    tables += [pltpu.make_async_copy(err_ref.at[:, j, :], errv.at[j], lsem.at[11 + j]) for j in range(ROWS)]
    own_wi = pltpu.make_async_copy(win_ref, wi.at[:, pl.ds(0, COLS)], lsem.at[4])
    own_wo = pltpu.make_async_copy(wout_ref, wo.at[pl.ds(0, COLS)], lsem.at[5])
    on_core(0, own_tok.start)
    on_core(1, own_cot.start)
    for load in loads:
        load.start()

    barrier = pltpu.get_barrier_semaphore()
    partners = [dev(dz=1), dev(dz=-1)]
    partners += [dev(dx=d, to=c) for d in (1, -1, 2) for c in (0, 1)]
    partners += [dev(dy=d, to=c) for d in (1, 2, 3) for c in (0, 1)] + [dev(to=other)]
    for partner in partners:
        pl.semaphore_signal(barrier, inc=1, device_id=partner, device_id_type=MESH)
    pl.semaphore_wait(barrier, len(partners))

    give_cot = remote(cot_ref, land, land_sem.at[0], land_sem.at[1], dev(to=other))
    give_tok = remote(tok_ref, land, land_sem.at[0], land_sem.at[1], dev(to=other))
    on_core(0, give_cot.start)
    on_core(1, give_tok.start)

    toward = jnp.where(core == 0, -1, 1)
    lower, upper = pl.ds(0, COLS), pl.ds(COLS, COLS)
    landing = pl.ds(pl.multiple_of(other * COLS, COLS), COLS)
    w_in_first = remote(win_ref, wi.at[:, landing], w_s.at[0], w_r.at[0], dev(dx=toward))
    w_out_first = remote(wout_ref, wo.at[landing], w_s.at[1], w_r.at[1], dev(dx=toward))
    w_in_next = remote(wi.at[:, upper], wi.at[:, upper], w_s.at[2], w_r.at[2], dev(dx=-1, to=1))
    w_out_next = remote(wo.at[lower], wo.at[upper], w_s.at[3], w_r.at[3], dev(dx=1, to=1))
    on_core(0, w_in_first.start, w_out_first.start, own_wi.start, own_wo.start)
    on_core(1, w_out_first.start, w_in_first.start)

    on_core(0, own_tok.wait, give_cot.wait)
    on_core(1, own_cot.wait, give_tok.wait)
    for c in range(4):
        at = slice(c * 512, (c + 1) * 512)
        mine, theirs = own[:, at].astype(F32), land[:, at].astype(F32)
        first, second = jnp.where(core == 0, mine, theirs), jnp.where(core == 0, theirs, mine)
        buf[core, 0:CHIP, at] = jnp.concatenate([first, second], axis=0).astype(BF16)

    def turn_of(way, sub):
        return sub if way == 0 else 1 - sub

    def unit_of(hops, turn):
        return 0 if hops == 0 else 2 * hops - 1 + turn

    def rows_of(unit, sub):
        return pl.ds(unit * CHIP + SUBS[sub][0], SUBS[sub][1])

    def ring(way, hops, sub):
        turn = turn_of(way, sub)
        return remote(
            buf.at[core, rows_of(unit_of(hops, turn), sub)],
            buf.at[core, rows_of(unit_of(hops + 1, turn), sub)],
            ring_s.at[way, hops, sub], ring_r.at[way, hops, sub],
            dev(dz=1 if way == 0 else -1),
        )

    def sibling(unit, sub):
        at = buf.at[core, rows_of(unit, sub)]
        return remote(at, at, sib_s.at[unit, sub], sib_r.at[unit, sub], dev(to=other))

    for turn in (0, 1):
        ring(0, 0, turn).start()
        ring(1, 0, 1 - turn).start()
    for sub in (0, 1):
        sibling(0, sub).start()
    loads[0].wait()
    listed = jnp.concatenate([lstv[...], jnp.full(lstv.shape, cnt_ref[0, 0], I32)], axis=1)
    meta[pl.ds(pl.multiple_of(CODE + 8 * rep, 8), 8), :] = jnp.where(iota((8, 128), 0) == rep, listed, 0)
    list_row = meta.at[pl.ds(pl.multiple_of(CODE + 8 * rep, 8), 8)]
    peers = [(0, 1), (1, 0), (1, 1), (2, 0), (2, 1), (3, 0), (3, 1)]
    peers = [(n, dev(dy=d, to=other if flip else core)) for n, (d, flip) in enumerate(peers)]
    list_copies = [remote(list_row, list_row, list_s.at[n], list_r.at[n], peer) for n, peer in peers]
    for copy in list_copies:
        copy.start()

    for load in tables:
        load.start()

    def arrive(hops, turn):
        for way in (0, 1):
            sub = turn if way == 0 else 1 - turn
            ring(way, hops - 1, sub).wait_recv()
            if hops < 3 or (hops == 3 and turn == 0):
                ring(way, hops, sub).start()
            sibling(unit_of(hops, turn), sub).start()

    loads[1].wait()
    loads[2].wait()
    invert(ordv, sgnv, meta)
    for copy in list_copies:
        copy.wait_recv()
    meta_first = remote(meta, meta2.at[other], meta_s.at[0], meta_r.at[0], dev(dx=toward))
    meta_next = remote(meta, meta2.at[1], meta_s.at[1], meta_r.at[1], dev(dx=2))
    meta_first.start()
    on_core(1, meta_next.start)

    @pl.when(core == 0)
    def _():
        meta2[0] = meta[...]

    gin[...] = jnp.zeros_like(gin)
    gout[...] = jnp.zeros_like(gout)

    arrive(1, 0)
    on_core(0, w_in_first.wait_recv, w_in_next.start)
    on_core(1, w_out_first.wait_recv, w_out_next.start)
    arrive(1, 1)
    for load in tables:
        load.wait()
    prepare(meta, momv, errv, medv, infov, acrossv)
    ready = [
        pltpu.make_async_copy(medv, med_ref, lsem.at[16]),
        pltpu.make_async_copy(infov, info_ref, lsem.at[17]),
        pltpu.make_async_copy(acrossv, across_ref, lsem.at[18]),
    ]
    for copy in ready:
        copy.start()
    meta_first.wait_recv()
    on_core(1, meta_next.wait_recv)
    for k in (0, 1):
        spots[k] = jnp.broadcast_to(compact(lists_of(meta2, k), 0), (LIVE, 128))
    ready += [
        pltpu.make_async_copy(meta2, codes_ref, lsem.at[21]),
        pltpu.make_async_copy(spots, spots_ref, lsem.at[22]),
    ]
    for copy in ready[3:]:
        copy.start()
    arrive(2, 0)
    on_core(0, w_out_first.wait_recv, own_wi.wait, own_wo.wait)
    on_core(1, w_in_first.wait_recv, w_in_next.wait_recv, w_out_next.wait_recv)

    def wait_sibling(*units):
        for unit in units:
            for sub in (0, 1):
                sibling(unit, sub).wait_recv()

    out_first = pltpu.make_async_copy(ghl.at[:, pl.ds(0, 4096)], ghl_ref.at[:, pl.ds(0, 4096)], lsem.at[19])
    out_last = pltpu.make_async_copy(ghl.at[:, pl.ds(4096, 4096)], ghl_ref.at[:, pl.ds(4096, 4096)], lsem.at[20])
    ready += [out_first, out_last]

    def work(start, count, last=False):
        rows = pl.ds(start, count)
        value, slope = gelu_pair(nn(buf[0, rows, :], wi[...]))
        back = nt(buf[1, rows, :], wo[...])
        hidden = value.astype(BF16)
        grad = (back * slope).astype(BF16)
        for c in range(4):
            at = slice(c * 512, (c + 1) * 512)
            total = gin[at, :] + tn(buf[0, rows, at], grad)
            if not last:
                gin[at, :] = total
                continue
            for k in range(2):
                for h in range(2):
                    part = total[:, k * COLS + h * 128 : k * COLS + (h + 1) * 128]
                    ghl[k, h * 2048 + c * 512 : h * 2048 + (c + 1) * 512, :] = split2(part)
        if last:
            out_first.start()
        for c in range(4):
            at = slice(c * 512, (c + 1) * 512)
            total = gout[:, at] + tn(hidden, buf[1, rows, at])
            if not last:
                gout[:, at] = total
                continue
            for k in range(2):
                for q in range(4 * c, 4 * c + 4):
                    part = total[k * COLS : (k + 1) * COLS, (q - 4 * c) * 128 : (q - 4 * c + 1) * 128]
                    ghl[k, 4096 + q * 256 : 4352 + q * 256, :] = split2(part)

    def work_pair(i, carry):
        @pl.when(i == 0)
        def _():
            wait_sibling(0, 1)

        @pl.when(i == 1)
        def _():
            wait_sibling(2, 3)

        @pl.when(i == 1)
        def _():
            arrive(2, 1)

        @pl.when(i == 2)
        def _():
            arrive(3, 0)
            wait_sibling(4, 5)

        work(pl.multiple_of(i * (2 * CHIP), 16), 2 * CHIP)
        return carry

    lax.fori_loop(0, 3, work_pair, 0)
    arrive(3, 1)
    wait_sibling(6)
    work(6 * CHIP, CHIP)
    ring(0, 3, 0).wait_recv()
    sibling(7, 0).start()
    ring(1, 3, 1).wait_recv()
    sibling(7, 1).start()
    wait_sibling(7)
    work(7 * CHIP, CHIP, last=True)
    out_last.start()

    for copy in list_copies + [w_in_first, w_out_first, meta_first]:
        copy.wait_send()
    for way in (0, 1):
        for hops in range(4):
            for sub in (0, 1):
                if hops < 3 or sub == way:
                    ring(way, hops, sub).wait_send()
    for unit in range(NZ):
        for sub in (0, 1):
            sibling(unit, sub).wait_send()
    on_core(0, w_in_next.wait_send)
    on_core(1, w_out_next.wait_send, meta_next.wait_send)
    for copy in ready:
        copy.wait()


def sketch_kernel(
    ghl_ref, codes_ref, spots_ref, table_ref,
    ghl, codes, spots, outb, recvx, yb, recvy, tot, lsem, x_s, x_r, y_s, y_r, a_s, a_r,
):
    rep, shard = lax.axis_index("rep"), lax.axis_index("shard")
    y, core = rep // 2, rep % 2
    x, z = shard // NZ, shard % NZ
    other = 1 - core

    def dev(dx=0, dy=0, dz=0, to=None):
        c = core if to is None else to
        return {
            "rep": lax.rem(y + dy + NY, NY) * 2 + c,
            "shard": lax.rem(x + dx + NX, NX) * NZ + lax.rem(z + dz + NZ, NZ),
        }

    def remote(src, dst, send, recv, device):
        return pltpu.make_async_remote_copy(
            src_ref=src, dst_ref=dst, send_sem=send, recv_sem=recv, device_id=device, device_id_type=MESH
        )

    def on_core(c, *actions):
        @pl.when(core == c)
        def _():
            for action in actions:
                action()

    loads = [
        pltpu.make_async_copy(codes_ref, codes, lsem.at[0]),
        pltpu.make_async_copy(spots_ref, spots, lsem.at[1]),
        pltpu.make_async_copy(ghl_ref.at[1], ghl.at[1], lsem.at[2]),
        pltpu.make_async_copy(ghl_ref.at[0], ghl.at[0], lsem.at[3]),
    ]
    for load in loads:
        load.start()
    barrier = pltpu.get_barrier_semaphore()
    partners = [dev(dx=d, to=c) for d in (1, -1, 2) for c in (0, 1)]
    partners += [dev(dy=d) for d in (1, 2, 3)] + [dev(to=other)]
    for partner in partners:
        pl.semaphore_signal(barrier, inc=1, device_id=partner, device_id_type=MESH)
    pl.semaphore_wait(barrier, len(partners))
    loads[0].wait()
    loads[1].wait()

    def spread(code):
        code = jnp.broadcast_to(code, (16, 128))
        bucket = (code >> 1).astype(F32)
        return jnp.where((code & 1) == 1, 1.0, -1.0).astype(BF16), [(bucket - 256.0 * h).astype(BF16) for h in (0, 1)]

    def one_hot(spread_code, quarter):
        sign, spot = spread_code[0], spread_code[1][quarter // 2]
        ramp = iota((256, 128), 0).astype(F32).astype(BF16)
        first = 8 * (quarter % 2)
        hits = [spot == ramp[g * 16 : (g + 1) * 16] for g in range(first, first + 8)]
        return jnp.concatenate([jnp.where(hit, sign, jnp.zeros_like(sign)) for hit in hits], axis=0)

    def sketch(k, work):
        step = 4
        per = NB // 512
        used = sorted({j for j, _ in work if j is not None})
        rows_in = [64 if part == (None, 1) else 128 for part in work]

        def run(*sums):
            def chunk(t, carry):
                first = [unit * per + t * step for unit in (0, 1)]

                def tile(unit, i):
                    return ghl[k, pl.ds(pl.multiple_of((first[unit] + i) * 256, 256), 256), :]

                found = [
                    {j: codes[k, pl.ds(pl.multiple_of(j * 64 + 2 * first[unit], 8), 2 * step), :] for j in used}
                    for unit in (0, 1)
                ]
                for unit in (0, 1):
                    pltpu.matmul_push_rhs(tile(unit, 0), 0, unit)
                for i in range(step):
                    if i + 1 < step:
                        for unit in (0, 1):
                            pltpu.matmul_push_rhs(tile(unit, i + 1), (i + 1) % 2, unit)
                    rows = [
                        {j: [spread(found[unit][j][2 * i + n : 2 * i + n + 1, :]) for n in (0, 1)] for j in used}
                        for unit in (0, 1)
                    ]
                    for c, (j, q) in enumerate(work):
                        for unit in (0, 1):
                            if j is None:
                                spot = spots[k, q * 128 : q * 128 + rows_in[c], :] - (first[unit] + i) * 256
                                lane = iota((rows_in[c], 128), 1)
                                hot = [jnp.where(spot == lane + 128 * n, 1.0, 0.0).astype(BF16) for n in (0, 1)]
                            else:
                                hot = [one_hot(rows[unit][j][n], q) for n in (0, 1)]
                            pltpu.matmul_acc_lhs(
                                sums[2 * c + unit],
                                jnp.concatenate(hot, axis=1),
                                load_staged_rhs=i % 2 if c == 0 else None,
                            )
                return carry

            lax.fori_loop(0, per // step, chunk, 0)
            for c, (j, q) in enumerate(work):
                total = pltpu.matmul_pop(sums[2 * c]) + pltpu.matmul_pop(sums[2 * c + 1])
                start = q * 128 + (LISTED if j is None else j * COUNT)
                outb[k, start : start + rows_in[c], :] = (total[:, :128] + total[:, 128:]).astype(BF16)

        pl.run_scoped(run, *[pltpu.ACC(mxu_id=unit)((rows, 256), F32) for rows in rows_in for unit in (0, 1)])

    def whole(*rows):
        return [(j, q) for j in rows for q in range(4)]

    def half_of(p):
        return PIECES[p][0] // 2, PIECES[p][1] // 2

    def quarter_of(p):
        return PIECES[p][0] // 8, PIECES[p][1] // 8

    def x_copy(k, p, h, slot, device):
        start, rows = half_of(p)
        return remote(
            outb.at[k, pl.ds(PIECES[p][0] + h * rows, rows)], recvx.at[slot, pl.ds(start, rows)],
            x_s.at[k, p, h], x_r.at[slot, p], device,
        )

    x_far = [[x_copy(1, p, h, 1 + 2 * core, dev(dx=1 + core, to=h)) for h in (0, 1)] for p in range(3)]
    x_near = [[x_copy(0, p, h, 2, dev(dx=-1, to=h)) for h in (0, 1)] for p in range(3)]
    x_home = [x_copy(0, p, 1, 0, dev(to=1)) for p in range(3)]

    def x_far_start(p):
        for copy in x_far[p]:
            copy.start()

    def x_near_start(p):
        start, rows = half_of(p)
        on_core(1, *[copy.start for copy in x_near[p]])

        @pl.when(core == 0)
        def _():
            x_home[p].start()
            recvx[0, start : start + rows, :] = outb[0, PIECES[p][0] : PIECES[p][0] + rows, :]

    def my_quarter(p):
        rows = PIECES[p][1] // 8
        return pl.ds(pl.multiple_of(PIECES[p][0] + core * (4 * rows) + y * rows, 16), rows)

    def y_copy(p, d):
        start, rows = quarter_of(p)
        there = pl.ds(pl.multiple_of(4 * start + lax.rem(y + d, NY) * rows, 16), rows)
        return remote(yb.at[there], recvy.at[d - 1, pl.ds(start, rows)], y_s.at[p, d - 1], y_r.at[p, d - 1], dev(dy=d))

    def y_start(p):
        start, rows = half_of(p)
        on_core(1, x_copy(0, p, 1, 0, dev(to=1)).wait_recv)
        for slot in (1, 2, 3):
            x_copy(1, p, 0, slot, dev(dx=1)).wait_recv()
        part = recvx[0, start : start + rows, :].astype(F32)
        for slot in (1, 2, 3):
            part = part + recvx[slot, start : start + rows, :].astype(F32)
        yb[start : start + rows, :] = part.astype(BF16)
        tot[pl.ds(pl.multiple_of(PIECES[p][0] + core * rows, 16), rows), :] = part
        for d in (1, 2, 3):
            y_copy(p, d).start()

    def a_copy(p, d):
        at = tot.at[my_quarter(p)]
        return remote(at, at, a_s.at[p, d - 1], a_r.at[p, d - 1], dev(dy=d))

    def a_start(p):
        start, rows = quarter_of(p)
        total = tot[my_quarter(p), :]
        for d in (1, 2, 3):
            y_copy(p, d).wait_recv()
            total = total + recvy[d - 1, start : start + rows, :].astype(F32)
        tot[my_quarter(p), :] = total
        for d in (1, 2, 3):
            a_copy(p, d).start()

    def e_copy(p):
        rows = PIECES[p][1] // 2
        at = tot.at[pl.ds(pl.multiple_of(PIECES[p][0] + core * rows, 16), rows)]
        return remote(at, at, a_s.at[p, 3], a_r.at[p, 3], dev(to=other))

    def e_start(p):
        for d in (1, 2, 3):
            a_copy(p, d).wait_recv()
        e_copy(p).start()

    def piece_out(p):
        at = pl.ds(*PIECES[p])
        return pltpu.make_async_copy(tot.at[at], table_ref.at[at], lsem.at[4 + p])

    def e_finish(p):
        e_copy(p).wait_recv()
        piece_out(p).start()

    passes = (whole(0, 1), whole(2, 3), whole(4) + [(None, 0), (None, 1)])
    for k in range(2):
        outb[k, LISTED + 192 :, :] = jnp.zeros((LIVE - 192, 128), BF16)
    loads[2].wait()
    sketch(1, passes[0])
    x_far_start(0)
    loads[3].wait()
    sketch(0, passes[0])
    x_near_start(0)
    sketch(1, passes[1])
    x_far_start(1)
    y_start(0)
    sketch(0, passes[1])
    x_near_start(1)
    a_start(0)
    sketch(1, passes[2])
    x_far_start(2)
    y_start(1)
    e_start(0)
    sketch(0, passes[2])
    x_near_start(2)
    a_start(1)
    e_finish(0)
    y_start(2)
    e_start(1)
    a_start(2)
    e_finish(1)
    e_start(2)
    e_finish(2)

    for p in range(3):
        for copy in x_far[p] + [y_copy(p, d) for d in (1, 2, 3)] + [a_copy(p, d) for d in (1, 2, 3)] + [e_copy(p)]:
            copy.wait_send()
    on_core(0, *[copy.wait_send for copy in x_home])
    on_core(1, *[c.wait_send for p in range(3) for c in x_near[p]])
    for p in range(3):
        piece_out(p).wait()


def run_main(*args):
    anywhere = pl.BlockSpec(memory_space=pl.ANY)
    dma = pltpu.SemaphoreType.DMA
    return pl.pallas_call(
        main_kernel,
        out_shape=(
            jax.ShapeDtypeStruct((2, NB, 256), BF16),
            jax.ShapeDtypeStruct((2, META, 128), I32),
            jax.ShapeDtypeStruct((2, LIVE, 128), I32),
            jax.ShapeDtypeStruct((LIVE, 128), F32),
            jax.ShapeDtypeStruct((LIVE, 128), I32),
            jax.ShapeDtypeStruct((8, LIVE), I32),
        ),
        in_specs=[anywhere] * 7 + [pl.BlockSpec(memory_space=pltpu.SMEM)] + [anywhere] * 2,
        out_specs=(anywhere,) * 6,
        scratch_shapes=[
            pltpu.VMEM((TOK, DW), BF16),
            pltpu.VMEM((TOK, DW), BF16),
            pltpu.VMEM((2, NZ * CHIP, DW), BF16),
            pltpu.VMEM((DW, 2 * COLS), BF16),
            pltpu.VMEM((2 * COLS, DW), BF16),
            pltpu.VMEM((DW, 2 * COLS), F32),
            pltpu.VMEM((2 * COLS, DW), F32),
            pltpu.VMEM((ROWS, NB), I32),
            pltpu.VMEM((ROWS, NB), I32),
            pltpu.VMEM((META, 128), I32),
            pltpu.VMEM((2, META, 128), I32),
            pltpu.VMEM((2, NB, 256), BF16),
            pltpu.VMEM((ROWS, COUNT, 128), F32),
            pltpu.VMEM((ROWS, COUNT, 128), F32),
            pltpu.VMEM((LIVE, 128), F32),
            pltpu.VMEM((LIVE, 128), I32),
            pltpu.VMEM((8, LIVE), I32),
            pltpu.VMEM((2, LIVE, 128), I32),
            pltpu.VMEM((1, 64), I32),
            dma((23,)), dma((2,)),
            dma((2, 4, 2)), dma((2, 4, 2)), dma((NZ, 2)), dma((NZ, 2)), dma((4,)), dma((4,)),
            dma((7,)), dma((7,)), dma((2,)), dma((2,)),
        ],
        compiler_params=pltpu.CompilerParams(
            collective_id=0, has_side_effects=True, vmem_limit_bytes=62 * 1024 * 1024
        ),
        cost_estimate=pl.CostEstimate(flops=15_000_000_000, bytes_accessed=20_000_000, transcendentals=2_000_000),
        name="gather_grad",
    )(*args)


def run_sketch(ghl, codes, spots):
    anywhere = pl.BlockSpec(memory_space=pl.ANY)
    dma = pltpu.SemaphoreType.DMA
    return pl.pallas_call(
        sketch_kernel,
        out_shape=jax.ShapeDtypeStruct((TAB, 128), F32),
        in_specs=[anywhere] * 3,
        out_specs=anywhere,
        scratch_shapes=[
            pltpu.VMEM((2, NB, 256), BF16),
            pltpu.VMEM((2, META, 128), I32),
            pltpu.VMEM((2, LIVE, 128), I32),
            pltpu.VMEM((2, TAB, 128), BF16),
            pltpu.VMEM((4, TAB // 2, 128), BF16),
            pltpu.VMEM((TAB // 2, 128), BF16),
            pltpu.VMEM((3, TAB // 8, 128), BF16),
            pltpu.VMEM((TAB, 128), F32),
            dma((7,)), dma((2, 3, 2)), dma((4, 3)), dma((3, 3)), dma((3, 3)), dma((3, 4)), dma((3, 4)),
        ],
        compiler_params=pltpu.CompilerParams(
            collective_id=1, has_side_effects=True, vmem_limit_bytes=62 * 1024 * 1024
        ),
        cost_estimate=pl.CostEstimate(flops=24_000_000_000, bytes_accessed=10_000_000, transcendentals=0),
        name="sketch_reduce",
    )(ghl, codes, spots)


def finish_kernel(
    table, med, info, across, mom, err, w_in, w_out,
    win_new, wout_new, mom_new, err_new,
    tabv, medv, infov, acrossv, momv, errv, winv, woutv, winn, woutn, momn, errn, sem, out_sem,
):
    pairs = [(info, infov), (med, medv), (table, tabv), (across, acrossv), (w_in, winv), (w_out, woutv)]
    for j in range(ROWS):
        pairs += [(mom.at[:, j, :], momv.at[j]), (err.at[:, j, :], errv.at[j])]
    loads = [pltpu.make_async_copy(src, dst, sem.at[n]) for n, (src, dst) in enumerate(pairs)]
    for load in loads:
        load.start()
    stores = []

    def store(src, dst):
        stores.append(pltpu.make_async_copy(src, dst, out_sem.at[len(stores)]))
        stores[-1].start()

    for load in loads[:4]:
        load.wait()
    codes = infov[...]
    update = medv[...] + LEARN * tabv[LISTED:, :]
    kept = split2(jnp.where(codes[:, ROWS : ROWS + 1] == 1, update, 0.0))
    places = acrossv[0:1, :]

    def delta(start, rows):
        hit = jnp.where(iota((rows, LIVE), 0) + start == places, 1.0, 0.0).astype(BF16)
        got = nn(hit, kept)
        return got[:, :128] + got[:, 128:]

    loads[4].wait()
    for c in range(4):
        rows = pl.ds(c * 512, 512)
        for h in range(2):
            at = slice(h * 128, (h + 1) * 128)
            winn[rows, at] = winv[rows, at].astype(F32) - delta(h * 2048 + c * 512, 512)
        store(winn.at[rows], win_new.at[rows])
    loads[5].wait()
    for c in range(4):
        for q in range(4 * c, 4 * c + 4):
            at = slice(q * 128, (q + 1) * 128)
            woutn[:, at] = woutv[:, at].astype(F32) - delta(4096 + q * 256, 256)
        at = pl.ds(c * 512, 512)
        store(woutn.at[:, at], wout_new.at[:, at])
    for j in range(ROWS):
        loads[6 + 2 * j].wait()
        loads[7 + 2 * j].wait()
        fresh = DECAY * momv[j] + tabv[j * COUNT : (j + 1) * COUNT, :]
        momn[j] = fresh
        store(momn.at[j], mom_new.at[:, j, :])
        gone = tn(signed_hit(codes[:, j : j + 1]), kept)
        errn[j] = errv[j] + LEARN * fresh - (gone[:, :128] + gone[:, 128:])
        store(errn.at[j], err_new.at[:, j, :])
    for copy in stores:
        copy.wait()


def run_finish(table, med, info, across, mom, err, w_in, w_out):
    anywhere = pl.BlockSpec(memory_space=pl.ANY)
    vmem = pltpu.VMEM
    deep = vmem((ROWS, COUNT, 128), F32)
    return pl.pallas_call(
        finish_kernel,
        out_shape=(
            jax.ShapeDtypeStruct(w_in.shape, F32),
            jax.ShapeDtypeStruct(w_out.shape, F32),
            jax.ShapeDtypeStruct(mom.shape, F32),
            jax.ShapeDtypeStruct(err.shape, F32),
        ),
        in_specs=[anywhere] * 8,
        out_specs=(anywhere,) * 4,
        scratch_shapes=[
            vmem((TAB, 128), F32), vmem((LIVE, 128), F32), vmem((LIVE, 128), I32), vmem((8, LIVE), I32),
            deep, deep, vmem(w_in.shape, BF16), vmem(w_out.shape, BF16), vmem(w_in.shape, F32), vmem(w_out.shape, F32),
            deep, deep, pltpu.SemaphoreType.DMA((16,)), pltpu.SemaphoreType.DMA((18,)),
        ],
        compiler_params=pltpu.CompilerParams(vmem_limit_bytes=62 * 1024 * 1024),
        cost_estimate=pl.CostEstimate(flops=3_000_000_000, bytes_accessed=16_000_000, transcendentals=0),
        name="finish",
    )(table, med, info, across, mom, err, w_in, w_out)


def per_device(
    tokens, cotangent, w_in, w_out, momentum, error, block_order, signs, heavy_blocks, heavy_count
):
    mom, err = by_bucket(momentum), by_bucket(error)
    ghl, codes, spots, med, info, across = run_main(
        tokens, cotangent, w_in, w_out, block_order, signs, heavy_blocks, heavy_count, mom, err
    )
    table = run_sketch(ghl, codes, spots)
    win_new, wout_new, mom_new, err_new = run_finish(table, med, info, across, mom, err, w_in, w_out)
    return win_new, wout_new, by_row(mom_new), by_row(err_new)


def by_bucket(table):
    return jnp.transpose(table.reshape(ROWS, COUNT, 128), (1, 0, 2))


def by_row(table):
    return jnp.transpose(table, (1, 0, 2)).reshape(ROWS, COUNT * 128)


def solution(mesh):
    placed = (
        P(("rep", "shard"), None),
        P(("rep", "shard"), None),
        P(None, "shard"),
        P("shard", None),
        P(None, "shard"),
        P(None, "shard"),
        P(None, "shard"),
        P(None, "shard"),
        P("rep", "shard"),
        P("rep", "shard"),
    )
    return jax.shard_map(
        per_device,
        mesh=mesh,
        in_specs=placed,
        out_specs=(P(None, "shard"), P("shard", None), P(None, "shard"), P(None, "shard")),
        check_vma=False,
    )
```

```python
import functools

import jax
import jax.numpy as jnp
from jax import lax
from jax.experimental import pallas as pl
from jax.experimental.pallas import tpu as pltpu
from jax.sharding import PartitionSpec as P

MESH = pl.DeviceIdType.MESH
F32, BF16, I32 = jnp.float32, jnp.bfloat16, jnp.int32
LEARN = 0.05
DECAY = 0.9
ROOT = 0.7978845608028654

NX, NY, NZ = 4, 4, 8
TOK = 104
CHIP = 2 * TOK
SUBS = ((0, 112), (112, 96))
DW, COLS = 2048, 256
NB = 8192
COUNT = 512
ROWS = 5
LIVE = 256
LISTED = ROWS * COUNT
TAB = LISTED + LIVE
PIECES = ((0, 1024), (1024, 1024), (2048, 768))
CODE = ROWS * 64
META = CODE + 64


def nt(a, b):
    return lax.dot_general(a, b, (((1,), (1,)), ((), ())), preferred_element_type=F32)


def tn(a, b):
    return lax.dot_general(a, b, (((0,), (0,)), ((), ())), preferred_element_type=F32)


def nn(a, b):
    return jnp.dot(a, b, preferred_element_type=F32)


def iota(shape, dim):
    return lax.broadcasted_iota(I32, shape, dim)


def split2(x):
    hi = x.astype(BF16)
    return jnp.concatenate([hi, (x - hi.astype(F32)).astype(BF16)], axis=1)


def place_of(block):
    rest = block - 4096
    return jnp.where(
        block < 4096, (block & 1) * 2048 + (block >> 1), 4096 + (rest & 15) * 256 + (rest >> 4)
    )


def gelu_pair(pre):
    tangent = jnp.tanh(ROOT * (pre + 0.044715 * pre * pre * pre))
    value = 0.5 * pre * (1.0 + tangent)
    slope = 0.5 * (1.0 + tangent) + 0.5 * pre * (1.0 - tangent * tangent) * ROOT * (
        1.0 + 0.134145 * pre * pre
    )
    return value, slope


def invert(ord_ref, sgn_ref, meta_ref):
    step = 1024
    for j in range(ROWS):

        def body(c, acc, j=j):
            at = pl.ds(pl.multiple_of(c * step, step), step)
            place = place_of(ord_ref[j : j + 1, at])
            sign = sgn_ref[j : j + 1, at]
            bucket = (c * step + iota((1, step), 1)) >> 4
            row = iota((128, step), 0)
            value = jnp.where(row < 64, bucket >> 1, (bucket & 1) * 2 + sign)
            left = jnp.where((row & 63) == (place >> 7), value, 0).astype(F32).astype(BF16)
            right = jnp.where(row == (place & 127), 1.0, 0.0).astype(BF16)
            return acc + nt(left, right)

        acc = lax.fori_loop(0, NB // step, body, jnp.zeros((128, 128), F32))
        meta_ref[j * 64 : (j + 1) * 64, :] = (acc[:64] * 4.0 + acc[64:]).astype(I32)


def compact(lists, along):
    full = jnp.concatenate([lists, jnp.zeros((120, 128), I32)], axis=0)
    shape = (LIVE, 128)
    slot, lane = iota(shape, 0), iota(shape, 1)
    wanted = jnp.where(slot < 128, slot & 15, jnp.where(slot < 176, slot - 112, 127))
    pick = jnp.where(lane == wanted, 1.0, 0.0).astype(BF16)
    pick_count = jnp.where(lane == 64, 1.0, 0.0).astype(BF16)
    high = (full >> 7).astype(F32).astype(BF16)
    low = (full & 127).astype(F32).astype(BF16)
    if along == 0:
        values = nt(pick, high) * 128.0 + nt(pick, low)
        counts = nt(pick_count, low)
        spot, rep, axis = slot, lane, 1
    else:
        values = nt(high, pick) * 128.0 + nt(low, pick)
        counts = nt(low, pick_count)
        spot, rep, axis = iota((128, LIVE), 1), iota((128, LIVE), 0), 0
    first = (spot < 128) & (rep == (spot >> 4)) & (counts > (spot & 15).astype(F32))
    later = (spot >= 128) & (spot < 176) & (rep < 8) & (counts > 63.5)
    hit = jnp.where(first | later, 1.0, 0.0)
    live = jnp.sum(hit, axis=axis, keepdims=True)
    block = jnp.sum(hit * values, axis=axis, keepdims=True).astype(I32)
    return jnp.where(live > 0.5, place_of(block), -1)


def lists_of(meta_ref, *lead):
    total = jnp.zeros((8, 128), I32)
    for r in range(8):
        total = total + meta_ref[(*lead, slice(CODE + 8 * r, CODE + 8 * r + 8), slice(None))]
    return total


def middle_value(values):
    values = list(values)
    total = len(values)
    for rounds in range(total):
        for i in range(rounds % 2, total - 1, 2):
            lower = jnp.minimum(values[i], values[i + 1])
            upper = jnp.maximum(values[i], values[i + 1])
            values[i] = lower
            values[i + 1] = upper
    return values[total // 2]


def prepare(meta, momv, errv, medv, infov, acrossv):
    lists = lists_of(meta)
    down, across = compact(lists, 0), compact(lists, 1)
    shape = (LIVE, LIVE)
    same = (down == across) & (across >= 0) & (iota(shape, 1) < iota(shape, 0))
    earlier = jnp.max(jnp.where(same, 1.0, 0.0), axis=1, keepdims=True)
    keep = jnp.where((down >= 0) & (earlier < 0.5), 1, 0)
    codes = meta[...]
    high = (codes >> 2).astype(F32).astype(BF16)
    low = (codes & 3).astype(F32).astype(BF16)
    lane = iota((LIVE, 128), 1)
    lane_hit = lane == (down & 127)
    info = jnp.where(lane == ROWS, keep, 0)
    found = []
    for j in range(ROWS):
        pick = jnp.where(iota((LIVE, META), 1) == (down >> 7) + j * 64, 1.0, 0.0)
        pick = jnp.where(down >= 0, pick, 0.0).astype(BF16)
        value = nn(pick, high) * 4.0 + nn(pick, low)
        code = jnp.sum(jnp.where(lane_hit, value, 0.0), axis=1, keepdims=True).astype(I32)
        info = jnp.where(lane == j, code, info)
        probe = errv[j] + LEARN * DECAY * momv[j]
        got = nn(signed_hit(code), split2(probe))
        found.append(got[:, :128] + got[:, 128:])
    medv[...] = middle_value(found)
    infov[...] = info
    acrossv[...] = jnp.broadcast_to(across, acrossv.shape)


def signed_hit(code):
    sign = jnp.where((code & 1) == 1, 1.0, -1.0)
    return jnp.where(iota((LIVE, COUNT), 1) == (code >> 1), sign, 0.0).astype(BF16)


def main_kernel(
    tok_ref, cot_ref, win_ref, wout_ref, ord_ref, sgn_ref, lst_ref, cnt_ref, mom_ref, err_ref,
    ghl_ref, codes_ref, spots_ref, med_ref, info_ref, across_ref,
    own, land, buf, wi, wo, gin, gout, ordv, sgnv, meta, meta2, ghl,
    momv, errv, medv, infov, acrossv, spots, lstv, early, late,
    lsem, land_sem, ring_s, ring_r, sib_s, sib_r, w_s, w_r, list_s, list_r, meta_s, meta_r,
):
    rep, shard = lax.axis_index("rep"), lax.axis_index("shard")
    y, core = rep // 2, rep % 2
    x, z = shard // NZ, shard % NZ
    other = 1 - core

    def dev(dx=0, dy=0, dz=0, to=None):
        c = core if to is None else to
        return {
            "rep": lax.rem(y + dy + NY, NY) * 2 + c,
            "shard": lax.rem(x + dx + NX, NX) * NZ + lax.rem(z + dz + NZ, NZ),
        }

    def remote(src, dst, send, recv, device):
        return pltpu.make_async_remote_copy(
            src_ref=src, dst_ref=dst, send_sem=send, recv_sem=recv, device_id=device, device_id_type=MESH
        )

    def on_core(c, *actions):
        @pl.when(core == c)
        def _():
            for action in actions:
                action()

    own_tok = pltpu.make_async_copy(tok_ref, own, lsem.at[0])
    own_cot = pltpu.make_async_copy(cot_ref, own, lsem.at[0])
    loads = [
        pltpu.make_async_copy(lst_ref, lstv, lsem.at[1]),
        pltpu.make_async_copy(ord_ref, ordv, lsem.at[2]),
        pltpu.make_async_copy(sgn_ref, sgnv, lsem.at[3]),
    ]
    tables = [pltpu.make_async_copy(mom_ref.at[:, j, :], momv.at[j], lsem.at[6 + j]) for j in range(ROWS)]
    tables += [pltpu.make_async_copy(err_ref.at[:, j, :], errv.at[j], lsem.at[11 + j]) for j in range(ROWS)]
    own_wi = pltpu.make_async_copy(win_ref, wi.at[:, pl.ds(0, COLS)], lsem.at[4])
    own_wo = pltpu.make_async_copy(wout_ref, wo.at[pl.ds(0, COLS)], lsem.at[5])
    on_core(0, own_tok.start)
    on_core(1, own_cot.start)
    for load in loads:
        load.start()

    barrier = pltpu.get_barrier_semaphore()
    partners = [dev(dz=1), dev(dz=-1)]
    partners += [dev(dx=d, to=c) for d in (1, -1, 2) for c in (0, 1)]
    partners += [dev(dy=d, to=c) for d in (1, 2, 3) for c in (0, 1)] + [dev(to=other)]
    for partner in partners:
        pl.semaphore_signal(barrier, inc=1, device_id=partner, device_id_type=MESH)
    pl.semaphore_wait(barrier, len(partners))

    give_cot = remote(cot_ref, land, land_sem.at[0], land_sem.at[1], dev(to=other))
    give_tok = remote(tok_ref, land, land_sem.at[0], land_sem.at[1], dev(to=other))
    on_core(0, give_cot.start)
    on_core(1, give_tok.start)

    toward = jnp.where(core == 0, -1, 1)
    lower, upper = pl.ds(0, COLS), pl.ds(COLS, COLS)
    landing = pl.ds(pl.multiple_of(other * COLS, COLS), COLS)
    w_in_first = remote(win_ref, wi.at[:, landing], w_s.at[0], w_r.at[0], dev(dx=toward))
    w_out_first = remote(wout_ref, wo.at[landing], w_s.at[1], w_r.at[1], dev(dx=toward))
    w_in_next = remote(wi.at[:, upper], wi.at[:, upper], w_s.at[2], w_r.at[2], dev(dx=-1, to=1))
    w_out_next = remote(wo.at[lower], wo.at[upper], w_s.at[3], w_r.at[3], dev(dx=1, to=1))
    on_core(0, w_in_first.start, w_out_first.start, own_wi.start, own_wo.start)
    on_core(1, w_out_first.start, w_in_first.start)

    loads[0].wait()
    listed = jnp.concatenate([lstv[...], jnp.full(lstv.shape, cnt_ref[0, 0], I32)], axis=1)
    meta[pl.ds(pl.multiple_of(CODE + 8 * rep, 8), 8), :] = jnp.where(iota((8, 128), 0) == rep, listed, 0)
    list_row = meta.at[pl.ds(pl.multiple_of(CODE + 8 * rep, 8), 8)]
    peers = [(0, 1), (1, 0), (1, 1), (2, 0), (2, 1), (3, 0), (3, 1)]
    peers = [(n, dev(dy=d, to=other if flip else core)) for n, (d, flip) in enumerate(peers)]
    list_copies = [remote(list_row, list_row, list_s.at[n], list_r.at[n], peer) for n, peer in peers]
    for copy in list_copies:
        copy.start()

    on_core(0, own_tok.wait, give_cot.wait)
    on_core(1, own_cot.wait, give_tok.wait)
    for c in range(4):
        at = slice(c * 512, (c + 1) * 512)
        mine, theirs = own[:, at].astype(F32), land[:, at].astype(F32)
        first, second = jnp.where(core == 0, mine, theirs), jnp.where(core == 0, theirs, mine)
        buf[core, 0:CHIP, at] = jnp.concatenate([first, second], axis=0).astype(BF16)

    def turn_of(way, sub):
        return sub if way == 0 else 1 - sub

    def unit_of(hops, turn):
        return 0 if hops == 0 else 2 * hops - 1 + turn

    def rows_of(unit, sub):
        return pl.ds(unit * CHIP + SUBS[sub][0], SUBS[sub][1])

    def ring(way, hops, sub):
        turn = turn_of(way, sub)
        return remote(
            buf.at[core, rows_of(unit_of(hops, turn), sub)],
            buf.at[core, rows_of(unit_of(hops + 1, turn), sub)],
            ring_s.at[way, hops, sub], ring_r.at[way, hops, sub],
            dev(dz=1 if way == 0 else -1),
        )

    def sibling(unit, sub):
        at = buf.at[core, rows_of(unit, sub)]
        return remote(at, at, sib_s.at[unit, sub], sib_r.at[unit, sub], dev(to=other))

    for turn in (0, 1):
        ring(0, 0, turn).start()
        ring(1, 0, 1 - turn).start()
    for sub in (0, 1):
        sibling(0, sub).start()
    for load in tables:
        load.start()

    def arrive(hops, turn):
        for way in (0, 1):
            sub = turn if way == 0 else 1 - turn
            ring(way, hops - 1, sub).wait_recv()
            if hops < 3 or (hops == 3 and turn == 0):
                ring(way, hops, sub).start()
            sibling(unit_of(hops, turn), sub).start()

    loads[1].wait()
    loads[2].wait()
    invert(ordv, sgnv, meta)
    for copy in list_copies:
        copy.wait_recv()
    meta_first = remote(meta, meta2.at[other], meta_s.at[0], meta_r.at[0], dev(dx=toward))
    meta_next = remote(meta, meta2.at[1], meta_s.at[1], meta_r.at[1], dev(dx=2))
    meta_first.start()
    on_core(1, meta_next.start)

    @pl.when(core == 0)
    def _():
        meta2[0] = meta[...]

    gin[...] = jnp.zeros_like(gin)
    gout[...] = jnp.zeros_like(gout)

    arrive(1, 0)
    on_core(0, w_in_first.wait_recv, w_in_next.start)
    on_core(1, w_out_first.wait_recv, w_out_next.start)
    arrive(1, 1)
    for load in tables:
        load.wait()
    prepare(meta, momv, errv, medv, infov, acrossv)
    ready = [
        pltpu.make_async_copy(medv, med_ref, lsem.at[16]),
        pltpu.make_async_copy(infov, info_ref, lsem.at[17]),
        pltpu.make_async_copy(acrossv, across_ref, lsem.at[18]),
    ]
    for copy in ready:
        copy.start()
    meta_first.wait_recv()
    on_core(1, meta_next.wait_recv)
    for k in (0, 1):
        spots[k] = jnp.broadcast_to(compact(lists_of(meta2, k), 0), (LIVE, 128))
    ready += [
        pltpu.make_async_copy(meta2, codes_ref, lsem.at[21]),
        pltpu.make_async_copy(spots, spots_ref, lsem.at[22]),
    ]
    for copy in ready[3:]:
        copy.start()
    arrive(2, 0)
    on_core(0, w_out_first.wait_recv, own_wi.wait, own_wo.wait)
    on_core(1, w_in_first.wait_recv, w_in_next.wait_recv, w_out_next.wait_recv)

    def wait_sibling(*units):
        for unit in units:
            for sub in (0, 1):
                sibling(unit, sub).wait_recv()

    out_first = pltpu.make_async_copy(ghl.at[:, pl.ds(0, 4096)], ghl_ref.at[:, pl.ds(0, 4096)], lsem.at[19])
    out_next = [
        pltpu.make_async_copy(ghl.at[:, pl.ds(start, 2048)], ghl_ref.at[:, pl.ds(start, 2048)], lsem.at[sem])
        for start, sem in ((4096, 20), (6144, 23))
    ]
    ready += [out_first, *out_next]

    def work(start, count, last=False):
        rows = pl.ds(start, count)
        if last:
            def product(kind, into):
                into[...] = nn(buf[0, rows, :], wi[...]) if kind == 0 else nt(buf[1, rows, :], wo[...])

            on_core(0, functools.partial(product, 0, early))
            on_core(1, functools.partial(product, 1, early))
            wait_sibling(7)
            on_core(0, functools.partial(product, 1, late))
            on_core(1, functools.partial(product, 0, late))
            one, two = early[...], late[...]
            value, slope = gelu_pair(jnp.where(core == 0, one, two))
            back = jnp.where(core == 0, two, one)
        else:
            value, slope = gelu_pair(nn(buf[0, rows, :], wi[...]))
            back = nt(buf[1, rows, :], wo[...])
        hidden = value.astype(BF16)
        grad = (back * slope).astype(BF16)
        for c in range(4):
            at = slice(c * 512, (c + 1) * 512)
            total = gin[at, :] + tn(buf[0, rows, at], grad)
            if not last:
                gin[at, :] = total
                continue
            for k in range(2):
                for h in range(2):
                    part = total[:, k * COLS + h * 128 : k * COLS + (h + 1) * 128]
                    ghl[k, h * 2048 + c * 512 : h * 2048 + (c + 1) * 512, :] = split2(part)
        if last:
            out_first.start()
        for c in range(4):
            at = slice(c * 512, (c + 1) * 512)
            total = gout[:, at] + tn(hidden, buf[1, rows, at])
            if not last:
                gout[:, at] = total
                continue
            for k in range(2):
                for q in range(4 * c, 4 * c + 4):
                    part = total[k * COLS : (k + 1) * COLS, (q - 4 * c) * 128 : (q - 4 * c + 1) * 128]
                    ghl[k, 4096 + q * 256 : 4352 + q * 256, :] = split2(part)
            if c % 2 == 1:
                out_next[c // 2].start()

    def work_pair(i, carry):
        @pl.when(i == 0)
        def _():
            wait_sibling(0, 1)

        @pl.when(i == 1)
        def _():
            wait_sibling(2, 3)

        @pl.when(i == 2)
        def _():
            arrive(2, 1)
            arrive(3, 0)
            wait_sibling(4, 5)

        work(pl.multiple_of(i * (2 * CHIP), 16), 2 * CHIP)
        return carry

    lax.fori_loop(0, 3, work_pair, 0)
    arrive(3, 1)
    wait_sibling(6)
    work(6 * CHIP, CHIP)
    ring(0, 3, 0).wait_recv()
    sibling(7, 0).start()
    ring(1, 3, 1).wait_recv()
    sibling(7, 1).start()
    work(7 * CHIP, CHIP, last=True)

    for copy in list_copies + [w_in_first, w_out_first, meta_first]:
        copy.wait_send()
    for way in (0, 1):
        for hops in range(4):
            for sub in (0, 1):
                if hops < 3 or sub == way:
                    ring(way, hops, sub).wait_send()
    for unit in range(NZ):
        for sub in (0, 1):
            sibling(unit, sub).wait_send()
    on_core(0, w_in_next.wait_send)
    on_core(1, w_out_next.wait_send, meta_next.wait_send)
    for copy in ready:
        copy.wait()


def sketch_kernel(
    ghl_ref, codes_ref, spots_ref, table_ref,
    ghl, codes, spots, outb, recvx, yb, recvy, tot, lsem, x_s, x_r, y_s, y_r, a_s, a_r,
):
    rep, shard = lax.axis_index("rep"), lax.axis_index("shard")
    y, core = rep // 2, rep % 2
    x, z = shard // NZ, shard % NZ
    other = 1 - core

    def dev(dx=0, dy=0, dz=0, to=None):
        c = core if to is None else to
        return {
            "rep": lax.rem(y + dy + NY, NY) * 2 + c,
            "shard": lax.rem(x + dx + NX, NX) * NZ + lax.rem(z + dz + NZ, NZ),
        }

    def remote(src, dst, send, recv, device):
        return pltpu.make_async_remote_copy(
            src_ref=src, dst_ref=dst, send_sem=send, recv_sem=recv, device_id=device, device_id_type=MESH
        )

    def on_core(c, *actions):
        @pl.when(core == c)
        def _():
            for action in actions:
                action()

    loads = [
        pltpu.make_async_copy(codes_ref, codes, lsem.at[0]),
        pltpu.make_async_copy(spots_ref, spots, lsem.at[1]),
        pltpu.make_async_copy(ghl_ref.at[1], ghl.at[1], lsem.at[2]),
        pltpu.make_async_copy(ghl_ref.at[0], ghl.at[0], lsem.at[3]),
    ]
    for load in loads:
        load.start()
    barrier = pltpu.get_barrier_semaphore()
    partners = [dev(dx=d, to=c) for d in (1, -1, 2) for c in (0, 1)]
    partners += [dev(dy=d) for d in (1, 2, 3)] + [dev(to=other)]
    for partner in partners:
        pl.semaphore_signal(barrier, inc=1, device_id=partner, device_id_type=MESH)
    pl.semaphore_wait(barrier, len(partners))
    loads[0].wait()
    loads[1].wait()

    def spread(code):
        code = jnp.broadcast_to(code, (16, 128))
        bucket = (code >> 1).astype(F32)
        return jnp.where((code & 1) == 1, 1.0, -1.0).astype(BF16), [(bucket - 256.0 * h).astype(BF16) for h in (0, 1)]

    def one_hot(spread_code, quarter):
        sign, spot = spread_code[0], spread_code[1][quarter // 2]
        ramp = iota((256, 128), 0).astype(F32).astype(BF16)
        first = 8 * (quarter % 2)
        hits = [spot == ramp[g * 16 : (g + 1) * 16] for g in range(first, first + 8)]
        return jnp.concatenate([jnp.where(hit, sign, jnp.zeros_like(sign)) for hit in hits], axis=0)

    def sketch(k, work):
        step = 4
        per = NB // 512
        used = sorted({j for j, _ in work if j is not None})

        def run(*sums):
            def chunk(t, carry):
                first = [unit * per + t * step for unit in (0, 1)]

                def tile(unit, i):
                    return ghl[k, pl.ds(pl.multiple_of((first[unit] + i) * 256, 256), 256), :]

                found = [
                    {j: codes[k, pl.ds(pl.multiple_of(j * 64 + 2 * first[unit], 8), 2 * step), :] for j in used}
                    for unit in (0, 1)
                ]
                for unit in (0, 1):
                    pltpu.matmul_push_rhs(tile(unit, 0), 0, unit)
                for i in range(step):
                    if i + 1 < step:
                        for unit in (0, 1):
                            pltpu.matmul_push_rhs(tile(unit, i + 1), (i + 1) % 2, unit)
                    rows = [
                        {j: [spread(found[unit][j][2 * i + n : 2 * i + n + 1, :]) for n in (0, 1)] for j in used}
                        for unit in (0, 1)
                    ]
                    for c, (j, q) in enumerate(work):
                        for unit in (0, 1):
                            if j is None:
                                spot = spots[k, q * 128 : (q + 1) * 128, :] - (first[unit] + i) * 256
                                lane = iota((128, 128), 1)
                                hot = [jnp.where(spot == lane + 128 * n, 1.0, 0.0).astype(BF16) for n in (0, 1)]
                            else:
                                hot = [one_hot(rows[unit][j][n], q) for n in (0, 1)]
                            pltpu.matmul_acc_lhs(
                                sums[2 * c + unit],
                                jnp.concatenate(hot, axis=1),
                                load_staged_rhs=i % 2 if c == 0 else None,
                            )
                return carry

            lax.fori_loop(0, per // step, chunk, 0)
            for c, (j, q) in enumerate(work):
                total = pltpu.matmul_pop(sums[2 * c]) + pltpu.matmul_pop(sums[2 * c + 1])
                start = q * 128 + (LISTED if j is None else j * COUNT)
                outb[k, start : start + 128, :] = (total[:, :128] + total[:, 128:]).astype(BF16)

        pl.run_scoped(run, *[pltpu.ACC(mxu_id=unit)((128, 256), F32) for _ in work for unit in (0, 1)])

    def whole(*rows):
        return [(j, q) for j in rows for q in range(4)]

    def half_of(p):
        return PIECES[p][0] // 2, PIECES[p][1] // 2

    def quarter_of(p):
        return PIECES[p][0] // 8, PIECES[p][1] // 8

    def x_copy(k, p, h, slot, device):
        start, rows = half_of(p)
        return remote(
            outb.at[k, pl.ds(PIECES[p][0] + h * rows, rows)], recvx.at[slot, pl.ds(start, rows)],
            x_s.at[k, p, h], x_r.at[slot, p], device,
        )

    x_far = [[x_copy(1, p, h, 1 + 2 * core, dev(dx=1 + core, to=h)) for h in (0, 1)] for p in range(3)]
    x_near = [[x_copy(0, p, h, 2, dev(dx=-1, to=h)) for h in (0, 1)] for p in range(3)]
    x_home = [x_copy(0, p, 1, 0, dev(to=1)) for p in range(3)]

    def x_far_start(p):
        for copy in x_far[p]:
            copy.start()

    def x_near_start(p):
        start, rows = half_of(p)
        on_core(1, *[copy.start for copy in x_near[p]])

        @pl.when(core == 0)
        def _():
            x_home[p].start()
            recvx[0, start : start + rows, :] = outb[0, PIECES[p][0] : PIECES[p][0] + rows, :]

    def my_quarter(p):
        rows = PIECES[p][1] // 8
        return pl.ds(pl.multiple_of(PIECES[p][0] + core * (4 * rows) + y * rows, 16), rows)

    def y_copy(p, d):
        start, rows = quarter_of(p)
        there = pl.ds(pl.multiple_of(4 * start + lax.rem(y + d, NY) * rows, 16), rows)
        return remote(yb.at[there], recvy.at[d - 1, pl.ds(start, rows)], y_s.at[p, d - 1], y_r.at[p, d - 1], dev(dy=d))

    def y_start(p):
        start, rows = half_of(p)
        on_core(1, x_copy(0, p, 1, 0, dev(to=1)).wait_recv)
        for slot in (1, 2, 3):
            x_copy(1, p, 0, slot, dev(dx=1)).wait_recv()
        part = recvx[0, start : start + rows, :].astype(F32)
        for slot in (1, 2, 3):
            part = part + recvx[slot, start : start + rows, :].astype(F32)
        yb[start : start + rows, :] = part.astype(BF16)
        tot[pl.ds(pl.multiple_of(PIECES[p][0] + core * rows, 16), rows), :] = part
        for d in (1, 2, 3):
            y_copy(p, d).start()

    def a_copy(p, d):
        at = tot.at[my_quarter(p)]
        return remote(at, at, a_s.at[p, d - 1], a_r.at[p, d - 1], dev(dy=d))

    def a_start(p):
        start, rows = quarter_of(p)
        total = tot[my_quarter(p), :]
        for d in (1, 2, 3):
            y_copy(p, d).wait_recv()
            total = total + recvy[d - 1, start : start + rows, :].astype(F32)
        tot[my_quarter(p), :] = total
        for d in (1, 2, 3):
            a_copy(p, d).start()

    def e_copy(p):
        rows = PIECES[p][1] // 2
        at = tot.at[pl.ds(pl.multiple_of(PIECES[p][0] + core * rows, 16), rows)]
        return remote(at, at, a_s.at[p, 3], a_r.at[p, 3], dev(to=other))

    def e_start(p):
        for d in (1, 2, 3):
            a_copy(p, d).wait_recv()
        e_copy(p).start()

    def piece_out(p):
        at = pl.ds(*PIECES[p])
        return pltpu.make_async_copy(tot.at[at], table_ref.at[at], lsem.at[4 + p])

    def e_finish(p):
        e_copy(p).wait_recv()
        piece_out(p).start()

    passes = (whole(0, 1), whole(2, 3), whole(4) + [(None, 0), (None, 1)])
    loads[2].wait()
    sketch(1, passes[0])
    x_far_start(0)
    loads[3].wait()
    sketch(0, passes[0])
    x_near_start(0)
    sketch(1, passes[1])
    x_far_start(1)
    y_start(0)
    sketch(0, passes[1])
    x_near_start(1)
    a_start(0)
    sketch(1, passes[2])
    x_far_start(2)
    y_start(1)
    e_start(0)
    sketch(0, passes[2])
    x_near_start(2)
    a_start(1)
    e_finish(0)
    y_start(2)
    e_start(1)
    a_start(2)
    e_finish(1)
    e_start(2)
    e_finish(2)

    for p in range(3):
        for copy in x_far[p] + [y_copy(p, d) for d in (1, 2, 3)] + [a_copy(p, d) for d in (1, 2, 3)] + [e_copy(p)]:
            copy.wait_send()
    on_core(0, *[copy.wait_send for copy in x_home])
    on_core(1, *[c.wait_send for p in range(3) for c in x_near[p]])
    for p in range(3):
        piece_out(p).wait()


def run_main(*args):
    anywhere = pl.BlockSpec(memory_space=pl.ANY)
    dma = pltpu.SemaphoreType.DMA
    return pl.pallas_call(
        main_kernel,
        out_shape=(
            jax.ShapeDtypeStruct((2, NB, 256), BF16),
            jax.ShapeDtypeStruct((2, META, 128), I32),
            jax.ShapeDtypeStruct((2, LIVE, 128), I32),
            jax.ShapeDtypeStruct((LIVE, 128), F32),
            jax.ShapeDtypeStruct((LIVE, 128), I32),
            jax.ShapeDtypeStruct((8, LIVE), I32),
        ),
        in_specs=[anywhere] * 7 + [pl.BlockSpec(memory_space=pltpu.SMEM)] + [anywhere] * 2,
        out_specs=(anywhere,) * 6,
        scratch_shapes=[
            pltpu.VMEM((TOK, DW), BF16),
            pltpu.VMEM((TOK, DW), BF16),
            pltpu.VMEM((2, NZ * CHIP, DW), BF16),
            pltpu.VMEM((DW, 2 * COLS), BF16),
            pltpu.VMEM((2 * COLS, DW), BF16),
            pltpu.VMEM((DW, 2 * COLS), F32),
            pltpu.VMEM((2 * COLS, DW), F32),
            pltpu.VMEM((ROWS, NB), I32),
            pltpu.VMEM((ROWS, NB), I32),
            pltpu.VMEM((META, 128), I32),
            pltpu.VMEM((2, META, 128), I32),
            pltpu.VMEM((2, NB, 256), BF16),
            pltpu.VMEM((ROWS, COUNT, 128), F32),
            pltpu.VMEM((ROWS, COUNT, 128), F32),
            pltpu.VMEM((LIVE, 128), F32),
            pltpu.VMEM((LIVE, 128), I32),
            pltpu.VMEM((8, LIVE), I32),
            pltpu.VMEM((2, LIVE, 128), I32),
            pltpu.VMEM((1, 64), I32),
            pltpu.VMEM((CHIP, 2 * COLS), F32),
            pltpu.VMEM((CHIP, 2 * COLS), F32),
            dma((24,)), dma((2,)),
            dma((2, 4, 2)), dma((2, 4, 2)), dma((NZ, 2)), dma((NZ, 2)), dma((4,)), dma((4,)),
            dma((7,)), dma((7,)), dma((2,)), dma((2,)),
        ],
        compiler_params=pltpu.CompilerParams(
            collective_id=0, has_side_effects=True, vmem_limit_bytes=62 * 1024 * 1024
        ),
        cost_estimate=pl.CostEstimate(flops=15_000_000_000, bytes_accessed=20_000_000, transcendentals=2_000_000),
        name="gather_grad",
    )(*args)


def run_sketch(ghl, codes, spots):
    anywhere = pl.BlockSpec(memory_space=pl.ANY)
    dma = pltpu.SemaphoreType.DMA
    return pl.pallas_call(
        sketch_kernel,
        out_shape=jax.ShapeDtypeStruct((TAB, 128), F32),
        in_specs=[anywhere] * 3,
        out_specs=anywhere,
        scratch_shapes=[
            pltpu.VMEM((2, NB, 256), BF16),
            pltpu.VMEM((2, META, 128), I32),
            pltpu.VMEM((2, LIVE, 128), I32),
            pltpu.VMEM((2, TAB, 128), BF16),
            pltpu.VMEM((4, TAB // 2, 128), BF16),
            pltpu.VMEM((TAB // 2, 128), BF16),
            pltpu.VMEM((3, TAB // 8, 128), BF16),
            pltpu.VMEM((TAB, 128), F32),
            dma((7,)), dma((2, 3, 2)), dma((4, 3)), dma((3, 3)), dma((3, 3)), dma((3, 4)), dma((3, 4)),
        ],
        compiler_params=pltpu.CompilerParams(
            collective_id=1, has_side_effects=True, vmem_limit_bytes=62 * 1024 * 1024
        ),
        cost_estimate=pl.CostEstimate(flops=24_000_000_000, bytes_accessed=10_000_000, transcendentals=0),
        name="sketch_reduce",
    )(ghl, codes, spots)


def finish_kernel(
    table, med, info, across, mom, err, w_in, w_out,
    win_new, wout_new, mom_new, err_new,
    tabv, medv, infov, acrossv, momv, errv, winv, woutv, winn, woutn, momn, errn, sem, out_sem,
):
    pairs = [(info, infov), (med, medv), (table, tabv), (across, acrossv), (w_in, winv), (w_out, woutv)]
    for j in range(ROWS):
        pairs += [(mom.at[:, j, :], momv.at[j]), (err.at[:, j, :], errv.at[j])]
    loads = [pltpu.make_async_copy(src, dst, sem.at[n]) for n, (src, dst) in enumerate(pairs)]
    for load in loads:
        load.start()
    stores = []

    def store(src, dst):
        stores.append(pltpu.make_async_copy(src, dst, out_sem.at[len(stores)]))
        stores[-1].start()

    for load in loads[:4]:
        load.wait()
    codes = infov[...]
    update = medv[...] + LEARN * tabv[LISTED:, :]
    kept = split2(jnp.where(codes[:, ROWS : ROWS + 1] == 1, update, 0.0))
    places = acrossv[0:1, :]

    def delta(start, rows):
        hit = jnp.where(iota((rows, LIVE), 0) + start == places, 1.0, 0.0).astype(BF16)
        got = nn(hit, kept)
        return got[:, :128] + got[:, 128:]

    loads[4].wait()
    for c in range(4):
        rows = pl.ds(c * 512, 512)
        for h in range(2):
            at = slice(h * 128, (h + 1) * 128)
            winn[rows, at] = winv[rows, at].astype(F32) - delta(h * 2048 + c * 512, 512)
        store(winn.at[rows], win_new.at[rows])
    loads[5].wait()
    for c in range(4):
        for q in range(4 * c, 4 * c + 4):
            at = slice(q * 128, (q + 1) * 128)
            woutn[:, at] = woutv[:, at].astype(F32) - delta(4096 + q * 256, 256)
        at = pl.ds(c * 512, 512)
        store(woutn.at[:, at], wout_new.at[:, at])
    for j in range(ROWS):
        loads[6 + 2 * j].wait()
        loads[7 + 2 * j].wait()
        fresh = DECAY * momv[j] + tabv[j * COUNT : (j + 1) * COUNT, :]
        momn[j] = fresh
        store(momn.at[j], mom_new.at[:, j, :])
        gone = tn(signed_hit(codes[:, j : j + 1]), kept)
        errn[j] = errv[j] + LEARN * fresh - (gone[:, :128] + gone[:, 128:])
        store(errn.at[j], err_new.at[:, j, :])
    for copy in stores:
        copy.wait()


def run_finish(table, med, info, across, mom, err, w_in, w_out):
    anywhere = pl.BlockSpec(memory_space=pl.ANY)
    vmem = pltpu.VMEM
    deep = vmem((ROWS, COUNT, 128), F32)
    return pl.pallas_call(
        finish_kernel,
        out_shape=(
            jax.ShapeDtypeStruct(w_in.shape, F32),
            jax.ShapeDtypeStruct(w_out.shape, F32),
            jax.ShapeDtypeStruct(mom.shape, F32),
            jax.ShapeDtypeStruct(err.shape, F32),
        ),
        in_specs=[anywhere] * 8,
        out_specs=(anywhere,) * 4,
        scratch_shapes=[
            vmem((TAB, 128), F32), vmem((LIVE, 128), F32), vmem((LIVE, 128), I32), vmem((8, LIVE), I32),
            deep, deep, vmem(w_in.shape, BF16), vmem(w_out.shape, BF16), vmem(w_in.shape, F32), vmem(w_out.shape, F32),
            deep, deep, pltpu.SemaphoreType.DMA((16,)), pltpu.SemaphoreType.DMA((18,)),
        ],
        compiler_params=pltpu.CompilerParams(vmem_limit_bytes=62 * 1024 * 1024),
        cost_estimate=pl.CostEstimate(flops=3_000_000_000, bytes_accessed=16_000_000, transcendentals=0),
        name="finish",
    )(table, med, info, across, mom, err, w_in, w_out)


def per_device(
    tokens, cotangent, w_in, w_out, momentum, error, block_order, signs, heavy_blocks, heavy_count
):
    mom, err = by_bucket(momentum), by_bucket(error)
    ghl, codes, spots, med, info, across = run_main(
        tokens, cotangent, w_in, w_out, block_order, signs, heavy_blocks, heavy_count, mom, err
    )
    table = run_sketch(ghl, codes, spots)
    win_new, wout_new, mom_new, err_new = run_finish(table, med, info, across, mom, err, w_in, w_out)
    return win_new, wout_new, by_row(mom_new), by_row(err_new)


def by_bucket(table):
    return jnp.transpose(table.reshape(ROWS, COUNT, 128), (1, 0, 2))


def by_row(table):
    return jnp.transpose(table, (1, 0, 2)).reshape(ROWS, COUNT * 128)


def solution(mesh):
    placed = (
        P(("rep", "shard"), None),
        P(("rep", "shard"), None),
        P(None, "shard"),
        P("shard", None),
        P(None, "shard"),
        P(None, "shard"),
        P(None, "shard"),
        P(None, "shard"),
        P("rep", "shard"),
        P("rep", "shard"),
    )
    return jax.shard_map(
        per_device,
        mesh=mesh,
        in_specs=placed,
        out_specs=(P(None, "shard"), P("shard", None), P(None, "shard"), P(None, "shard")),
        check_vma=False,
    )
```
